32 devices in a mesh: seq: 8 (over y, x, core), chan: 4 (over z).
Axes of the slice: x: 2, y: 2, z: 4, core: 2. Of those that a mesh axis runs over, the one named last changes fastest.
Arguments:
- tokens: float32 [6, 4096, 1024], P(None, 'seq'), may hold values from -6 to 6
- segment_ids: int32 [6, 4096], P(None, 'seq'), may hold values from 0 to 4095, as said below
- cotangent: float32 [6, 4096, 1024], P(None, 'seq'), may hold values from -6 to 6
- norm_gains: float32 [2, 1024], replicated, may hold values from 0.5 to 1.5
- filter_weight: float32 [3, 1024], P(None, 'chan'), may hold values from -0.6 to 0.6
- in_weight: float32 [1024, 3, 1024], P('seq', None, 'chan'), may hold values from -0.1875 to 0.1875
- out_weight: float32 [1024, 1024], P('seq', 'chan'), may hold values from -0.1875 to 0.1875
- gate_weight: float32 [1024, 4608], P('seq', 'chan'), may hold values from -0.1875 to 0.1875
- up_weight: float32 [1024, 4608], P('seq', 'chan'), may hold values from -0.1875 to 0.1875
- down_weight: float32 [1024, 4608], P('seq', 'chan'), may hold values from -0.09375 to 0.09375
- norm_gains_mean: float32 [2, 1024], replicated
- norm_gains_square: float32 [2, 1024], replicated
- filter_mean: float32 [3, 1024], P(None, 'chan')
- filter_square: float32 [3, 1024], P(None, 'chan')
- in_momentum: float32 [1024, 3, 1024], P('seq', None, 'chan')
- out_momentum: float32 [1024, 1024], P('seq', 'chan')
- gate_momentum: float32 [1024, 4608], P('seq', 'chan')
- up_momentum: float32 [1024, 4608], P('seq', 'chan')
- down_momentum: float32 [1024, 4608], P('seq', 'chan')
Outputs:
- block_out: float32 [6, 4096, 1024], P(None, 'seq')
- input_grad: float32 [6, 4096, 1024], P(None, 'seq')
- norm_gains_new: float32 [2, 1024], replicated
- norm_gains_mean_new: float32 [2, 1024], replicated
- norm_gains_square_new: float32 [2, 1024], replicated
- filter_new: float32 [3, 1024], P(None, 'chan')
- filter_mean_new: float32 [3, 1024], P(None, 'chan')
- filter_square_new: float32 [3, 1024], P(None, 'chan')
- in_momentum_new: float32 [1024, 3, 1024], P('seq', None, 'chan')
- in_weight_new: float32 [1024, 3, 1024], P('seq', None, 'chan')
- out_momentum_new: float32 [1024, 1024], P('seq', 'chan')
- out_weight_new: float32 [1024, 1024], P('seq', 'chan')
- gate_momentum_new: float32 [1024, 4608], P('seq', 'chan')
- gate_weight_new: float32 [1024, 4608], P('seq', 'chan')
- up_momentum_new: float32 [1024, 4608], P('seq', 'chan')
- up_weight_new: float32 [1024, 4608], P('seq', 'chan')
- down_momentum_new: float32 [1024, 4608], P('seq', 'chan')
- down_weight_new: float32 [1024, 4608], P('seq', 'chan')
The draws below stay inside these ranges and needn't reach their ends.
Inputs may be any that keep to these rules, and one draw needn't show every extreme that they name: `segment_ids`: in each sequence, a token's id is the position (from 0) at which its document begins: ids never fall, each id is at most its position, and a token whose id equals its position begins a document. One sequence, drawn afresh, is a single document.
All inputs are finite; a program needn't handle non-finite values.
Results may differ from the reference program's by a relative error of at most 0.018.
Values may be sent and summed in bfloat16 or wider, within the bound.
A program may use at most 256 MiB of HBM per device.

```python
import math
import jax
import jax.numpy as jnp
from jax import lax

D = 1024
FF = 4608
SEQS = 6
TOK_ROW = 512
BREAKS = 4
NS_ITERS = 4
STEP = 10
SEQ_LEN = 4096
TOKENS = 24576


lead_strengths = (2.0, 1.7, 1.5, 1.35, 1.2, 1.1)


factor_span = 1.0986


def momentum_field(key, shape, base, rise):
    entry_key = jax.random.fold_in(key, 0)
    row_key = jax.random.fold_in(key, 1)
    column_key = jax.random.fold_in(key, 2)
    left_key = jax.random.fold_in(key, 4)
    right_key = jax.random.fold_in(key, 5)
    strength_key = jax.random.fold_in(key, 6)
    row_count = shape[0]
    column_count = math.prod(shape[1:])
    normal_part = jax.random.normal(entry_key, (row_count, column_count), jnp.float32)
    entries = normal_part
    row_place = jnp.arange(row_count, dtype=jnp.float32) / row_count
    row_rise = rise ** row_place
    row_scale = row_rise * jnp.exp(jax.random.uniform(row_key, (row_count,), jnp.float32, 0.0, factor_span))
    column_scale = jnp.exp(jax.random.uniform(column_key, (column_count,), jnp.float32, 0.0, factor_span))
    field = base * entries * row_scale[:, None] * column_scale[None, :] / 3.0
    rise_power = (rise * rise - 1.0) / (2.0 * math.log(rise))
    factor_power = (math.exp(2.0 * factor_span) - 1.0) / (2.0 * factor_span)
    noise_norm = base / 3.0 * factor_power * math.sqrt(rise_power * row_count * column_count)
    left_all = jax.random.normal(left_key, (len(lead_strengths), row_count), jnp.float32) * row_rise[None, :] / math.sqrt(row_count * rise_power)
    right_all = jax.random.normal(right_key, (len(lead_strengths), column_count), jnp.float32) / math.sqrt(column_count)
    jitter = jax.random.uniform(strength_key, (len(lead_strengths),), jnp.float32, 0.92, 1.08)
    for index, strength in enumerate(lead_strengths):
        left_vector = strength * noise_norm * jitter[index] * left_all[index]
        field = field + left_vector[:, None] * right_all[index][None, :]
    return field.reshape(shape)


def draw_segment_ids(key, part):
    key = jax.random.fold_in(key, 11)
    whole_key, starts_key, edge_key, offset_key = jax.random.split(key, 4)
    whole_row = jax.random.randint(whole_key, (), 0, SEQS)
    random_starts = jax.random.randint(starts_key, (SEQS, BREAKS), 1, SEQ_LEN)
    edge_starts = TOK_ROW * jax.random.randint(edge_key, (SEQS, 2), 1, SEQ_LEN // TOK_ROW) + jax.random.randint(offset_key, (SEQS, 2), 0, 2)
    starts = jnp.concatenate([random_starts, edge_starts], axis=1)
    positions = jnp.arange(SEQ_LEN, dtype=jnp.int32)
    candidates = jnp.where(starts[:, :, None] <= positions[None, None, :], starts[:, :, None], 0)
    ids = jnp.max(candidates, axis=1)
    ids = jnp.where(jnp.arange(SEQS, dtype=jnp.int32)[:, None] == whole_row, 0, ids)
    return ids.astype(jnp.int32)


def draw_norm_gains_mean(key, part):
    key = jax.random.fold_in(key, 31)
    return 0.11 * math.sqrt(TOKENS) * jax.random.normal(key, (2, D), jnp.float32)


def draw_norm_gains_square(key, part):
    key = jax.random.fold_in(key, 32)
    return 0.001 * TOKENS * jax.random.uniform(key, (2, D), jnp.float32, 1.0, 4.0)


def draw_filter_mean(key, part):
    key = jax.random.fold_in(key, 33)
    return 0.11 * math.sqrt(TOKENS) * jax.random.normal(key, (3, D), jnp.float32)


def draw_filter_square(key, part):
    key = jax.random.fold_in(key, 34)
    return 0.001 * TOKENS * jax.random.uniform(key, (3, D), jnp.float32, 1.0, 4.0)


def draw_in_momentum(key, part):
    key = jax.random.fold_in(key, 21)
    return momentum_field(key, (D, 3, D), 0.5 * math.sqrt(TOKENS), 2.0)


def draw_out_momentum(key, part):
    key = jax.random.fold_in(key, 22)
    return momentum_field(key, (D, D), 0.5 * math.sqrt(TOKENS), 2.0)


def draw_gate_momentum(key, part):
    key = jax.random.fold_in(key, 23)
    return momentum_field(key, (D, FF), 0.3 * math.sqrt(TOKENS), 2.0)


def draw_up_momentum(key, part):
    key = jax.random.fold_in(key, 24)
    return momentum_field(key, (D, FF), 0.3 * math.sqrt(TOKENS), 2.0)


def draw_down_momentum(key, part):
    key = jax.random.fold_in(key, 25)
    return momentum_field(key, (D, FF), 0.6 * math.sqrt(TOKENS), 2.0)


def strengthened(values, rng, source, target, blocks, factor):
    def block_of(position):
        return (jnp.arange(values.shape[position]) // (values.shape[position] // blocks)).reshape((-1,) + (1,) * (values.ndim - 1 - position))

    first = jax.random.permutation(rng, blocks)[block_of(target)]
    other_side = (block_of(target) + blocks // 2) % blocks
    return jnp.where((block_of(source) == first) | (block_of(source) == other_side), factor * values, values)


def block_scale(rng, extent, pieces, low, high):
    factor_of, own = 1.0, jax.random.fold_in(rng, 6)
    for axis_at, parts in pieces:
        draws = jnp.exp(jax.random.uniform(jax.random.fold_in(own, axis_at), (parts,), jnp.float32, low / len(pieces), high / len(pieces)))
        factor_of = factor_of * jnp.repeat(draws, extent[axis_at] // parts).reshape([-1 if axis == axis_at else 1 for axis in range(len(extent))])
    return factor_of


def centred(own_key, shape, scale, limit, cuts=(), kind=jnp.bfloat16):
    values = scale * jax.random.normal(own_key, shape, jnp.float32)
    if cuts:
        values = values * block_scale(own_key, shape, cuts, -0.22, 0.18)
    return jnp.clip(values, -limit, limit).astype(kind)


def heavy_noise(key, shape, deviation, bound, cuts, heavy, kind=jnp.bfloat16):
    values = deviation * jax.random.normal(key, shape, jnp.float32)
    if cuts:
        values = values * block_scale(key, shape, cuts, -0.22, 0.18)
    return jnp.clip(strengthened(values, jax.random.fold_in(key, 3), *heavy), -bound, bound).astype(kind)


def setup_inputs(seed: int = 0) -> dict:
    streams_of = jax.random.split(jax.random.key(seed), 20)
    tokens = heavy_noise(streams_of[0], (SEQS, SEQ_LEN, D), 1.0, 6.0, ((1, 8),), (1, 2, 8, 2.0), jnp.float32)
    segment_ids = draw_segment_ids(jax.random.fold_in(streams_of[19], 71), 0)
    cotangent = heavy_noise(streams_of[2], (SEQS, SEQ_LEN, D), 1.0, 6.0, ((1, 8),), (1, 2, 8, 2.0), jnp.float32)
    norm_gains = jnp.clip(1.0 + 0.1 * jax.random.normal(streams_of[3], (2, D), jnp.float32), 0.5, 1.5)
    filter_weight = jnp.clip(jax.random.uniform(streams_of[4], (3, D), jnp.float32, -0.6, 0.6) * block_scale(streams_of[4], (3, D), ((1, 4),), -0.4, 0.0), -0.6, 0.6)
    in_weight = centred(streams_of[5], (D, 3, D), D ** -0.5, 0.1875, ((0, 8), (2, 4)), jnp.float32)
    out_weight = centred(streams_of[6], (D, D), D ** -0.5, 0.1875, ((0, 8), (1, 4)), jnp.float32)
    gate_weight = centred(streams_of[7], (D, FF), D ** -0.5, 0.1875, ((0, 8), (1, 4)), jnp.float32)
    up_weight = centred(streams_of[8], (D, FF), D ** -0.5, 0.1875, ((0, 8), (1, 4)), jnp.float32)
    down_weight = centred(streams_of[9], (D, FF), FF ** -0.5, 0.09375, ((0, 8), (1, 4)), jnp.float32)
    norm_gains_mean = draw_norm_gains_mean(jax.random.fold_in(streams_of[19], 71), 0)
    norm_gains_square = draw_norm_gains_square(jax.random.fold_in(streams_of[19], 71), 0)
    filter_mean = draw_filter_mean(jax.random.fold_in(streams_of[19], 71), 0)
    filter_square = draw_filter_square(jax.random.fold_in(streams_of[19], 71), 0)
    in_momentum = draw_in_momentum(jax.random.fold_in(streams_of[19], 71), 0)
    out_momentum = draw_out_momentum(jax.random.fold_in(streams_of[19], 71), 0)
    gate_momentum = draw_gate_momentum(jax.random.fold_in(streams_of[19], 71), 0)
    up_momentum = draw_up_momentum(jax.random.fold_in(streams_of[19], 71), 0)
    down_momentum = draw_down_momentum(jax.random.fold_in(streams_of[19], 71), 0)
    return {"tokens": tokens, "segment_ids": segment_ids, "cotangent": cotangent, "norm_gains": norm_gains, "filter_weight": filter_weight, "in_weight": in_weight, "out_weight": out_weight, "gate_weight": gate_weight, "up_weight": up_weight, "down_weight": down_weight, "norm_gains_mean": norm_gains_mean, "norm_gains_square": norm_gains_square, "filter_mean": filter_mean, "filter_square": filter_square, "in_momentum": in_momentum, "out_momentum": out_momentum, "gate_momentum": gate_momentum, "up_momentum": up_momentum, "down_momentum": down_momentum}


NORM_EPS = 1e-05
QUINTIC_FIRST = 3.4445
QUINTIC_SECOND = -4.775
QUINTIC_THIRD = 2.0315
MOMENTUM_DECAY = 0.95
FIRST_DECAY = 0.9
SECOND_DECAY = 0.999
ADAM_EPS = 1e-08
ADAM_RATE = 0.4
WEIGHT_DECAY = 0.01
ORTHO_EPS = 1e-07

@jax.custom_vjp
def low(v):
    return lax.optimization_barrier(v.astype(jnp.bfloat16)).astype(jnp.float32)

@jax.custom_vjp
def low_back(v):
    return v

def low_keep(v):
    return (low(v), None)

def low_pass(kept, grad):
    return (grad,)

def back_keep(v):
    return (v, None)

def back_low(kept, grad):
    return (low(grad),)
low.defvjp(low_keep, low_pass)
low_back.defvjp(back_keep, back_low)

def matmul(left, right):
    return jnp.dot(left, right, precision=lax.Precision.HIGHEST, preferred_element_type=jnp.float32)

def rms_normed(values, gain):
    return values * lax.rsqrt(lax.optimization_barrier(jnp.mean(values * values, axis=-1, keepdims=True)) + NORM_EPS) * gain

def mixer_block(tokens, norm_gains, filter_weight, in_weight, out_weight, gate_weight, up_weight, down_weight, segment_ids):
    total_rows = SEQS * SEQ_LEN
    flat_tokens = tokens.reshape(total_rows, D)
    first_normed = low(rms_normed(flat_tokens, norm_gains[0]))
    streams = low_back(matmul(first_normed, low(in_weight.reshape(D, 3 * D))))
    streams = streams.reshape(SEQS, SEQ_LEN, 3, D)
    input_gate = streams[:, :, 0]
    output_gate = streams[:, :, 1]
    value_stream = streams[:, :, 2]
    gated_input = input_gate * value_stream
    positions = jnp.arange(SEQ_LEN, dtype=jnp.int32)[None, :]
    filtered = filter_weight[2] * gated_input
    for offset in (1, 2):
        shifted = jnp.pad(gated_input, ((0, 0), (offset, 0), (0, 0)))[:, :SEQ_LEN]
        keep_mask = (segment_ids <= positions - offset).astype(jnp.float32)[:, :, None]
        filtered = filtered + filter_weight[2 - offset] * keep_mask * shifted
    mixer_input = low((output_gate * filtered).reshape(total_rows, D))
    residual = flat_tokens + low_back(matmul(mixer_input, low(out_weight).T))
    second_normed = low(rms_normed(residual, norm_gains[1]))
    gate_value = low_back(matmul(second_normed, low(gate_weight)))
    up_value = low_back(matmul(second_normed, low(up_weight)))
    activated = low(jax.nn.silu(gate_value) * up_value)
    result = residual + low_back(matmul(activated, low(down_weight).T))
    return result.reshape(SEQS, SEQ_LEN, D)

def adam_update(param, gradient, first, second):
    first_new = FIRST_DECAY * first + (1.0 - FIRST_DECAY) * gradient
    second_new = SECOND_DECAY * second + (1.0 - SECOND_DECAY) * gradient * gradient
    first_fix = 1.0 - FIRST_DECAY ** STEP
    second_fix = 1.0 - SECOND_DECAY ** STEP
    param_new = param - ADAM_RATE * (first_new / first_fix) / (jnp.sqrt(second_new / second_fix) + ADAM_EPS)
    return (param_new, first_new, second_new)

def orthogonalized(matrix):
    total = jnp.sqrt(jnp.sum(matrix * matrix))
    state = low(matrix / (total + ORTHO_EPS))
    for iteration in range(NS_ITERS):
        gram = low(matmul(state, state.T))
        poly = low(QUINTIC_SECOND * gram + QUINTIC_THIRD * matmul(gram, gram))
        state = low(QUINTIC_FIRST * state + matmul(poly, state))
    return state

def muon_update(weight, gradient, momentum, rate):
    momentum_new = MOMENTUM_DECAY * momentum + gradient
    matrix = momentum_new.reshape(D, -1)
    columns = matrix.shape[1]
    ortho = orthogonalized(matrix).reshape(weight.shape)
    weight_new = weight * (1.0 - WEIGHT_DECAY * rate) - rate * math.sqrt(columns / D) * ortho
    return (momentum_new, weight_new)

def reference(tokens, segment_ids, cotangent, norm_gains, filter_weight, in_weight, out_weight, gate_weight, up_weight, down_weight, norm_gains_mean, norm_gains_square, filter_mean, filter_square, in_momentum, out_momentum, gate_momentum, up_momentum, down_momentum):

    def forward(tokens_in, gains_in, filter_in, in_matrix, out_matrix, gate_matrix, up_matrix, down_matrix):
        return mixer_block(tokens_in, gains_in, filter_in, in_matrix, out_matrix, gate_matrix, up_matrix, down_matrix, segment_ids)
    block_out, pullback = jax.vjp(forward, tokens, norm_gains, filter_weight, in_weight, out_weight, gate_weight, up_weight, down_weight)
    grads = pullback(cotangent)
    gains_new, gains_mean_new, gains_square_new = adam_update(norm_gains, grads[1], norm_gains_mean, norm_gains_square)
    filter_new, filter_mean_new, filter_square_new = adam_update(filter_weight, grads[2], filter_mean, filter_square)
    in_moment, in_new = muon_update(in_weight, grads[3], in_momentum, 1.0)
    out_moment, out_new = muon_update(out_weight, grads[4], out_momentum, 1.0)
    gate_moment, gate_new = muon_update(gate_weight, grads[5], gate_momentum, 1.0)
    up_moment, up_new = muon_update(up_weight, grads[6], up_momentum, 1.0)
    down_moment, down_new = muon_update(down_weight, grads[7], down_momentum, 0.5)
    return (block_out, grads[0], gains_new, gains_mean_new, gains_square_new, filter_new, filter_mean_new, filter_square_new, in_moment, in_new, out_moment, out_new, gate_moment, gate_new, up_moment, up_new, down_moment, down_new)
```

```python
import functools
import math

import jax
import jax.numpy as jnp
from jax import lax
from jax.experimental import pallas as pl
from jax.experimental.pallas import tpu as pltpu
from jax.sharding import PartitionSpec as P

D = 1024
FF = 4608
NS_ITERS = 4
STEP = 10


NORM_EPS = 1e-05
QUINTIC_FIRST = 3.4445
QUINTIC_SECOND = -4.775
QUINTIC_THIRD = 2.0315
MOMENTUM_DECAY = 0.95
FIRST_DECAY = 0.9
SECOND_DECAY = 0.999
ADAM_EPS = 1e-08
ADAM_RATE = 0.4
WEIGHT_DECAY = 0.01
ORTHO_EPS = 1e-07

MESH = pl.DeviceIdType.MESH
BF16 = jnp.bfloat16
F32 = jnp.float32

PIECES = 32
PER_CHAN = 8
PIECE = FF // PIECES
LANES = 128
TILES = FF // 4 // LANES
UNIT = LANES // PER_CHAN
SMALL_PIECE = 4 * D // PIECES
IN_PIECES = 6


def remote(src, dst, send, recv, **place):
    return pltpu.make_async_remote_copy(
        src_ref=src, dst_ref=dst, send_sem=send, recv_sem=recv, device_id=place, device_id_type=MESH
    )


def flip(index, bit):
    step = 1 << bit
    return index + step * (1 - 2 * lax.rem(lax.div(index, step), 2))


def flips(index, bits):
    found = [index]
    for bit in bits:
        found = found + [flip(one, bit) for one in found]
    return found


def greet(places):
    barrier = pltpu.get_barrier_semaphore()
    for place in places:
        pl.semaphore_signal(barrier, inc=1, device_id=place, device_id_type=MESH)
    pl.semaphore_wait(barrier, len(places))


def high_bits(bits, half):
    order = list(range(1, bits))
    return order if half == 0 else order[::-1]


def call(kernel, outs, in_spaces, out_spaces, scratch, ident, *args, vmem=48):
    return pl.pallas_call(
        kernel,
        out_shape=outs,
        in_specs=[pl.BlockSpec(memory_space=space) for space in in_spaces],
        out_specs=jax.tree.map(lambda space: pl.BlockSpec(memory_space=space), out_spaces),
        scratch_shapes=scratch,
        compiler_params=pltpu.CompilerParams(
            collective_id=ident, has_side_effects=True, vmem_limit_bytes=vmem * 1024 * 1024
        ),
    )(*args)


def holder(r, c, seqs):
    at = lax.rem(r + PIECES * seqs - PER_CHAN * c, seqs)
    return at, at < PER_CHAN, lax.div(PER_CHAN * c + at, seqs)


class Homeward:
    def __init__(self, seqs, chans, held, out, between, sems):
        self.seqs, self.chans, self.held, self.out, self.between = seqs, chans, held, out, between
        self.own_sem, self.stay_sem, self.a_send, self.a_recv, self.b_send, self.b_recv = sems
        self.r, self.c = lax.axis_index("seq"), lax.axis_index("chan")
        self.at_out, self.has, self.place = holder(self.r, self.c, seqs)

    def target(self, at):
        return lax.div(self.r + self.seqs * at, PER_CHAN)

    def dropping(self, at):
        return remote(
            self.held.at[at], self.between.at[self.c], self.a_send.at[at], self.a_recv.at[self.c],
            chan=self.target(at),
        )

    def keeping(self, at):
        return pltpu.make_async_copy(self.held.at[at], self.between.at[self.c], self.own_sem.at[0])

    def spreading(self, m, r_to):
        return remote(
            self.between.at[m, r_to], self.out.at[m, self.at_out],
            self.b_send.at[m, r_to], self.b_recv.at[m, self.at_out], seq=r_to,
        )

    def staying(self, m):
        return pltpu.make_async_copy(
            self.between.at[m, self.r], self.out.at[m, self.at_out], self.stay_sem.at[m]
        )

    def drop(self, at):
        @pl.when(self.target(at) != self.c)
        def _():
            self.dropping(at).start()

        @pl.when(self.target(at) == self.c)
        def _():
            self.keeping(at).start()

    def spread(self):
        @pl.when(self.has)
        def _():
            for off in (0, 1, 3, 2):
                m = lax.rem(self.c + off, self.chans)
                if off == 0:
                    self.keeping(0).wait()
                else:
                    remote(
                        self.held.at[0], self.between.at[m], self.a_send.at[0], self.a_recv.at[m], chan=m
                    ).wait_recv()
                for step in range(1, self.seqs):
                    self.spreading(m, lax.rem(self.r + step, self.seqs)).start()
                self.staying(m).start()

    def finish(self):
        @pl.when(self.has)
        def _():
            for m in range(self.chans):
                self.staying(m).wait()

        for piece in range(PER_CHAN):
            r_from = lax.rem(PER_CHAN * self.c + piece, self.seqs)

            @pl.when(r_from != self.r)
            def _():
                for m in range(self.chans):
                    remote(
                        self.between.at[m, self.r], self.out.at[m, piece],
                        self.b_send.at[m, self.r], self.b_recv.at[m, piece], seq=r_from,
                    ).wait_recv()

        for at in range(PIECES // self.seqs):

            @pl.when(self.target(at) != self.c)
            def _():
                self.dropping(at).wait_send()

        @pl.when(self.has)
        def _():
            for m in range(self.chans):
                for step in range(1, self.seqs):
                    self.spreading(m, lax.rem(self.r + step, self.seqs)).wait_send()

    @staticmethod
    def semaphores(seqs, chans):
        dma = pltpu.SemaphoreType.DMA
        return [
            dma((1,)), dma((chans,)), dma((PIECES // seqs,)), dma((chans,)),
            dma((chans, seqs)), dma((chans, PER_CHAN)),
        ]


class Relay:
    def __init__(self, chans, own, blocks, sems):
        self.chans, self.own, self.blocks = chans, own, blocks
        self.own_sem, self.send, self.recv = sems
        self.c = lax.axis_index("chan")

    def keeping(self):
        return pltpu.make_async_copy(self.own, self.blocks.at[self.c], self.own_sem.at[0])

    def copies(self, hop):
        c = self.c
        for side, block, sends in (
            (0, c - hop, (c < self.chans - 1) & (c >= hop)),
            (1, c + hop, (c > 0) & (c + hop < self.chans)),
        ):
            source = self.own if hop == 0 else self.blocks.at[block]
            yield sends, remote(
                source, self.blocks.at[block], self.send.at[side, hop], self.recv.at[side, hop],
                chan=c + 1 - 2 * side,
            )

    def await_hop(self, hop):
        c = self.c
        for side, block, comes in ((0, c - 1 - hop, c > hop), (1, c + 1 + hop, c + 1 + hop < self.chans)):

            @pl.when(comes)
            def _():
                remote(
                    self.own, self.blocks.at[block], self.send.at[side, hop], self.recv.at[side, hop],
                    chan=c - 1 + 2 * side,
                ).wait_recv()

    def step(self, hop):
        if hop == 0:
            self.keeping().start()
        else:
            self.await_hop(hop - 1)
        for sends, copy in self.copies(hop):

            @pl.when(sends)
            def _():
                copy.start()

    def finish(self):
        self.await_hop(self.chans - 2)
        self.keeping().wait()
        for hop in range(self.chans - 1):
            for sends, copy in self.copies(hop):

                @pl.when(sends)
                def _():
                    copy.wait_send()

    @staticmethod
    def semaphores(chans):
        dma = pltpu.SemaphoreType.DMA
        return [dma((1,)), dma((2, chans - 1)), dma((2, chans - 1))]


def dot(left, right):
    return jnp.dot(left, right, preferred_element_type=F32)


def contract_last(left, right):
    return lax.dot_general(left, right, (((1,), (1,)), ((), ())), preferred_element_type=F32)


def contract_first(left, right):
    return lax.dot_general(left, right, (((0,), (0,)), ((), ())), preferred_element_type=F32)


def ortho_kernel(
    seqs, chans, grad, moment, input_grad, grad_home, ortho_home, input_blocks,
    out, cut_grad, cut_ortho, between_grad, between_ortho,
    part, own, swapped, paired, parts, sums, gram, poly, half_way,
    x_send, x_recv, s_send, s_recv, g_send, g_recv, f_send, f_recv, *home_sems
):
    r, c = lax.axis_index("seq"), lax.axis_index("chan")
    core, h = lax.rem(r, 2), lax.div(r, 2)
    other = flip(r, 0)
    count, half, block = seqs // 2, D // 2, D // seqs
    tile = min(256, half)
    peers = [lax.rem(h + off, count) for off in range(1, count)]
    greet(
        [{"seq": lax.rem(r + off, seqs)} for off in range(1, seqs)]
        + [{"chan": lax.rem(c + off, chans)} for off in range(1, chans)]
    )
    home_grad = Homeward(seqs, chans, cut_grad, grad_home, between_grad, home_sems[:6])
    home_ortho = Homeward(seqs, chans, cut_ortho, ortho_home, between_ortho, home_sems[6:12])
    relay = Relay(chans, input_grad, input_blocks, home_sems[12:])
    columns = out.shape[0]
    slab = PIECE

    @pl.loop(0, columns // slab)
    def _(at):
        here = pl.ds(pl.multiple_of(at * slab, slab), slab)
        out[here] = (MOMENTUM_DECAY * moment[here].astype(F32) + grad[here].astype(F32)).astype(BF16)
        for to in range(seqs):
            cut_grad[at, to] = grad[here, to * block : (to + 1) * block]

    for at in range(columns // slab):
        home_grad.drop(at)
    relay.step(0)

    apart = c == chans - 1

    def kind(pair):
        return jnp.where(lax.rem(pair, 4) == 3, 1, 0)

    mine = kind(h)
    own_first = pl.multiple_of(core * half, half)
    other_first = pl.multiple_of((1 - core) * half, half)

    def block_at(pair, which):
        return pl.ds(pl.multiple_of(which * half + pair * block, block), block)

    def exchange():
        return remote(part, swapped, x_send, x_recv, seq=other)

    def scatter(peer):
        return remote(
            paired.at[peer], parts.at[h], s_send.at[peer], s_recv.at[h], seq=2 * peer + core
        )

    def scatter_in(peer):
        return remote(
            paired.at[peer], parts.at[peer], s_send.at[peer], s_recv.at[peer], seq=2 * peer + core
        )

    def share(peer):
        return remote(
            sums.at[kind(peer)], gram.at[block_at(h, core)], g_send.at[peer], g_recv.at[h],
            seq=2 * peer + core,
        )

    def share_in(peer):
        return remote(
            sums.at[0], gram.at[block_at(peer, core)], g_send.at[peer], g_recv.at[peer],
            seq=2 * peer + core,
        )

    def forward(pair):
        return remote(
            gram.at[block_at(pair, core)], gram.at[block_at(pair, core)],
            f_send.at[pair], f_recv.at[pair], seq=other,
        )

    def forward_in(pair):
        return remote(
            gram.at[block_at(pair, 1 - core)], gram.at[block_at(pair, 1 - core)],
            f_send.at[pair], f_recv.at[pair], seq=other,
        )

    for turn in range(NS_ITERS // 2):

        @pl.loop(0, half // tile)
        def _(at):
            here = pl.ds(pl.multiple_of(at * tile, tile), tile)
            there = pl.ds(pl.multiple_of(other_first + at * tile, tile), tile)
            part[here] = contract_first(out[:, there], out[...]).astype(BF16)

        exchange().start()

        @pl.loop(0, half // tile)
        def _(at):
            here = pl.ds(pl.multiple_of(at * tile, tile), tile)
            there = pl.ds(pl.multiple_of(own_first + at * tile, tile), tile)
            own[here] = contract_first(out[:, there], out[...])

        exchange().wait()

        @pl.loop(0, count)
        def _(at):
            here = pl.ds(pl.multiple_of(at * block, block), block)
            paired[at] = (own[here] + swapped[here].astype(F32)).astype(BF16)

        for peer in peers:
            scatter(peer).start()
        parts[h] = paired[h]
        for peer in peers:
            scatter_in(peer).wait_recv()
        groups = [jnp.zeros((block, D), F32), jnp.zeros((block, D), F32)]
        for pair in range(count):
            groups[int(pair % 4 == 3)] += parts[pair].astype(F32)
        both = groups[0] + groups[1]
        sums[0] = jnp.where(apart, groups[0], both).astype(BF16)
        sums[1] = jnp.where(apart, groups[1], both).astype(BF16)
        for peer in peers:
            share(peer).start()
        gram[block_at(h, core)] = sums[mine]
        forward(h).start()
        for peer in peers:
            share_in(peer).wait_recv()
            forward(peer).start()
        for pair in [h] + peers:
            forward_in(pair).wait_recv()
        for peer in peers:
            scatter(peer).wait_send()
            share(peer).wait_send()
        for pair in [h] + peers:
            forward(pair).wait_send()
        if turn == 1:
            relay.step(2)

        scale = jnp.ones((1, 1), F32)
        if turn == 0:
            trace = jnp.zeros((1, 1), F32)
            for at in range(D // 128):
                square = gram[at * 128 : (at + 1) * 128, at * 128 : (at + 1) * 128].astype(F32)
                row = lax.broadcasted_iota(jnp.int32, square.shape, 0)
                column = lax.broadcasted_iota(jnp.int32, square.shape, 1)
                trace += jnp.sum(jnp.where(row == column, square, 0.0), keepdims=True)
            scale = 1.0 / (jnp.sqrt(trace) + ORTHO_EPS)

            @pl.loop(0, D // tile)
            def _(at):
                here = pl.ds(pl.multiple_of(at * tile, tile), tile)
                gram[here] = (gram[here].astype(F32) * scale * scale).astype(BF16)

        def each_tile(work):
            @pl.loop(0, D // tile)
            def _(at):
                work(pl.ds(pl.multiple_of(at * tile, tile), tile))

        def polynomial(values, whole):
            return (
                QUINTIC_SECOND * values.astype(F32) + QUINTIC_THIRD * dot(values, whole[...])
            ).astype(BF16)

        def first_poly(here):
            poly[here] = polynomial(gram[here], gram)

        def halfway(here):
            half_way[here] = (
                QUINTIC_FIRST * gram[here].astype(F32) + dot(poly[here], gram[...])
            ).astype(BF16)

        def next_gram(here):
            gram[here] = (
                QUINTIC_FIRST * half_way[here].astype(F32) + dot(half_way[here], poly[...])
            ).astype(BF16)

        def second_poly(here):
            half_way[here] = polynomial(gram[here], gram)

        for work in (first_poly, halfway, next_gram, second_poly):
            each_tile(work)

        @pl.loop(0, columns // slab)
        def _(at):
            here = pl.ds(pl.multiple_of(at * slab, slab), slab)
            new = QUINTIC_FIRST * out[here].astype(F32) + dot(out[here], poly[...])
            if turn == 0:
                new = new * scale
            new = QUINTIC_FIRST * new + dot(new.astype(BF16), half_way[...])
            if turn < NS_ITERS // 2 - 1:
                out[here] = new.astype(BF16)
            else:
                for to in range(seqs):
                    cut_ortho[at, to] = new[:, to * block : (to + 1) * block].astype(BF16)
                home_ortho.drop(at)

        if turn == 0:
            home_grad.spread()
            relay.step(1)

    home_ortho.spread()
    home_grad.finish()
    relay.finish()
    home_ortho.finish()


def orthogonalize(seqs, chans, grad, moment, input_grad):
    dma = pltpu.SemaphoreType.DMA
    count, block, held = seqs // 2, D // seqs, PIECES // seqs
    return call(
        functools.partial(ortho_kernel, seqs, chans),
        [jax.ShapeDtypeStruct((chans, PER_CHAN, PIECE, block), BF16)] * 2
        + [jax.ShapeDtypeStruct((chans,) + input_grad.shape, BF16)],
        [pltpu.VMEM] * 2 + [pl.ANY],
        [pl.ANY] * 3,
        [
            pltpu.VMEM(grad.shape, BF16),
            pltpu.VMEM((held, seqs, PIECE, block), BF16),
            pltpu.VMEM((held, seqs, PIECE, block), BF16),
            pltpu.VMEM((chans, seqs, PIECE, block), BF16),
            pltpu.VMEM((chans, seqs, PIECE, block), BF16),
            pltpu.VMEM((D // 2, D), BF16),
            pltpu.VMEM((D // 2, D), F32),
            pltpu.VMEM((D // 2, D), BF16),
            pltpu.VMEM((count, block, D), BF16),
            pltpu.VMEM((count, block, D), BF16),
            pltpu.VMEM((2, block, D), BF16),
            pltpu.VMEM((D, D), BF16),
            pltpu.VMEM((D, D), BF16),
            pltpu.VMEM((D, D), BF16),
            dma(()),
            dma(()),
        ]
        + [dma((count,))] * 6
        + Homeward.semaphores(seqs, chans) * 2
        + Relay.semaphores(chans),
        2,
        grad,
        moment,
        input_grad,
    )


HEAD = 8


def own_rows(values, seqs_held):
    length = values.shape[0] // seqs_held
    return [values[s * length + HEAD : (s + 1) * length] for s in range(seqs_held)]


def row_scale(values):
    return lax.rsqrt(jnp.mean(values * values, axis=1, keepdims=True) + NORM_EPS)


def filtering(gated, taps, keep_one, keep_two):
    back_one, back_two = pltpu.roll(gated, 1, 0), pltpu.roll(gated, 2, 0)
    return taps[2:3] * gated + taps[1:2] * keep_one * back_one + taps[0:1] * keep_two * back_two


def forward_kernel(seqs, chans, held, *refs):
    forward_work(seqs, chans, held, refs[:5], refs[5:10], *refs[10:])


def forward_work(
    seqs, chans, held,
    weights, moments, own_taps, token_source, cotangent_source, keeps, gains,
    in_full, out_full, ffn_full, taps_all, held_out, between, streams, ffn_g,
    tokens, cotangent, residual, second_grad, block_out,
    in_shard, out_shard, ffn_shard, taps, packed, shelf, shelf_sem,
    u, u_own, halo, row_sem, halo_sem, halo_send, halo_recv, normed, mixed, stream, x, x_own, ffn_out, act, gate_low, up_low, in_v, out_v, taps_v, w_v, grad_v,
    own_sem, z_send, z_recv, b_send, b_recv, c_send, c_recv,
    t_own, t_send, t_recv, p_own, ps_send, ps_recv, pl_send, pl_recv,
    mix_sem, taps_sem, stream_sem, load_sem, grad_sem,
):
    bits = seqs.bit_length() - 1
    r, c = lax.axis_index("seq"), lax.axis_index("chan")
    last = TILES + 1
    greet(
        [{"chan": lax.rem(c + off, chans)} for off in range(1, chans)]
        + [{"seq": lax.rem(r + off, seqs)} for off in range(1, seqs)]
    )

    def shard(k):
        if isinstance(k, int) and k < 2:
            return (in_shard, out_shard)[k]
        return ffn_shard.at[k - 2]

    def full(k, part, block):
        if isinstance(k, int) and k < 2:
            return (in_full, out_full)[k].at[part, block]
        return ffn_full.at[k - 2, part, block]

    def own(k):
        return pltpu.make_async_copy(shard(k), full(k, c, r), own_sem.at[k])

    def along_chan(k, off, incoming):
        source = lax.rem(c + chans - off, chans) if incoming else c
        return remote(
            shard(k), full(k, source, r), z_send.at[k, off - 1], z_recv.at[k, off - 1],
            chan=lax.rem(c + off, chans),
        )

    def across(k, half, step, incoming):
        order = high_bits(bits, half)
        bit, done = order[step], order[:step]
        base = flip(r, bit) if incoming else r
        part = pl.ds(half * (chans // 2), chans // 2)
        first = (1 << step) - 1
        return [
            remote(
                full(k, part, block), full(k, part, block),
                b_send.at[k, half, first + at], b_recv.at[k, half, first + at], seq=flip(r, bit),
            )
            for at, block in enumerate(flips(base, done))
        ]

    def core(k, incoming):
        base = flip(r, 0) if incoming else r
        return [
            remote(
                full(k, slice(None), block), full(k, slice(None), block),
                c_send.at[k, at], c_recv.at[k, at], seq=flip(r, 0),
            )
            for at, block in enumerate(flips(base, range(1, bits)))
        ]

    def start_chan(k):
        own(k).start()
        for off in (2, 1, 3):
            along_chan(k, off, False).start()

    def first_level(k):
        own(k).wait()
        for off in range(1, chans):
            along_chan(k, off, True).wait_recv()
        for half in range(2):
            for copy in across(k, half, 0, False):
                copy.start()

    def next_level(k, level):
        for half in range(2):
            for copy in across(k, half, level - 1, True):
                copy.wait_recv()
            for copy in across(k, half, level, False):
                copy.start()

    def to_core(k):
        for half in range(2):
            for copy in across(k, half, bits - 2, True):
                copy.wait_recv()
        for copy in core(k, False):
            copy.start()

    def arrived(k):
        for copy in core(k, True):
            copy.wait_recv()

    def sent(k):
        for off in range(1, chans):
            along_chan(k, off, False).wait_send()
        for half in range(2):
            for step in range(bits - 1):
                for copy in across(k, half, step, False):
                    copy.wait_send()
        for copy in core(k, False):
            copy.wait_send()

    def taps_copy(off, incoming):
        source = lax.rem(c + chans - off, chans) if incoming else c
        return remote(
            taps, taps_all.at[source], t_send.at[off - 1], t_recv.at[off - 1],
            chan=lax.rem(c + off, chans),
        )

    _, has, place = holder(r, c, seqs)

    def spread(piece, r_to):
        return remote(
            packed.at[:, piece], between.at[:, r], ps_send.at[piece], ps_recv.at[r], seq=r_to
        )

    def lift(m):
        return remote(between.at[m], held_out.at[place], pl_send.at[m], pl_recv.at[place], chan=m)

    def pieces_start():
        for piece in range(PER_CHAN):
            r_to = lax.rem(PER_CHAN * c + piece, seqs)

            @pl.when(r_to != r)
            def _():
                spread(piece, r_to).start()

            @pl.when(r_to == r)
            def _():
                pltpu.make_async_copy(packed.at[:, piece], between.at[:, r], p_own.at[0]).start()

    def pieces_lift():
        @pl.when(has)
        def _():
            pltpu.make_async_copy(packed.at[:, 0], between.at[:, r], p_own.at[0]).wait()
            for off in range(1, seqs):
                r_from = lax.rem(r + off, seqs)
                remote(
                    packed.at[:, 0], between.at[:, r_from], ps_send.at[0], ps_recv.at[r_from], seq=r_from
                ).wait_recv()
            for m in range(chans):

                @pl.when(m != c)
                def _():
                    lift(m).start()

                @pl.when(m == c)
                def _():
                    copy = pltpu.make_async_copy(between.at[m], held_out.at[place], p_own.at[1])
                    copy.start()
                    copy.wait()

    def pieces_finish():
        for at in range(PIECES // seqs):
            c_from = lax.div(r + seqs * at, PER_CHAN)

            @pl.when(c_from != c)
            def _():
                remote(
                    between.at[0], held_out.at[at], pl_send.at[0], pl_recv.at[at], chan=c_from
                ).wait_recv()

        for piece in range(PER_CHAN):
            r_to = lax.rem(PER_CHAN * c + piece, seqs)

            @pl.when(r_to != r)
            def _():
                spread(piece, r_to).wait_send()

        @pl.when(has)
        def _():
            for m in range(chans):

                @pl.when(m != c)
                def _():
                    lift(m).wait_send()

    rows, width = tokens.shape
    part = out_full.shape[-1]
    tile = rows // 3
    per_tile = held // 3
    size = rows // held - HEAD
    tiles = [pl.ds(at * tile, tile) for at in range(3)]

    def mix_loads(j):
        slot = lax.rem(j, 2)
        return [
            pltpu.make_async_copy(in_full.at[j], in_v.at[slot], mix_sem.at[slot, 0]),
            pltpu.make_async_copy(out_full.at[j], out_v.at[slot], mix_sem.at[slot, 1]),
        ]

    def stream_out(j):
        return pltpu.make_async_copy(stream, streams.at[j], stream_sem)

    local_rows = token_source.shape[1]
    before_at = pl.multiple_of(lax.rem(c + chans - 1, chans) * size + size - HEAD, HEAD)
    after_at = pl.multiple_of(lax.rem(c + 1, chans) * size, HEAD)
    halos = [
        (token_source, before_at, c == 0, r > 0, r < seqs - 1, 1),
        (token_source, after_at, c == chans - 1, r < seqs - 1, r > 0, -1),
        (cotangent_source, after_at, c == chans - 1, r < seqs - 1, r > 0, -1),
    ]

    def row_copies():
        return [
            pltpu.make_async_copy(
                source.at[s, pl.ds(pl.multiple_of(c * size, size), size)],
                rows_to.at[pl.ds(s * (size + HEAD) + HEAD, size)],
                row_sem.at[n, s],
            )
            for n, (source, rows_to) in enumerate(
                ((token_source, tokens), (cotangent_source, cotangent))
            )
            for s in range(held)
        ]

    def halo_local(n):
        source, at, _, _, _, _ = halos[n]
        return pltpu.make_async_copy(source.at[:, pl.ds(at, HEAD)], halo.at[n], halo_sem.at[n])

    def halo_remote(n):
        source, at, _, _, _, step = halos[n]
        return remote(
            source.at[:, pl.ds(at, HEAD)], halo.at[n], halo_send.at[n], halo_recv.at[n], seq=r + step
        )

    def rows_start():
        for copy in row_copies():
            copy.start()
        for n, (_, _, edge, takes, gives, _) in enumerate(halos):

            @pl.when(jnp.logical_not(edge))
            def _():
                halo_local(n).start()

            @pl.when(edge & gives)
            def _():
                halo_remote(n).start()

            @pl.when(edge & jnp.logical_not(takes))
            def _():
                halo[n] = jnp.zeros(halo.shape[1:], F32)

    def rows_finish():
        for copy in row_copies():
            copy.wait()
        for n, (_, _, edge, takes, gives, _) in enumerate(halos):

            @pl.when(jnp.logical_not(edge))
            def _():
                halo_local(n).wait()

            @pl.when(edge & takes)
            def _():
                halo_remote(n).wait_recv()

            @pl.when(edge & gives)
            def _():
                halo_remote(n).wait_send()

        row = lax.broadcasted_iota(jnp.int32, (HEAD, width), 0)
        for s in range(held):
            head = pl.ds(s * (size + HEAD), HEAD)
            earlier = (s - 1) % held
            tokens[head] = jnp.where(row < 2, halo[1, earlier], halo[0, s])
            cotangent[head] = jnp.where(row < 2, halo[2, earlier], 0.0)
        for at, here in enumerate(tiles):
            values = cotangent[here]
            u[here] = values.astype(BF16)
            for s, one in enumerate(own_rows(values, per_tile)):
                u_own[pl.ds((at * per_tile + s) * size, size)] = one.astype(BF16)

    def mix_prepare():
        rows_finish()
        for here in tiles:
            values = tokens[here]
            normed[here] = (values * row_scale(values) * gains[0:1]).astype(BF16)
            residual[here] = values

    def mix():
        for copy in mix_loads(0):
            copy.start()
        copy = pltpu.make_async_copy(taps_all, taps_v, taps_sem)
        copy.start()
        copy.wait()

        @pl.loop(0, chans)
        def _(j):
            slot = lax.rem(j, 2)
            for copy in mix_loads(j):
                copy.wait()

            @pl.when(j + 1 < chans)
            def _():
                for copy in mix_loads(j + 1):
                    copy.start()

            @pl.when(j > 0)
            def _():
                stream_out(j - 1).wait()

            in_w = in_v[slot].reshape(width, 3 * part)
            out_w = out_v[slot].reshape(width, part)
            for here in tiles:
                stream[here] = dot(normed[here], in_w)
            filters = taps_v[j]
            gated = stream[:, 0:part] * stream[:, 2 * part :]
            filtered = filtering(gated, filters, keeps[:, 0:1], keeps[:, 1:2])
            mixed[...] = (stream[:, part : 2 * part] * filtered).astype(BF16)
            stream_out(j).start()
            for here in tiles:
                residual[here] += contract_last(mixed[here], out_w)

        for at, here in enumerate(tiles):
            values = residual[here]
            new = values * row_scale(values) * gains[1:2]
            x[here] = new.astype(BF16)
            for s, one in enumerate(own_rows(new, per_tile)):
                x_own[pl.ds((at * per_tile + s) * size, size)] = one.astype(BF16)
            ffn_out[here] = jnp.zeros((tile, width), F32)
            second_grad[here] = jnp.zeros((tile, width), F32)
        stream_out(chans - 1).wait()

    def loads(t):
        slot = lax.rem(t, 2)
        return [
            pltpu.make_async_copy(
                ffn_full.at[t, j, :, m],
                w_v.at[slot, m, :, :, pl.ds(j * LANES, LANES)],
                load_sem.at[slot, m, j],
            )
            for m in range(3)
            for j in range(chans)
        ]

    def grads_out(t):
        slot = lax.rem(t, 2)
        return [
            pltpu.make_async_copy(grad_v.at[slot, m], ffn_g.at[m, :, t], grad_sem.at[slot, m])
            for m in range(3)
        ]

    def feed_forward(t):
        slot = lax.rem(t, 2)
        for copy in loads(t):
            copy.wait()

        @pl.when(t >= 2)
        def _():
            for copy in grads_out(t - 2):
                copy.wait()

        wg, wu, wd = (w_v[slot, m].reshape(width, chans * LANES) for m in range(3))
        for at, here in enumerate(tiles):
            gate = dot(x[here], wg)
            up = dot(x[here], wu)
            grad = dot(u[here], wd)
            sigmoid = jax.nn.sigmoid(gate)
            silu = gate * sigmoid
            new_act = silu * up
            new_gate = grad * up * sigmoid * (1.0 + gate * (1.0 - sigmoid))
            new_up = grad * silu
            for ref, values in ((act, new_act), (gate_low, new_gate), (up_low, new_up)):
                for s, one in enumerate(own_rows(values, per_tile)):
                    ref[pl.ds((at * per_tile + s) * size, size)] = one.astype(BF16)
            ffn_out[here] += contract_last(new_act.astype(BF16), wd)
            second_grad[here] += contract_last(new_gate.astype(BF16), wg) + contract_last(
                new_up.astype(BF16), wu
            )
        for m, (low, right) in enumerate(((gate_low, x_own), (up_low, x_own), (act, u_own))):
            grad_v[slot, m] = (
                contract_first(low[...], right[...]).astype(BF16).reshape(PIECES, UNIT, width)
            )
        for copy in grads_out(t):
            copy.start()

    def shelf_copies(group, n):
        slot = n % 2
        if n % 4 == 0:
            part_of = [(group[0].at[k], k) for k in range(3)] + [(group[1], 3)]
            return [
                pltpu.make_async_copy(
                    source, shelf.at[slot, :, pl.ds(k * part, part)], shelf_sem.at[slot, k]
                )
                for source, k in part_of
            ]
        return [pltpu.make_async_copy(group[n % 4 + 1], shelf.at[slot], shelf_sem.at[slot, 0])]

    def shelves(n):
        return shelf_copies(weights if n < 4 else moments, n)

    for copy in shelves(0):
        copy.start()
    taps[...] = jnp.zeros_like(taps)
    taps[0:3] = own_taps[...]
    rows_start()
    for n in range(8):
        if n < 7:
            for copy in shelves(n + 1):
                copy.start()
        for copy in shelves(n):
            copy.wait()
        slot, m = n % 2, n % 4 - 1
        if n == 0:
            in_shard[...] = shelf[slot, :, : 3 * part].astype(BF16)
            out_shard[...] = shelf[slot, :, 3 * part : 4 * part].astype(BF16)
            start_chan(0)
            start_chan(1)
        elif n < 4:
            for t in range(TILES):
                ffn_shard[t, m] = shelf[slot, :, t * LANES : (t + 1) * LANES].astype(BF16)
        elif n == 4:
            packed[3] = jnp.zeros(packed.shape[1:], BF16)
            for q in range(PER_CHAN):
                block = shelf[slot, :, q * SMALL_PIECE : (q + 1) * SMALL_PIECE]
                packed[3, q, 0:SMALL_PIECE] = block.T.astype(BF16)
        else:
            for t in range(TILES):
                block = shelf[slot, :, t * LANES : (t + 1) * LANES].T.astype(BF16)
                packed[m, :, t * UNIT : (t + 1) * UNIT] = block.reshape(PER_CHAN, UNIT, -1)
    pieces_start()
    taps_own = pltpu.make_async_copy(taps, taps_all.at[c], t_own)
    taps_own.start()
    for off in range(1, chans):
        taps_copy(off, False).start()
    mix_prepare()

    for tick in range(bits + 2):
        start_chan(tick + 2)
        first_level(tick)
        for level in range(1, bits - 1):
            if tick >= level:
                next_level(tick - level, level)
        if tick >= bits - 1:
            to_core(tick - bits + 1)
        if tick >= bits:
            arrived(tick - bits)
        if tick == 1:
            pieces_lift()
    taps_own.wait()
    for off in range(1, chans):
        taps_copy(off, True).wait_recv()
    mix()

    @pl.loop(bits + 2, last + bits + 2)
    def _(tick):
        @pl.when(tick + 2 <= last)
        def _():
            start_chan(tick + 2)

        @pl.when(tick <= last)
        def _():
            first_level(tick)

        for level in range(1, bits - 1):

            @pl.when(tick - level <= last)
            def _():
                next_level(tick - level, level)

        @pl.when(tick - bits + 1 <= last)
        def _():
            to_core(tick - bits + 1)

        @pl.when(tick - bits <= last)
        def _():
            arrived(tick - bits)
            for copy in loads(tick - bits - 2):
                copy.start()

        @pl.when(tick - bits - 3 >= 0)
        def _():
            feed_forward(tick - bits - 3)

    for s in range(held):
        here = pl.ds(s * (size + HEAD) + HEAD, size)
        block_out[pl.ds(s * size, size)] = (residual[here] + ffn_out[here]).astype(BF16)
    for t in (TILES - 2, TILES - 1):
        for copy in grads_out(t):
            copy.wait()
    pieces_finish()
    for off in range(1, chans):
        taps_copy(off, False).wait_send()
    sent(0)
    sent(1)

    @pl.loop(2, last + 1)
    def _(k):
        sent(k)


def forward_pass(seqs, chans, weights, moments, taps, tokens, cotangent, keeps, gains):
    held, local_rows, width = tokens.shape
    block, part = weights[1].shape
    own_count, hidden = held * local_rows // chans, chans * LANES
    rows = own_count + held * HEAD
    tail = (PIECE, block)
    shape = jax.ShapeDtypeStruct
    outs = [
        shape((chans, seqs, block, 3 * part), BF16),
        shape((chans, seqs, block, part), BF16),
        shape((TILES, chans, seqs, 3, block, LANES), BF16),
        shape((chans, 8, part), F32),
        shape((PIECES // seqs, seqs) + tail, BF16),
        shape((chans, seqs) + tail, BF16),
        shape((chans, rows, 3 * part), F32),
    ]
    outs.append(shape((3, PIECES, TILES, UNIT, width), BF16))
    outs += [shape((rows, width), F32)] * 4 + [shape((own_count, width), BF16)]
    dma = pltpu.SemaphoreType.DMA
    count = TILES + 2
    vmem = pltpu.VMEM
    found = call(
        functools.partial(forward_kernel, seqs, chans, held),
        outs,
        [pl.ANY] * 10 + [vmem] + [pl.ANY] * 2 + [vmem] * 2,
        [pl.ANY] * 8 + [vmem] * 5,
        [
            vmem((block, 3 * part), BF16),
            vmem((block, part), BF16),
            vmem((TILES, 3, block, LANES), BF16),
            vmem((8, part), F32),
            vmem((chans, PER_CHAN) + tail, BF16),
            vmem((2, block, TILES * LANES), F32),
            dma((2, 4)),
            vmem((rows, width), BF16),
            vmem((own_count, width), BF16),
            vmem((3, held, HEAD, width), F32),
            dma((2, held)),
            dma((3,)),
            dma((3,)),
            dma((3,)),
            vmem((rows, width), BF16),
            vmem((rows, part), BF16),
            vmem((rows, 3 * part), F32),
            vmem((rows, width), BF16),
            vmem((own_count, width), BF16),
            vmem((rows, width), F32),
            vmem((own_count, hidden), BF16),
            vmem((own_count, hidden), BF16),
            vmem((own_count, hidden), BF16),
            vmem((2, seqs, block, 3 * part), BF16),
            vmem((2, seqs, block, part), BF16),
            vmem((chans, 8, part), F32),
            vmem((2, 3, seqs, block, hidden), BF16),
            vmem((2, 3, PIECES, UNIT, width), BF16),
            dma((count,)),
            dma((count, chans - 1)),
            dma((count, chans - 1)),
            dma((count, 2, seqs // 2 - 1)),
            dma((count, 2, seqs // 2 - 1)),
            dma((count, seqs // 2)),
            dma((count, seqs // 2)),
            dma(()),
            dma((chans - 1,)),
            dma((chans - 1,)),
            dma((2,)),
            dma((PER_CHAN,)),
            dma((seqs,)),
            dma((chans,)),
            dma((PIECES // seqs,)),
            dma((2, 2)),
            dma(()),
            dma(()),
            dma((2, 3, chans)),
            dma((2, 3)),
        ],
        0,
        *weights, *moments, taps, tokens, cotangent, keeps, gains,
        vmem=62,
    )
    return found


LAG = 2


def add_rows(acc, other):
    return (acc.astype(F32) + other.astype(F32)).astype(BF16)


def backward_kernel(
    seqs, chans, held,
    ffn_g, in_full, out_full, streams, block_own,
    tokens, residual, second_grad, cotangent, keeps, gains, taps,
    result, total, input_grad, io_g, blocks, *refs
):
    bits = seqs.bit_length() - 1
    levels = bits - 1
    landed, line_land = refs[: levels + 1], refs[levels + 1]
    temps, refs = refs[levels + 2 : 2 * levels + 3], refs[2 * levels + 3 :]
    (
        acc, line_temp, sent, got, sums,
        residual_low, low_own, first_own, residual_grad, stream_own, mixed_own, mixer_grad, first_grad,
        stream, in_v, out_v, staging,
        load_sem, temp_sem, fetch_sem, c_send, c_recv, b_send, b_recv, z_send, z_recv, n_send, n_recv,
        mix_sem, io_sem, *relay_sems
    ) = refs
    parts, half_seqs = PIECES // seqs, seqs // 2
    chunks = chans * parts
    slots, group = acc.shape[0], temps[0].shape[0]
    at_once = group == half_seqs
    r, c = lax.axis_index("seq"), lax.axis_index("chan")
    core, h = lax.rem(r, 2), lax.div(r, 2)
    partners = [{"seq": flip(r, bit)} for bit in range(bits)]
    greet(partners + [{"chan": lax.rem(c + off, chans)} for off in range(1, chans)])
    partners += [{"chan": flip(c, bit)} for bit in range(chans.bit_length() - 1)]

    def slot_of(k):
        return lax.rem(k, slots)

    def core_copy(k, source):
        return remote(source.at[:, 1 - core], landed[0].at[k], c_send.at[k], c_recv.at[k], seq=flip(r, 0))

    def load(k, source):
        return pltpu.make_async_copy(source.at[:, core], acc.at[slot_of(k)], load_sem.at[k])

    def with_source(k, work):
        @pl.when(k < 3 * parts)
        def _():
            work(ffn_g.at[lax.div(k, parts), lax.rem(k, parts)])

        @pl.when(k >= 3 * parts)
        def _():
            work(io_g.at[k - 3 * parts])

    def lanes(half):
        return pl.ds(half * (D // 2), D // 2)

    def across(k, half, level):
        order = high_bits(bits, half)
        bit, rest = order[level], [one - 1 for one in order[level + 1 :]]
        base = h
        for one in rest:
            base = base - (1 << one) * lax.rem(lax.div(h, 1 << one), 2)
        first = half_seqs - (half_seqs >> level)
        copies, keeps = [], []
        for at in range(1 << len(rest)):
            place = base + sum((1 << one) for n, one in enumerate(rest) if at >> n & 1)
            copies.append(
                remote(
                    acc.at[slot_of(k), flip(place, bit - 1), :, lanes(half)],
                    landed[level + 1].at[k, at, :, lanes(half)],
                    b_send.at[k, half, first + at], b_recv.at[k, half, first + at],
                    seq=flip(r, bit),
                )
            )
            keeps.append(place)
        return copies, keeps

    def fetch(src, dst):
        copy = pltpu.make_async_copy(src, dst, temp_sem)
        copy.start()
        copy.wait()

    def begin(k):
        def work(source):
            core_copy(k, source).start()
            load(k, source).start()

        with_source(k, work)

    def level_start(k, level):
        for half in range(2):
            for copy in across(k, half, level)[0]:
                copy.start()

    def fetch_level(k, level):
        return pltpu.make_async_copy(landed[level].at[k], temps[level], fetch_sem.at[level])

    def core_arrive(k):
        load(k, io_g.at[0]).wait()
        core_copy(k, io_g.at[0]).wait_recv()
        if at_once:
            fetch_level(k, 0).start()

    def core_sum(k):
        if at_once:
            fetch_level(k, 0).wait()
        for start in range(0, half_seqs, group):
            if not at_once:
                fetch(landed[0].at[k, pl.ds(start, group)], temps[0])

            @pl.loop(0, group)
            def _(b):
                acc[slot_of(k), start + b] = add_rows(acc[slot_of(k), start + b], temps[0][b])

        level_start(k, 0)

    def level_arrive(k, level):
        for half in range(2):
            for copy in across(k, half, level)[0]:
                copy.wait_recv()
        if at_once:
            fetch_level(k, level + 1).start()

    def level_sum(k, level):
        both = [across(k, half, level) for half in range(2)]
        if at_once:
            fetch_level(k, level + 1).wait()
        temp = temps[level + 1 if at_once else 0]
        count = half_seqs >> (level + 1)
        for start in range(0, count, group):
            here = min(group, count - start)
            if not at_once:
                fetch(landed[level + 1].at[k, pl.ds(start, here)], temp.at[pl.ds(0, here)])
            for half in range(2):
                for at in range(here):
                    place = both[half][1][start + at]
                    acc[slot_of(k), place, :, lanes(half)] = add_rows(
                        acc[slot_of(k), place, :, lanes(half)], temp[at, :, lanes(half)]
                    )
        if level + 1 < levels:
            level_start(k, level + 1)

    def line(k, side):
        return remote(
            acc.at[slot_of(k), h], line_land.at[side, k], z_send.at[k], z_recv.at[side, k],
            chan=c + 1 - 2 * side,
        )

    def hop(k, step):
        keeper = lax.div(k, parts)
        for side, sends in ((0, (c < keeper) & (c == step)), (1, (c > keeper) & (chans - 1 - c == step))):

            @pl.when(sends)
            def _():
                if step > 0:
                    line(k, side).wait_recv()
                    fetch(line_land.at[side, k], line_temp.at[0])
                    acc[slot_of(k), h] = add_rows(acc[slot_of(k), h], line_temp[0])
                line(k, side).start()

    def finish(k):
        keeper = lax.div(k, parts)

        @pl.when(c == keeper)
        def _():
            for side, there in ((0, c > 0), (1, c < chans - 1)):

                @pl.when(there)
                def _():
                    line(k, side).wait_recv()
                    fetch(line_land.at[side, k], line_temp.at[side])

                @pl.when(jnp.logical_not(there))
                def _():
                    line_temp[side] = jnp.zeros(line_temp.shape[1:], BF16)

            result[lax.rem(k, parts)] = (
                acc[slot_of(k), h].astype(F32) + line_temp[0].astype(F32) + line_temp[1].astype(F32)
            ).astype(BF16)

        @pl.when(c < keeper)
        def _():
            line(k, 0).wait_send()

        @pl.when(c > keeper)
        def _():
            line(k, 1).wait_send()

        core_copy(k, io_g.at[0]).wait_send()
        for level in range(levels):
            for half in range(2):
                for copy in across(k, half, level)[0]:
                    copy.wait_send()

    def small_copy(level):
        return remote(
            sent.at[level], got.at[level], n_send.at[level], n_recv.at[level], **partners[level]
        )

    def small_step(level):
        if level == 0:
            sent[0] = sums[...]
        else:
            small_copy(level - 1).wait()
            new = sent[level - 1] + got[level - 1]
            if level == len(partners):
                total[...] = new
            else:
                sent[level] = new
        if level < len(partners):
            small_copy(level).start()

    rows, full = tokens.shape
    width = out_v.shape[-1]
    length = rows // held
    size = length - HEAD
    tile, per_tile = rows // 3, held // 3
    tiles = [pl.ds(at * tile, tile) for at in range(3)]
    own_tiles = [pl.ds(at * per_tile * size, per_tile * size) for at in range(3)]

    def mix_loads(j):
        return [
            pltpu.make_async_copy(in_full.at[j], in_v, mix_sem.at[0]),
            pltpu.make_async_copy(out_full.at[j], out_v, mix_sem.at[1]),
            pltpu.make_async_copy(streams.at[j], stream, mix_sem.at[2]),
        ]

    def io_out(j):
        at, first = lax.div(4 * j, half_seqs), lax.rem(4 * j, half_seqs)
        return pltpu.make_async_copy(staging, io_g.at[at, pl.ds(first, 4)], io_sem)

    def mix_prepare():
        gain_sum = jnp.zeros((1, full), F32)
        for at, here in enumerate(tiles):
            values = residual[here]
            scale = row_scale(values)
            unit = values * scale
            grad = second_grad[here]
            scaled = grad * gains[1:2]
            new = cotangent[here] + scale * (
                scaled - unit * jnp.mean(scaled * unit, axis=1, keepdims=True)
            )
            residual_low[here] = new.astype(BF16)
            for s, (one, two) in enumerate(
                zip(own_rows(new, per_tile), own_rows(grad * unit, per_tile))
            ):
                where = pl.ds((at * per_tile + s) * size, size)
                residual_grad[where] = one
                low_own[where] = one.astype(BF16)
                gain_sum += jnp.sum(two, axis=0, keepdims=True)
            first = tokens[here]
            first = first * row_scale(first) * gains[0:1]
            for s, one in enumerate(own_rows(first, per_tile)):
                first_own[pl.ds((at * per_tile + s) * size, size)] = one.astype(BF16)
        sums[...] = jnp.zeros_like(sums)
        sums[1:2] = gain_sum
        first_grad[...] = jnp.zeros_like(first_grad)
        staging[...] = jnp.zeros_like(staging)

    def mix_step(j):
        for copy in mix_loads(j):
            copy.wait()
        in_w, out_w = in_v[...].reshape(full, 3 * width), out_v[...].reshape(full, width)
        filters = taps[j]
        for here in tiles:
            mixer_grad[here] = dot(residual_low[here], out_w)
        input_gate, output_gate, value = (
            stream[:, k * width : (k + 1) * width] for k in range(3)
        )
        keep_one, keep_two = keeps[:, 0:1], keeps[:, 1:2]
        gated = input_gate * value
        back_one, back_two = pltpu.roll(gated, 1, 0), pltpu.roll(gated, 2, 0)
        filtered = (
            filters[2:3] * gated
            + filters[1:2] * keep_one * back_one
            + filters[0:1] * keep_two * back_two
        )
        grad = mixer_grad[...]
        inner = grad * output_gate
        one, two = keep_one * inner, keep_two * inner
        gated_grad = (
            filters[2:3] * inner
            + filters[1:2] * pltpu.roll(one, rows - 1, 0)
            + filters[0:1] * pltpu.roll(two, rows - 2, 0)
        )

        def own_sum(values):
            return sum(jnp.sum(part, axis=0, keepdims=True) for part in own_rows(values, held))

        where = pl.ds(pl.multiple_of(j * width, width), width)
        sums[4:5, where] = own_sum(inner * gated)
        sums[3:4, where] = own_sum(one * back_one)
        sums[2:3, where] = own_sum(two * back_two)
        for k, values in enumerate((gated_grad * value, grad * filtered, gated_grad * input_gate)):
            for s, part in enumerate(own_rows(values, held)):
                stream_own[pl.ds(s * size, size), k * width : (k + 1) * width] = part.astype(BF16)
        for s, part in enumerate(own_rows(output_gate * filtered, held)):
            mixed_own[pl.ds(s * size, size)] = part.astype(BF16)
        for here in own_tiles:
            first_grad[here] += contract_last(stream_own[here], in_w)

        @pl.when(j > 0)
        def _():
            io_out(j - 1).wait()

        for k in range(4):
            if k < 3:
                new = contract_first(stream_own[:, k * width : (k + 1) * width], first_own[...])
            else:
                new = contract_first(mixed_own[...], low_own[...])
            staging[k, :, pl.ds(0, SMALL_PIECE)] = new.astype(BF16).reshape(2, SMALL_PIECE, full)
        io_out(j).start()

        @pl.when(j + 1 < chans)
        def _():
            for copy in mix_loads(j + 1):
                copy.start()

    def mix_end():
        gain_sum = jnp.zeros((1, full), F32)
        for s in range(held):
            here = pl.ds(s * size, size)
            values = tokens[pl.ds(s * length + HEAD, size)]
            scale = row_scale(values)
            unit = values * scale
            grad = first_grad[here]
            scaled = grad * gains[0:1]
            gain_sum += jnp.sum(grad * unit, axis=0, keepdims=True)
            input_grad[here] = (
                residual_grad[here]
                + scale * (scaled - unit * jnp.mean(scaled * unit, axis=1, keepdims=True))
            ).astype(BF16)
        sums[0:1] = gain_sum
        io_out(chans - 1).wait()

    spread_out = parts == 4
    mix_first, mix_last = (1, 3 * parts - 2) if spread_out else (-1, -1)
    relay = Relay(chans, block_own, blocks, relay_sems)
    for copy in mix_loads(0):
        copy.start()
    begin(0)
    relay.step(0)
    mix_prepare()
    if not spread_out:

        @pl.loop(0, chans)
        def _(j):
            mix_step(j)

        mix_end()

    summed = LAG * (1 + levels)

    @pl.loop(1, chunks + summed + LAG * (chans - 1))
    def _(tick):
        def stage(k, work):
            @pl.when((k >= 0) & (k < chunks))
            def _():
                work(k)

        stage(tick - summed - LAG * (chans - 1), finish)
        stage(tick, begin)
        for step in range(chans - 2, 0, -1):
            stage(tick - summed - LAG * step, lambda k: hop(k, step))
        for level in range(levels - 1, -1, -1):
            stage(tick - LAG * (2 + level), lambda k: level_arrive(k, level))
        stage(tick - LAG, core_arrive)
        for level in range(levels - 1, -1, -1):

            def work(k):
                level_sum(k, level)
                if level == levels - 1:
                    hop(k, 0)

            stage(tick - LAG * (2 + level), work)
        stage(tick - LAG, core_sum)
        if spread_out:

            @pl.when((tick >= mix_first) & (tick < mix_first + 2 * chans) & (lax.rem(tick - mix_first, 2) == 0))
            def _():
                mix_step(lax.div(tick - mix_first, 2))

            @pl.when(tick == mix_last)
            def _():
                mix_end()

        for level in range(len(partners) + 1):

            @pl.when(tick == mix_last + 2 + level)
            def _():
                small_step(level)

        for step in (1, 2):

            @pl.when(tick == 7 * step)
            def _():
                relay.step(step)

    relay.finish()


def backward_pass(
    seqs, chans, held, ffn_g, in_full, out_full, streams, block_own, tokens, residual, second_grad,
    cotangent, keeps, gains, taps,
):
    dma, vmem, shape = pltpu.SemaphoreType.DMA, pltpu.VMEM, jax.ShapeDtypeStruct
    parts, half_seqs = PIECES // seqs, seqs // 2
    levels = seqs.bit_length() - 2
    chunks = chans * parts
    slots = min(chunks, LAG * (levels + chans) + 1)
    group = min(4, half_seqs)
    sizes = [group] + [half_seqs >> level if group == half_seqs else 1 for level in range(1, levels + 1)]
    partners = (seqs * chans).bit_length() - 1
    rows, width = tokens.shape
    own_count = rows - held * HEAD
    part = out_full.shape[-1]
    outs = [
        shape((parts, PIECE, D), BF16),
        shape((8, width), F32),
        shape((own_count, width), BF16),
        shape((parts, half_seqs, 2, PIECE, D), BF16),
        shape((chans,) + block_own.shape, BF16),
        shape((chunks, half_seqs, PIECE, D), BF16),
    ]
    outs += [
        shape((chunks, half_seqs >> (level + 1), PIECE, D), BF16) for level in range(levels)
    ]
    outs.append(shape((2, chunks, PIECE, D), BF16))
    return call(
        functools.partial(backward_kernel, seqs, chans, held),
        outs,
        [pl.ANY] * 5 + [vmem] * 7,
        [vmem] * 3 + [pl.ANY] * (len(outs) - 3),
        [
            *[vmem((size, PIECE, D), BF16) for size in sizes],
            vmem((slots, half_seqs, PIECE, D), BF16),
            vmem((2, PIECE, D), BF16),
            vmem((partners, 8, width), F32),
            vmem((partners, 8, width), F32),
            vmem((8, width), F32),
            vmem((rows, width), BF16),
            vmem((own_count, width), BF16),
            vmem((own_count, width), BF16),
            vmem((own_count, width), F32),
            vmem((own_count, 3 * part), BF16),
            vmem((own_count, part), BF16),
            vmem((rows, part), F32),
            vmem((own_count, width), F32),
            vmem((rows, 3 * part), F32),
            vmem(in_full.shape[1:], BF16),
            vmem(out_full.shape[1:], BF16),
            vmem((4, 2, PIECE, D), BF16),
            dma((chunks,)),
            dma(()),
            dma((levels + 1,)),
            dma((chunks,)),
            dma((chunks,)),
            dma((chunks, 2, half_seqs)),
            dma((chunks, 2, half_seqs)),
            dma((chunks,)),
            dma((2, chunks)),
            dma((partners,)),
            dma((partners,)),
            dma((3,)),
            dma(()),
            *Relay.semaphores(chans),
        ],
        1,
        ffn_g.reshape(3, parts, half_seqs, 2, PIECE, D),
        in_full, out_full, streams, block_own, tokens, residual, second_grad, cotangent, keeps, gains,
        taps,
        vmem=62,
    )[:5]


def shifted(value, axes, by):
    length = lax.axis_size(axes)
    pairs = [(i, i + by) for i in range(length) if 0 <= i + by < length]
    return lax.ppermute(value, axes, pairs)


def adam_update(param, gradient, first, second):
    first_new = FIRST_DECAY * first + (1.0 - FIRST_DECAY) * gradient
    second_new = SECOND_DECAY * second + (1.0 - SECOND_DECAY) * gradient * gradient
    first_fix = 1.0 - FIRST_DECAY**STEP
    second_fix = 1.0 - SECOND_DECAY**STEP
    param_new = param - ADAM_RATE * (first_new / first_fix) / (
        jnp.sqrt(second_new / second_fix) + ADAM_EPS
    )
    return (param_new, first_new, second_new)


COLUMNS = [3 * D, D, FF, FF, FF]
RATES = [1.0, 1.0, 1.0, 1.0, 0.5]


def last_kernel(block_low, input_low, grad_home, ortho_home, *refs):
    weights, moments, (block_out, input_grad) = refs[:5], refs[5:10], refs[10:12]
    moments_new, weights_new = refs[12:22:2], refs[13:22:2]
    step = pl.program_id(0)
    for low, whole in ((block_low, block_out), (input_low, input_grad)):
        rows = low.shape[2]
        for at in range(low.shape[0]):
            whole[0, at * rows : (at + 1) * rows] = low[at, 0].astype(F32)

    def update(index, at, lanes, grad, ortho):
        rate = RATES[index]
        here = at + (slice(None), lanes)
        moments_new[index][here] = MOMENTUM_DECAY * moments[index][here] + grad.astype(F32).T
        weights_new[index][here] = (
            weights[index][here] * (1.0 - WEIGHT_DECAY * rate)
            - rate * math.sqrt(COLUMNS[index] / D) * ortho.astype(F32).T
        )

    for m in range(3):

        @pl.when(step == m)
        def _():
            for t in range(TILES):
                rows = slice(t * UNIT, (t + 1) * UNIT)
                update(
                    m + 2, (), slice(t * LANES, (t + 1) * LANES),
                    *(home[m, :, rows].reshape(LANES, -1) for home in (grad_home, ortho_home)),
                )

    @pl.when(step == 3)
    def _():
        for q in range(PER_CHAN):
            lanes = slice(q % 2 * SMALL_PIECE, (q % 2 + 1) * SMALL_PIECE)
            blocks = [home[3, q, 0:SMALL_PIECE] for home in (grad_home, ortho_home)]
            update(*((0, (q // 2,)) if q < IN_PIECES else (1, ())), lanes, *blocks)


def last_pass(block_low, input_low, homes, weights, moments):
    chans, held, sub, width = block_low.shape
    low = pl.BlockSpec((chans, 1, sub, width), lambda s: (0, s, 0, 0))
    whole = pl.BlockSpec((1, chans * sub, width), lambda s: (s, 0, 0))

    def all_of(array):
        return pl.BlockSpec(array.shape, lambda s: (0,) * array.ndim)

    shape = jax.ShapeDtypeStruct
    outs = [shape((held, chans * sub, width), F32)] * 2
    out_specs = [whole] * 2
    for weight in weights:
        outs += [shape(weight.shape, F32)] * 2
        out_specs += [all_of(weight)] * 2
    return pl.pallas_call(
        last_kernel,
        grid=(held,),
        out_shape=outs,
        in_specs=[low] * 2 + [all_of(one) for one in (*homes, *weights, *moments)],
        out_specs=out_specs,
        compiler_params=pltpu.CompilerParams(vmem_limit_bytes=60 * 1024 * 1024),
    )(block_low, input_low, *homes, *weights, *moments)


def on_device(
    tokens,
    segment_ids,
    cotangent,
    norm_gains,
    filter_weight,
    in_weight,
    out_weight,
    gate_weight,
    up_weight,
    down_weight,
    norm_gains_mean,
    norm_gains_square,
    filter_mean,
    filter_square,
    in_momentum,
    out_momentum,
    gate_momentum,
    up_momentum,
    down_momentum,
):
    seqs, chans = lax.axis_size("seq"), lax.axis_size("chan")
    r, c = lax.axis_index("seq"), lax.axis_index("chan")
    seq_total, local_rows, width = tokens.shape
    sub = local_rows // chans
    chan_width = filter_weight.shape[1]

    weights = [in_weight.transpose(1, 0, 2), out_weight, gate_weight, up_weight, down_weight]
    moments = [
        in_momentum.transpose(1, 0, 2), out_momentum, gate_momentum, up_momentum, down_momentum
    ]

    def share(array, start, length):
        return lax.dynamic_slice_in_dim(array, start, length, axis=1)

    positions = r * local_rows + jnp.arange(local_rows, dtype=jnp.int32)
    local_keeps = jnp.stack(
        [(segment_ids <= positions[None, :] - offset).astype(F32) for offset in (1, 2)], axis=-1
    )
    following = jnp.where(
        c == chans - 1,
        shifted(local_keeps[:, :2], "seq", -1),
        share(local_keeps, lax.rem(c + 1, chans) * sub, 2),
    )
    following = jnp.concatenate([following[-1:], following[:-1]])
    gap = jnp.zeros((seq_total, HEAD - 2, 2), F32)
    keeps = jnp.concatenate([following, gap, share(local_keeps, c * sub, sub)], axis=1).reshape(-1, 2)

    (
        in_full, out_full, _, taps, moments_held, _, streams, ffn_grads,
        token_rows, upstream_rows, residual, second_grad, block_out,
    ) = forward_pass(
        seqs, chans, weights, moments, filter_weight, tokens, cotangent, keeps, norm_gains
    )
    moments_held = moments_held.transpose(0, 2, 1, 3).reshape(-1, D)
    grads_held, small, input_grad, _, block_out = backward_pass(
        seqs, chans, seq_total, ffn_grads, in_full, out_full, streams, block_out, token_rows, residual,
        second_grad, upstream_rows, keeps, norm_gains, taps,
    )

    gains_new, gains_mean_new, gains_square_new = adam_update(
        norm_gains, small[:2], norm_gains_mean, norm_gains_square
    )
    filter_new, filter_mean_new, filter_square_new = adam_update(
        filter_weight, share(small[2:5], c * chan_width, chan_width), filter_mean, filter_square
    )

    *homes, input_grad = orthogonalize(
        seqs, chans, grads_held.reshape(-1, D), moments_held, input_grad
    )
    block_out, input_grad = (
        one.reshape(chans, seq_total, sub, width) for one in (block_out, input_grad)
    )
    block_out, input_grad, *results = last_pass(block_out, input_grad, homes, weights, moments)
    results[:2] = [one.transpose(1, 0, 2) for one in results[:2]]
    return (
        block_out,
        input_grad,
        gains_new,
        gains_mean_new,
        gains_square_new,
        filter_new,
        filter_mean_new,
        filter_square_new,
        *results,
    )


def solution(mesh):
    return jax.shard_map(
        on_device,
        mesh=mesh,
        in_specs=(
            P(None, "seq", None),
            P(None, "seq"),
            P(None, "seq", None),
            P(),
            P(None, "chan"),
            P("seq", None, "chan"),
            P("seq", "chan"),
            P("seq", "chan"),
            P("seq", "chan"),
            P("seq", "chan"),
            P(),
            P(),
            P(None, "chan"),
            P(None, "chan"),
            P("seq", None, "chan"),
            P("seq", "chan"),
            P("seq", "chan"),
            P("seq", "chan"),
            P("seq", "chan"),
        ),
        out_specs=(
            P(None, "seq", None),
            P(None, "seq", None),
            P(),
            P(),
            P(),
            P(None, "chan"),
            P(None, "chan"),
            P(None, "chan"),
            P("seq", None, "chan"),
            P("seq", None, "chan"),
            P("seq", "chan"),
            P("seq", "chan"),
            P("seq", "chan"),
            P("seq", "chan"),
            P("seq", "chan"),
            P("seq", "chan"),
            P("seq", "chan"),
            P("seq", "chan"),
        ),
        check_vma=False,
    )
```

```python
import functools
import math

import jax
import jax.numpy as jnp
from jax import lax
from jax.experimental import pallas as pl
from jax.experimental.pallas import tpu as pltpu
from jax.sharding import PartitionSpec as P

D = 1024
FF = 4608
NS_ITERS = 4
STEP = 10


NORM_EPS = 1e-05
QUINTIC_FIRST = 3.4445
QUINTIC_SECOND = -4.775
QUINTIC_THIRD = 2.0315
MOMENTUM_DECAY = 0.95
FIRST_DECAY = 0.9
SECOND_DECAY = 0.999
ADAM_EPS = 1e-08
ADAM_RATE = 0.4
WEIGHT_DECAY = 0.01
ORTHO_EPS = 1e-07

MESH = pl.DeviceIdType.MESH
BF16 = jnp.bfloat16
F32 = jnp.float32

PIECES = 32
PER_CHAN = 8
PIECE = FF // PIECES
LANES = 128
TILES = FF // 4 // LANES
UNIT = LANES // PER_CHAN
SMALL_PIECE = 4 * D // PIECES
IN_PIECES = 6


def remote(src, dst, send, recv, **place):
    return pltpu.make_async_remote_copy(
        src_ref=src, dst_ref=dst, send_sem=send, recv_sem=recv, device_id=place, device_id_type=MESH
    )


def flip(index, bit):
    step = 1 << bit
    return index + step * (1 - 2 * lax.rem(lax.div(index, step), 2))


def flips(index, bits):
    found = [index]
    for bit in bits:
        found = found + [flip(one, bit) for one in found]
    return found


def greet(places):
    barrier = pltpu.get_barrier_semaphore()
    for place in places:
        pl.semaphore_signal(barrier, inc=1, device_id=place, device_id_type=MESH)
    pl.semaphore_wait(barrier, len(places))


def high_bits(bits, half):
    order = list(range(1, bits))
    return order if half == 0 else order[::-1]


def call(kernel, outs, in_spaces, out_spaces, scratch, ident, *args, vmem=48, aliases=None):
    return pl.pallas_call(
        kernel,
        out_shape=outs,
        in_specs=[pl.BlockSpec(memory_space=space) for space in in_spaces],
        out_specs=jax.tree.map(lambda space: pl.BlockSpec(memory_space=space), out_spaces),
        scratch_shapes=scratch,
        input_output_aliases=aliases or {},
        compiler_params=pltpu.CompilerParams(
            collective_id=ident, has_side_effects=True, vmem_limit_bytes=vmem * 1024 * 1024
        ),
    )(*args)


def holder(r, c, seqs):
    at = lax.rem(r + PIECES * seqs - PER_CHAN * c, seqs)
    return at, at < PER_CHAN, lax.div(PER_CHAN * c + at, seqs)


class Homeward:
    def __init__(self, seqs, chans, held, out, between, sems):
        self.seqs, self.chans, self.held, self.out, self.between = seqs, chans, held, out, between
        self.own_sem, self.stay_sem, self.a_send, self.a_recv, self.b_send, self.b_recv = sems
        self.r, self.c = lax.axis_index("seq"), lax.axis_index("chan")
        self.at_out, self.has, self.place = holder(self.r, self.c, seqs)

    def target(self, at):
        return lax.div(self.r + self.seqs * at, PER_CHAN)

    def dropping(self, at):
        return remote(
            self.held.at[at], self.between.at[self.c], self.a_send.at[at], self.a_recv.at[self.c],
            chan=self.target(at),
        )

    def keeping(self, at):
        return pltpu.make_async_copy(self.held.at[at], self.between.at[self.c], self.own_sem.at[0])

    def spreading(self, m, r_to):
        return remote(
            self.between.at[m, r_to], self.out.at[m, self.at_out],
            self.b_send.at[m, r_to], self.b_recv.at[m, self.at_out], seq=r_to,
        )

    def staying(self, m):
        return pltpu.make_async_copy(
            self.between.at[m, self.r], self.out.at[m, self.at_out], self.stay_sem.at[m]
        )

    def drop(self, at):
        @pl.when(self.target(at) != self.c)
        def _():
            self.dropping(at).start()

        @pl.when(self.target(at) == self.c)
        def _():
            self.keeping(at).start()

    def spread(self):
        @pl.when(self.has)
        def _():
            for off in (0, 1, 3, 2):
                m = lax.rem(self.c + off, self.chans)
                if off == 0:
                    self.keeping(0).wait()
                else:
                    remote(
                        self.held.at[0], self.between.at[m], self.a_send.at[0], self.a_recv.at[m], chan=m
                    ).wait_recv()
                for step in range(1, self.seqs):
                    self.spreading(m, lax.rem(self.r + step, self.seqs)).start()
                self.staying(m).start()

    def finish(self):
        @pl.when(self.has)
        def _():
            for m in range(self.chans):
                self.staying(m).wait()

        for piece in range(PER_CHAN):
            r_from = lax.rem(PER_CHAN * self.c + piece, self.seqs)

            @pl.when(r_from != self.r)
            def _():
                for m in range(self.chans):
                    remote(
                        self.between.at[m, self.r], self.out.at[m, piece],
                        self.b_send.at[m, self.r], self.b_recv.at[m, piece], seq=r_from,
                    ).wait_recv()

        for at in range(PIECES // self.seqs):

            @pl.when(self.target(at) != self.c)
            def _():
                self.dropping(at).wait_send()

        @pl.when(self.has)
        def _():
            for m in range(self.chans):
                for step in range(1, self.seqs):
                    self.spreading(m, lax.rem(self.r + step, self.seqs)).wait_send()

    @staticmethod
    def semaphores(seqs, chans):
        dma = pltpu.SemaphoreType.DMA
        return [
            dma((1,)), dma((chans,)), dma((PIECES // seqs,)), dma((chans,)),
            dma((chans, seqs)), dma((chans, PER_CHAN)),
        ]


class Relay:
    def __init__(self, chans, own, blocks, sems):
        self.chans, self.own, self.blocks = chans, own, blocks
        self.own_sem, self.send, self.recv = sems
        self.c = lax.axis_index("chan")

    def keeping(self):
        return pltpu.make_async_copy(self.own, self.blocks.at[self.c], self.own_sem.at[0])

    def copies(self, hop):
        c = self.c
        for side, block, sends in (
            (0, c - hop, (c < self.chans - 1) & (c >= hop)),
            (1, c + hop, (c > 0) & (c + hop < self.chans)),
        ):
            source = self.own if hop == 0 else self.blocks.at[block]
            yield sends, remote(
                source, self.blocks.at[block], self.send.at[side, hop], self.recv.at[side, hop],
                chan=c + 1 - 2 * side,
            )

    def await_hop(self, hop):
        c = self.c
        for side, block, comes in ((0, c - 1 - hop, c > hop), (1, c + 1 + hop, c + 1 + hop < self.chans)):

            @pl.when(comes)
            def _():
                remote(
                    self.blocks.at[block], self.blocks.at[block],
                    self.send.at[side, hop], self.recv.at[side, hop], chan=c - 1 + 2 * side,
                ).wait_recv()

    def step(self, hop, first=False):
        if hop == 0:
            self.keeping().start()
        elif not first:
            self.await_hop(hop - 1)
        for sends, copy in self.copies(hop):

            @pl.when(sends)
            def _():
                copy.start()

    def finish(self, hops):
        self.await_hop(hops[-1])
        if 0 in hops:
            self.keeping().wait()
        for hop in hops:
            for sends, copy in self.copies(hop):

                @pl.when(sends)
                def _():
                    copy.wait_send()

    @staticmethod
    def semaphores(chans):
        dma = pltpu.SemaphoreType.DMA
        return [dma((1,)), dma((2, chans - 1)), dma((2, chans - 1))]


def dot(left, right):
    return jnp.dot(left, right, preferred_element_type=F32)


def contract_last(left, right):
    return lax.dot_general(left, right, (((1,), (1,)), ((), ())), preferred_element_type=F32)


def contract_first(left, right):
    return lax.dot_general(left, right, (((0,), (0,)), ((), ())), preferred_element_type=F32)


def ortho_kernel(
    seqs, chans, grad, moment, _, grad_home, ortho_home, input_blocks,
    out, cut_grad, cut_ortho, between_grad, between_ortho,
    part, own, swapped, paired, parts, sums, gram, poly, half_way,
    x_send, x_recv, s_send, s_recv, g_send, g_recv, f_send, f_recv, *home_sems
):
    r, c = lax.axis_index("seq"), lax.axis_index("chan")
    core, h = lax.rem(r, 2), lax.div(r, 2)
    other = flip(r, 0)
    count, half, block = seqs // 2, D // 2, D // seqs
    tile = min(256, half)
    peers = [lax.rem(h + off, count) for off in range(1, count)]
    greet(
        [{"seq": lax.rem(r + off, seqs)} for off in range(1, seqs)]
        + [{"chan": lax.rem(c + off, chans)} for off in range(1, chans)]
    )
    home_grad = Homeward(seqs, chans, cut_grad, grad_home, between_grad, home_sems[:6])
    home_ortho = Homeward(seqs, chans, cut_ortho, ortho_home, between_ortho, home_sems[6:12])
    relay = Relay(chans, None, input_blocks, home_sems[12:])
    columns = out.shape[0]
    slab = PIECE

    @pl.loop(0, columns // slab)
    def _(at):
        here = pl.ds(pl.multiple_of(at * slab, slab), slab)
        out[here] = (MOMENTUM_DECAY * moment[here].astype(F32) + grad[here].astype(F32)).astype(BF16)
        for to in range(seqs):
            cut_grad[at, to] = grad[here, to * block : (to + 1) * block]

    for at in range(columns // slab):
        home_grad.drop(at)
    relay.step(1, first=True)

    apart = c == chans - 1

    def kind(pair):
        return jnp.where(lax.rem(pair, 4) == 3, 1, 0)

    mine = kind(h)
    own_first = pl.multiple_of(core * half, half)
    other_first = pl.multiple_of((1 - core) * half, half)

    def block_at(pair, which):
        return pl.ds(pl.multiple_of(which * half + pair * block, block), block)

    def exchange():
        return remote(part, swapped, x_send, x_recv, seq=other)

    def scatter(peer):
        return remote(
            paired.at[peer], parts.at[h], s_send.at[peer], s_recv.at[h], seq=2 * peer + core
        )

    def scatter_in(peer):
        return remote(
            paired.at[peer], parts.at[peer], s_send.at[peer], s_recv.at[peer], seq=2 * peer + core
        )

    def share(peer):
        return remote(
            sums.at[kind(peer)], gram.at[block_at(h, core)], g_send.at[peer], g_recv.at[h],
            seq=2 * peer + core,
        )

    def share_in(peer):
        return remote(
            sums.at[0], gram.at[block_at(peer, core)], g_send.at[peer], g_recv.at[peer],
            seq=2 * peer + core,
        )

    def forward(pair):
        return remote(
            gram.at[block_at(pair, core)], gram.at[block_at(pair, core)],
            f_send.at[pair], f_recv.at[pair], seq=other,
        )

    def forward_in(pair):
        return remote(
            gram.at[block_at(pair, 1 - core)], gram.at[block_at(pair, 1 - core)],
            f_send.at[pair], f_recv.at[pair], seq=other,
        )

    for turn in range(NS_ITERS // 2):

        @pl.loop(0, half // tile)
        def _(at):
            here = pl.ds(pl.multiple_of(at * tile, tile), tile)
            there = pl.ds(pl.multiple_of(other_first + at * tile, tile), tile)
            part[here] = contract_first(out[:, there], out[...]).astype(BF16)

        exchange().start()

        @pl.loop(0, half // tile)
        def _(at):
            here = pl.ds(pl.multiple_of(at * tile, tile), tile)
            there = pl.ds(pl.multiple_of(own_first + at * tile, tile), tile)
            own[here] = contract_first(out[:, there], out[...])

        exchange().wait()

        @pl.loop(0, count)
        def _(at):
            here = pl.ds(pl.multiple_of(at * block, block), block)
            paired[at] = (own[here] + swapped[here].astype(F32)).astype(BF16)

        for peer in peers:
            scatter(peer).start()
        parts[h] = paired[h]
        for peer in peers:
            scatter_in(peer).wait_recv()
        groups = [jnp.zeros((block, D), F32), jnp.zeros((block, D), F32)]
        for pair in range(count):
            groups[int(pair % 4 == 3)] += parts[pair].astype(F32)
        both = groups[0] + groups[1]
        sums[0] = jnp.where(apart, groups[0], both).astype(BF16)
        sums[1] = jnp.where(apart, groups[1], both).astype(BF16)
        for peer in peers:
            share(peer).start()
        gram[block_at(h, core)] = sums[mine]
        forward(h).start()
        for peer in peers:
            share_in(peer).wait_recv()
            forward(peer).start()
        for pair in [h] + peers:
            forward_in(pair).wait_recv()
        for peer in peers:
            scatter(peer).wait_send()
            share(peer).wait_send()
        for pair in [h] + peers:
            forward(pair).wait_send()

        scale = jnp.ones((1, 1), F32)
        if turn == 0:
            trace = jnp.zeros((1, 1), F32)
            for at in range(D // 128):
                square = gram[at * 128 : (at + 1) * 128, at * 128 : (at + 1) * 128].astype(F32)
                row = lax.broadcasted_iota(jnp.int32, square.shape, 0)
                column = lax.broadcasted_iota(jnp.int32, square.shape, 1)
                trace += jnp.sum(jnp.where(row == column, square, 0.0), keepdims=True)
            scale = 1.0 / (jnp.sqrt(trace) + ORTHO_EPS)

            @pl.loop(0, D // tile)
            def _(at):
                here = pl.ds(pl.multiple_of(at * tile, tile), tile)
                gram[here] = (gram[here].astype(F32) * scale * scale).astype(BF16)

        def each_tile(work):
            @pl.loop(0, D // tile)
            def _(at):
                work(pl.ds(pl.multiple_of(at * tile, tile), tile))

        def polynomial(values, whole):
            return (
                QUINTIC_SECOND * values.astype(F32) + QUINTIC_THIRD * dot(values, whole[...])
            ).astype(BF16)

        def first_poly(here):
            poly[here] = polynomial(gram[here], gram)

        def halfway(here):
            half_way[here] = (
                QUINTIC_FIRST * gram[here].astype(F32) + dot(poly[here], gram[...])
            ).astype(BF16)

        def next_gram(here):
            gram[here] = (
                QUINTIC_FIRST * half_way[here].astype(F32) + dot(half_way[here], poly[...])
            ).astype(BF16)

        def second_poly(here):
            half_way[here] = polynomial(gram[here], gram)

        for work in (first_poly, halfway, next_gram, second_poly):
            each_tile(work)

        @pl.loop(0, columns // slab)
        def _(at):
            here = pl.ds(pl.multiple_of(at * slab, slab), slab)
            new = QUINTIC_FIRST * out[here].astype(F32) + dot(out[here], poly[...])
            if turn == 0:
                new = new * scale
            new = QUINTIC_FIRST * new + dot(new.astype(BF16), half_way[...])
            if turn < NS_ITERS // 2 - 1:
                out[here] = new.astype(BF16)
            else:
                for to in range(seqs):
                    cut_ortho[at, to] = new[:, to * block : (to + 1) * block].astype(BF16)
                home_ortho.drop(at)

        if turn == 0:
            home_grad.spread()
            relay.step(2)

    home_ortho.spread()
    home_grad.finish()
    relay.finish(range(1, chans - 1))
    home_ortho.finish()


def orthogonalize(seqs, chans, grad, moment, input_blocks):
    dma = pltpu.SemaphoreType.DMA
    count, block, held = seqs // 2, D // seqs, PIECES // seqs
    return call(
        functools.partial(ortho_kernel, seqs, chans),
        [jax.ShapeDtypeStruct((chans, PER_CHAN, PIECE, block), BF16)] * 2
        + [jax.ShapeDtypeStruct(input_blocks.shape, BF16)],
        [pltpu.VMEM] * 2 + [pl.ANY],
        [pl.ANY] * 3,
        [
            pltpu.VMEM(grad.shape, BF16),
            pltpu.VMEM((held, seqs, PIECE, block), BF16),
            pltpu.VMEM((held, seqs, PIECE, block), BF16),
            pltpu.VMEM((chans, seqs, PIECE, block), BF16),
            pltpu.VMEM((chans, seqs, PIECE, block), BF16),
            pltpu.VMEM((D // 2, D), BF16),
            pltpu.VMEM((D // 2, D), F32),
            pltpu.VMEM((D // 2, D), BF16),
            pltpu.VMEM((count, block, D), BF16),
            pltpu.VMEM((count, block, D), BF16),
            pltpu.VMEM((2, block, D), BF16),
            pltpu.VMEM((D, D), BF16),
            pltpu.VMEM((D, D), BF16),
            pltpu.VMEM((D, D), BF16),
            dma(()),
            dma(()),
        ]
        + [dma((count,))] * 6
        + Homeward.semaphores(seqs, chans) * 2
        + Relay.semaphores(chans),
        2,
        grad,
        moment,
        input_blocks,
        aliases={2: 2},
    )


HEAD = 8


def own_rows(values, seqs_held):
    length = values.shape[0] // seqs_held
    return [values[s * length + HEAD : (s + 1) * length] for s in range(seqs_held)]


def row_scale(values):
    return lax.rsqrt(jnp.mean(values * values, axis=1, keepdims=True) + NORM_EPS)


def filtering(gated, taps, keep_one, keep_two):
    back_one, back_two = pltpu.roll(gated, 1, 0), pltpu.roll(gated, 2, 0)
    return taps[2:3] * gated + taps[1:2] * keep_one * back_one + taps[0:1] * keep_two * back_two


def forward_kernel(seqs, chans, held, *refs):
    forward_work(seqs, chans, held, refs[:5], refs[5:10], *refs[10:])


def forward_work(
    seqs, chans, held,
    weights, moments, own_taps, token_source, cotangent_source, keeps, gains,
    io_full, ffn_full, taps_all, held_out, between, streams, ffn_g,
    tokens, cotangent, residual, second_grad, block_out,
    io_shard, ffn_shard, taps, packed, shelf, shelf_sem,
    io_own, p_send, p_recv, q_send, q_recv, line_send, line_recv,
    u, u_own, halo, row_sem, halo_sem, halo_send, halo_recv, normed, mixed, stream, x, x_own, ffn_out, act, gate_low, up_low, io_v, taps_v, w_v, grad_v,
    own_sem, z_send, z_recv, b_send, b_recv, c_send, c_recv,
    t_own, t_send, t_recv, p_own, ps_send, ps_recv, pl_send, pl_recv,
    mix_sem, taps_sem, stream_sem, load_sem, grad_sem,
):
    bits = seqs.bit_length() - 1
    r, c = lax.axis_index("seq"), lax.axis_index("chan")
    last = TILES - 1
    pair, mine = lax.div(r, 2), lax.rem(r, 2)
    greet(
        [{"chan": lax.rem(c + off, chans)} for off in range(1, chans)]
        + [{"seq": lax.rem(r + off, seqs)} for off in range(1, seqs)]
    )

    def shard(k):
        return ffn_shard.at[k]

    def full(k, part, block):
        return ffn_full.at[k, part, block]

    def own(k):
        return pltpu.make_async_copy(shard(k), full(k, c, r), own_sem.at[k])

    def along_chan(k, off, incoming):
        source = lax.rem(c + chans - off, chans) if incoming else c
        return remote(
            shard(k), full(k, source, r), z_send.at[k, off - 1], z_recv.at[k, off - 1],
            chan=lax.rem(c + off, chans),
        )

    def across(k, half, step, incoming):
        order = high_bits(bits, half)
        bit, done = order[step], order[:step]
        base = flip(r, bit) if incoming else r
        part = pl.ds(half * (chans // 2), chans // 2)
        first = (1 << step) - 1
        return [
            remote(
                full(k, part, block), full(k, part, block),
                b_send.at[k, half, first + at], b_recv.at[k, half, first + at], seq=flip(r, bit),
            )
            for at, block in enumerate(flips(base, done))
        ]

    def core(k, incoming):
        base = flip(r, 0) if incoming else r
        return [
            remote(
                full(k, slice(None), block), full(k, slice(None), block),
                c_send.at[k, at], c_recv.at[k, at], seq=flip(r, 0),
            )
            for at, block in enumerate(flips(base, range(1, bits)))
        ]

    def start_chan(k):
        own(k).start()
        for off in (2, 1, 3):
            along_chan(k, off, False).start()

    def first_level(k):
        own(k).wait()
        for off in range(1, chans):
            along_chan(k, off, True).wait_recv()
        for half in range(2):
            for copy in across(k, half, 0, False):
                copy.start()

    def next_level(k, level):
        for half in range(2):
            for copy in across(k, half, level - 1, True):
                copy.wait_recv()
            for copy in across(k, half, level, False):
                copy.start()

    def to_core(k):
        for half in range(2):
            for copy in across(k, half, bits - 2, True):
                copy.wait_recv()
        for copy in core(k, False):
            copy.start()

    def arrived(k):
        for copy in core(k, True):
            copy.wait_recv()

    def sent(k):
        for off in range(1, chans):
            along_chan(k, off, False).wait_send()
        for half in range(2):
            for step in range(bits - 1):
                for copy in across(k, half, step, False):
                    copy.wait_send()
        for copy in core(k, False):
            copy.wait_send()

    def taps_copy(off, incoming):
        source = lax.rem(c + chans - off, chans) if incoming else c
        return remote(
            taps, taps_all.at[source], t_send.at[off - 1], t_recv.at[off - 1],
            chan=lax.rem(c + off, chans),
        )

    _, has, place = holder(r, c, seqs)

    def spread(piece, r_to):
        return remote(
            packed.at[:, piece], between.at[:, r], ps_send.at[piece], ps_recv.at[r], seq=r_to
        )

    def lift(m):
        return remote(between.at[m], held_out.at[place], pl_send.at[m], pl_recv.at[place], chan=m)

    def pieces_start():
        for piece in range(PER_CHAN):
            r_to = lax.rem(PER_CHAN * c + piece, seqs)

            @pl.when(r_to != r)
            def _():
                spread(piece, r_to).start()

            @pl.when(r_to == r)
            def _():
                pltpu.make_async_copy(packed.at[:, piece], between.at[:, r], p_own.at[0]).start()

    def pieces_lift():
        @pl.when(has)
        def _():
            pltpu.make_async_copy(packed.at[:, 0], between.at[:, r], p_own.at[0]).wait()
            for off in range(1, seqs):
                r_from = lax.rem(r + off, seqs)
                remote(
                    packed.at[:, 0], between.at[:, r_from], ps_send.at[0], ps_recv.at[r_from], seq=r_from
                ).wait_recv()
            for m in range(chans):

                @pl.when(m != c)
                def _():
                    lift(m).start()

                @pl.when(m == c)
                def _():
                    copy = pltpu.make_async_copy(between.at[m], held_out.at[place], p_own.at[1])
                    copy.start()
                    copy.wait()

    def pieces_finish():
        for at in range(PIECES // seqs):
            c_from = lax.div(r + seqs * at, PER_CHAN)

            @pl.when(c_from != c)
            def _():
                remote(
                    between.at[0], held_out.at[at], pl_send.at[0], pl_recv.at[at], chan=c_from
                ).wait_recv()

        for piece in range(PER_CHAN):
            r_to = lax.rem(PER_CHAN * c + piece, seqs)

            @pl.when(r_to != r)
            def _():
                spread(piece, r_to).wait_send()

        @pl.when(has)
        def _():
            for m in range(chans):

                @pl.when(m != c)
                def _():
                    lift(m).wait_send()

    rows, width = tokens.shape
    part = io_full.shape[-1] // 4
    tile = rows // 3
    per_tile = held // 3
    size = rows // held - HEAD
    tiles = [pl.ds(at * tile, tile) for at in range(3)]

    io_block = io_shard.shape[0] // 2

    def io_keep():
        return pltpu.make_async_copy(io_shard, io_full.at[c, pair, mine], io_own)

    def io_across(half, level, incoming):
        order = high_bits(bits, half)
        bit, done = order[level], [one - 1 for one in order[:level]]
        base = flip(pair, bit - 1) if incoming else pair
        where = pl.ds(half * io_block, io_block)
        first = (1 << level) - 1
        return [
            remote(
                io_shard.at[where] if level == 0 and not incoming else io_full.at[c, block, mine, where],
                io_full.at[c, block, mine, where],
                p_send.at[half, first + at], p_recv.at[half, first + at], seq=flip(r, bit),
            )
            for at, block in enumerate(flips(base, done))
        ]

    def io_level(level):
        for half in range(2):
            if level > 0:
                for copy in io_across(half, level - 1, True):
                    copy.wait_recv()
            if level < bits - 1:
                for copy in io_across(half, level, False):
                    copy.start()

    def io_core(quarter, core):
        return remote(
            io_full.at[quarter, :, core], io_full.at[quarter, :, core],
            q_send.at[quarter], q_recv.at[quarter], seq=flip(r, 0),
        )

    def io_sides(hop, arriving):
        away = hop + 1 if arriving else hop
        return (
            (0, c - away, (c >= away) & ((c < chans - 1) | arriving)),
            (1, c + away, (c + away < chans) & ((c > 0) | arriving)),
        )

    def io_line(side, quarter, hop):
        return remote(
            io_full.at[quarter, :, mine], io_full.at[quarter, :, mine],
            line_send.at[side, hop], line_recv.at[side, hop], chan=c + 1 - 2 * side,
        )

    def io_line_in(side, quarter, hop):
        return remote(
            io_full.at[quarter, :, mine], io_full.at[quarter, :, mine],
            line_send.at[side, hop], line_recv.at[side, hop], chan=c - 1 + 2 * side,
        )

    def io_start(hop):
        for side, quarter, does in io_sides(hop, False):

            @pl.when(does)
            def _():
                io_line(side, quarter, hop).start()

    def io_arrive(hop):
        for side, quarter, does in io_sides(hop, True):

            @pl.when(does)
            def _():
                io_line_in(side, quarter, hop).wait_recv()
                io_core(quarter, mine).start()

        if hop + 1 < chans - 1:
            io_start(hop + 1)

    def io_sent():
        for half in range(2):
            for level in range(bits - 1):
                for copy in io_across(half, level, False):
                    copy.wait_send()
        for hop in range(chans - 1):
            for side, quarter, does in io_sides(hop, False):

                @pl.when(does)
                def _():
                    io_line(side, quarter, hop).wait_send()

        for quarter in range(chans):
            io_core(quarter, mine).wait_send()

    def reached(hops):
        return jnp.minimum(c, hops) + jnp.minimum(chans - 1 - c, hops) + 1

    def quarter_at(n):
        quarter = jnp.int32(0)
        for place in range(chans):
            order = sorted(range(chans), key=lambda one: (abs(one - place), one))
            for at, one in enumerate(order):
                quarter = quarter + jnp.where((c == place) & (n == at), one, 0)
        return quarter

    def stream_out(j):
        return pltpu.make_async_copy(stream, streams.at[j], stream_sem)

    local_rows = token_source.shape[1]
    before_at = pl.multiple_of(lax.rem(c + chans - 1, chans) * size + size - HEAD, HEAD)
    after_at = pl.multiple_of(lax.rem(c + 1, chans) * size, HEAD)
    halos = [
        (token_source, before_at, c == 0, r > 0, r < seqs - 1, 1),
        (token_source, after_at, c == chans - 1, r < seqs - 1, r > 0, -1),
        (cotangent_source, after_at, c == chans - 1, r < seqs - 1, r > 0, -1),
    ]

    def row_copies():
        return [
            pltpu.make_async_copy(
                source.at[s, pl.ds(pl.multiple_of(c * size, size), size)],
                rows_to.at[pl.ds(s * (size + HEAD) + HEAD, size)],
                row_sem.at[n, s],
            )
            for n, (source, rows_to) in enumerate(
                ((token_source, tokens), (cotangent_source, cotangent))
            )
            for s in range(held)
        ]

    def halo_local(n):
        source, at, _, _, _, _ = halos[n]
        return pltpu.make_async_copy(source.at[:, pl.ds(at, HEAD)], halo.at[n], halo_sem.at[n])

    def halo_remote(n):
        source, at, _, _, _, step = halos[n]
        return remote(
            source.at[:, pl.ds(at, HEAD)], halo.at[n], halo_send.at[n], halo_recv.at[n], seq=r + step
        )

    def rows_start():
        for copy in row_copies():
            copy.start()
        for n, (_, _, edge, takes, gives, _) in enumerate(halos):

            @pl.when(jnp.logical_not(edge))
            def _():
                halo_local(n).start()

            @pl.when(edge & gives)
            def _():
                halo_remote(n).start()

            @pl.when(edge & jnp.logical_not(takes))
            def _():
                halo[n] = jnp.zeros(halo.shape[1:], F32)

    def rows_finish():
        for copy in row_copies():
            copy.wait()
        for n, (_, _, edge, takes, gives, _) in enumerate(halos):

            @pl.when(jnp.logical_not(edge))
            def _():
                halo_local(n).wait()

            @pl.when(edge & takes)
            def _():
                halo_remote(n).wait_recv()

            @pl.when(edge & gives)
            def _():
                halo_remote(n).wait_send()

        row = lax.broadcasted_iota(jnp.int32, (HEAD, width), 0)
        for s in range(held):
            head = pl.ds(s * (size + HEAD), HEAD)
            earlier = (s - 1) % held
            tokens[head] = jnp.where(row < 2, halo[1, earlier], halo[0, s])
            cotangent[head] = jnp.where(row < 2, halo[2, earlier], 0.0)
        for at, here in enumerate(tiles):
            values = cotangent[here]
            u[here] = values.astype(BF16)
            for s, one in enumerate(own_rows(values, per_tile)):
                u_own[pl.ds((at * per_tile + s) * size, size)] = one.astype(BF16)

    def mix_prepare():
        rows_finish()
        for here in tiles:
            values = tokens[here]
            normed[here] = (values * row_scale(values) * gains[0:1]).astype(BF16)
            residual[here] = values

    def mix_some(hops):
        first = 0 if hops == 0 else reached(hops - 1)

        @pl.loop(first, reached(hops))
        def _(n):
            j = quarter_at(n)
            io_core(j, 1 - mine).wait_recv()
            load = pltpu.make_async_copy(io_full.at[j], io_v, mix_sem)
            load.start()

            @pl.when(n > 0)
            def _():
                stream_out(j).wait()

            load.wait()
            in_w = io_v[:, :, :, 0 : 3 * part].reshape(width, 3 * part)
            out_w = io_v[:, :, :, 3 * part :].reshape(width, part)
            for here in tiles:
                stream[here] = dot(normed[here], in_w)
            filters = taps_v[j]
            gated = stream[:, 0:part] * stream[:, 2 * part :]
            filtered = filtering(gated, filters, keeps[:, 0:1], keeps[:, 1:2])
            mixed[...] = (stream[:, part : 2 * part] * filtered).astype(BF16)
            stream_out(j).start()
            for here in tiles:
                residual[here] += contract_last(mixed[here], out_w)

    def mix_finish():
        for at, here in enumerate(tiles):
            values = residual[here]
            new = values * row_scale(values) * gains[1:2]
            x[here] = new.astype(BF16)
            for s, one in enumerate(own_rows(new, per_tile)):
                x_own[pl.ds((at * per_tile + s) * size, size)] = one.astype(BF16)
            ffn_out[here] = jnp.zeros((tile, width), F32)
            second_grad[here] = jnp.zeros((tile, width), F32)
        stream_out(c).wait()

    def loads(t):
        slot = lax.rem(t, 2)
        return [
            pltpu.make_async_copy(
                ffn_full.at[t, j, :, m],
                w_v.at[slot, m, :, :, pl.ds(j * LANES, LANES)],
                load_sem.at[slot, m, j],
            )
            for m in range(3)
            for j in range(chans)
        ]

    def grads_out(t):
        slot = lax.rem(t, 2)
        return [
            pltpu.make_async_copy(grad_v.at[slot, m], ffn_g.at[m, :, t], grad_sem.at[slot, m])
            for m in range(3)
        ]

    def feed_forward(t, arrived_last):
        slot = lax.rem(t, 2)

        @pl.when(t + 1 <= arrived_last)
        def _():
            for copy in loads(t + 1):
                copy.start()

        for copy in loads(t):
            copy.wait()

        @pl.when(t >= 2)
        def _():
            for copy in grads_out(t - 2):
                copy.wait()

        wg, wu, wd = (w_v[slot, m].reshape(width, chans * LANES) for m in range(3))
        for at, here in enumerate(tiles):
            gate = dot(x[here], wg)
            up = dot(x[here], wu)
            grad = dot(u[here], wd)
            sigmoid = jax.nn.sigmoid(gate)
            silu = gate * sigmoid
            new_act = silu * up
            new_gate = grad * up * sigmoid * (1.0 + gate * (1.0 - sigmoid))
            new_up = grad * silu
            for ref, values in ((act, new_act), (gate_low, new_gate), (up_low, new_up)):
                for s, one in enumerate(own_rows(values, per_tile)):
                    ref[pl.ds((at * per_tile + s) * size, size)] = one.astype(BF16)
            ffn_out[here] += contract_last(new_act.astype(BF16), wd)
            second_grad[here] += contract_last(new_gate.astype(BF16), wg) + contract_last(
                new_up.astype(BF16), wu
            )
        for m, (low, right) in enumerate(((gate_low, x_own), (up_low, x_own), (act, u_own))):
            grad_v[slot, m] = (
                contract_first(low[...], right[...]).astype(BF16).reshape(PIECES, UNIT, width)
            )
        for copy in grads_out(t):
            copy.start()

    def shelf_copies(group, n):
        slot = n % 2
        if n % 4 == 0:
            part_of = [(group[0].at[k], k) for k in range(3)] + [(group[1], 3)]
            return [
                pltpu.make_async_copy(
                    source, shelf.at[slot, :, pl.ds(k * part, part)], shelf_sem.at[slot, k]
                )
                for source, k in part_of
            ]
        return [pltpu.make_async_copy(group[n % 4 + 1], shelf.at[slot], shelf_sem.at[slot, 0])]

    def shelves(n):
        return shelf_copies(weights if n < 4 else moments, n)

    def shelve(n):
        if n < 7:
            for copy in shelves(n + 1):
                copy.start()
        for copy in shelves(n):
            copy.wait()
        slot, m = n % 2, n % 4 - 1
        if n == 0:
            io_shard[...] = shelf[slot, :, : 4 * part].astype(BF16)
        elif n < 4:
            for t in range(TILES):
                ffn_shard[t, m] = shelf[slot, :, t * LANES : (t + 1) * LANES].astype(BF16)
        elif n == 4:
            packed[3] = jnp.zeros(packed.shape[1:], BF16)
            for q in range(PER_CHAN):
                block = shelf[slot, :, q * SMALL_PIECE : (q + 1) * SMALL_PIECE]
                packed[3, q, 0:SMALL_PIECE] = block.T.astype(BF16)
        else:
            for t in range(TILES):
                block = shelf[slot, :, t * LANES : (t + 1) * LANES].T.astype(BF16)
                packed[m, :, t * UNIT : (t + 1) * UNIT] = block.reshape(PER_CHAN, UNIT, -1)

    for copy in shelves(0):
        copy.start()
    taps[...] = jnp.zeros_like(taps)
    taps[0:3] = own_taps[...]
    shelve(0)
    io_keep().start()
    io_level(0)
    rows_start()
    taps_own = pltpu.make_async_copy(taps, taps_all.at[c], t_own)
    taps_own.start()
    for off in range(1, chans):
        taps_copy(off, False).start()
    for n in (1, 2, 3):
        shelve(n)
    start_chan(0)
    io_keep().wait()
    for level in range(1, bits):
        io_level(level)
    io_start(0)
    io_core(c, mine).start()
    start_chan(1)
    for n in (4, 5, 6, 7):
        shelve(n)
    pieces_start()
    mix_prepare()
    taps_own.wait()
    for off in range(1, chans):
        taps_copy(off, True).wait_recv()
    copy = pltpu.make_async_copy(taps_all, taps_v, taps_sem)
    copy.start()
    copy.wait()
    mix_some(0)

    settled = 2 * (chans - 1)
    for tick in range(settled):
        start_chan(tick + 2)
        first_level(tick)
        for level in range(1, bits - 1):
            if tick >= level:
                next_level(tick - level, level)
        if tick >= bits - 1:
            to_core(tick - bits + 1)
        if tick >= bits:
            arrived(tick - bits)
        if tick == 1:
            pieces_lift()
        if tick % 2 == 0:
            io_arrive(tick // 2)
        else:
            mix_some(tick // 2 + 1)
    mix_finish()

    def done_by(tick):
        some = jnp.minimum(2 * (tick - settled + 1), tick - bits + 1)
        return jnp.minimum(jnp.maximum(some, 0), TILES)

    @pl.loop(settled, TILES + bits)
    def _(tick):
        @pl.when(tick + 2 <= last)
        def _():
            start_chan(tick + 2)

        @pl.when(tick <= last)
        def _():
            first_level(tick)

        for level in range(1, bits - 1):

            @pl.when(tick - level <= last)
            def _():
                next_level(tick - level, level)

        @pl.when(tick - bits + 1 <= last)
        def _():
            to_core(tick - bits + 1)

        arrived(tick - bits)
        first = done_by(tick - 1)

        @pl.when((tick == settled) | (first >= tick - bits))
        def _():
            for copy in loads(first):
                copy.start()

        @pl.loop(first, done_by(tick))
        def _(t):
            feed_forward(t, tick - bits)

    for s in range(held):
        here = pl.ds(s * (size + HEAD) + HEAD, size)
        block_out[pl.ds(s * size, size)] = (residual[here] + ffn_out[here]).astype(BF16)
    for t in (TILES - 2, TILES - 1):
        for copy in grads_out(t):
            copy.wait()
    pieces_finish()
    for off in range(1, chans):
        taps_copy(off, False).wait_send()
    io_sent()

    @pl.loop(0, last + 1)
    def _(k):
        sent(k)


def forward_pass(seqs, chans, weights, moments, taps, tokens, cotangent, keeps, gains):
    held, local_rows, width = tokens.shape
    block, part = weights[1].shape
    own_count, hidden = held * local_rows // chans, chans * LANES
    rows = own_count + held * HEAD
    tail = (PIECE, block)
    shape = jax.ShapeDtypeStruct
    outs = [
        shape((chans, seqs // 2, 2, block, 4 * part), BF16),
        shape((TILES, chans, seqs, 3, block, LANES), BF16),
        shape((chans, 8, part), F32),
        shape((PIECES // seqs, seqs) + tail, BF16),
        shape((chans, seqs) + tail, BF16),
        shape((chans, rows, 3 * part), F32),
    ]
    outs.append(shape((3, PIECES, TILES, UNIT, width), BF16))
    outs += [shape((rows, width), F32)] * 4 + [shape((own_count, width), BF16)]
    dma = pltpu.SemaphoreType.DMA
    count = TILES
    vmem = pltpu.VMEM
    found = call(
        functools.partial(forward_kernel, seqs, chans, held),
        outs,
        [pl.ANY] * 10 + [vmem] + [pl.ANY] * 2 + [vmem] * 2,
        [pl.ANY] * 7 + [vmem] * 5,
        [
            vmem((block, 4 * part), BF16),
            vmem((TILES, 3, block, LANES), BF16),
            vmem((8, part), F32),
            vmem((chans, PER_CHAN) + tail, BF16),
            vmem((2, block, TILES * LANES), F32),
            dma((2, 4)),
            dma(()),
            dma((2, seqs // 2 - 1)),
            dma((2, seqs // 2 - 1)),
            dma((chans,)),
            dma((chans,)),
            dma((2, chans - 1)),
            dma((2, chans - 1)),
            vmem((rows, width), BF16),
            vmem((own_count, width), BF16),
            vmem((3, held, HEAD, width), F32),
            dma((2, held)),
            dma((3,)),
            dma((3,)),
            dma((3,)),
            vmem((rows, width), BF16),
            vmem((rows, part), BF16),
            vmem((rows, 3 * part), F32),
            vmem((rows, width), BF16),
            vmem((own_count, width), BF16),
            vmem((rows, width), F32),
            vmem((own_count, hidden), BF16),
            vmem((own_count, hidden), BF16),
            vmem((own_count, hidden), BF16),
            vmem((seqs // 2, 2, block, 4 * part), BF16),
            vmem((chans, 8, part), F32),
            vmem((2, 3, seqs, block, hidden), BF16),
            vmem((2, 3, PIECES, UNIT, width), BF16),
            dma((count,)),
            dma((count, chans - 1)),
            dma((count, chans - 1)),
            dma((count, 2, seqs // 2 - 1)),
            dma((count, 2, seqs // 2 - 1)),
            dma((count, seqs // 2)),
            dma((count, seqs // 2)),
            dma(()),
            dma((chans - 1,)),
            dma((chans - 1,)),
            dma((2,)),
            dma((PER_CHAN,)),
            dma((seqs,)),
            dma((chans,)),
            dma((PIECES // seqs,)),
            dma(()),
            dma(()),
            dma(()),
            dma((2, 3, chans)),
            dma((2, 3)),
        ],
        0,
        *weights, *moments, taps, tokens, cotangent, keeps, gains,
        vmem=62,
    )
    return found


LAG = 2


def add_rows(acc, other):
    return (acc.astype(F32) + other.astype(F32)).astype(BF16)


def backward_kernel(
    seqs, chans, held,
    ffn_g, io_full, streams, block_own,
    tokens, residual, second_grad, cotangent, keeps, gains, taps,
    result, total, input_grad, io_g, blocks, input_blocks, *refs
):
    bits = seqs.bit_length() - 1
    levels = bits - 1
    landed, line_land = refs[: levels + 1], refs[levels + 1]
    temps, refs = refs[levels + 2 : 2 * levels + 3], refs[2 * levels + 3 :]
    (
        acc, line_temp, sent, got, sums,
        residual_low, low_own, first_own, residual_grad, stream_own, mixed_own, mixer_grad, first_grad,
        stream, in_v, out_v, staging,
        load_sem, temp_sem, fetch_sem, c_send, c_recv, b_send, b_recv, z_send, z_recv, n_send, n_recv,
        mix_sem, io_sem, *relay_sems
    ) = refs
    parts, half_seqs = PIECES // seqs, seqs // 2
    chunks = chans * parts
    slots, group = acc.shape[0], temps[0].shape[0]
    at_once = group == half_seqs
    r, c = lax.axis_index("seq"), lax.axis_index("chan")
    core, h = lax.rem(r, 2), lax.div(r, 2)
    partners = [{"seq": flip(r, bit)} for bit in range(bits)]
    greet(partners + [{"chan": lax.rem(c + off, chans)} for off in range(1, chans)])
    partners += [{"chan": flip(c, bit)} for bit in range(chans.bit_length() - 1)]

    def slot_of(k):
        return lax.rem(k, slots)

    def core_copy(k, source):
        return remote(source.at[:, 1 - core], landed[0].at[k], c_send.at[k], c_recv.at[k], seq=flip(r, 0))

    def load(k, source):
        return pltpu.make_async_copy(source.at[:, core], acc.at[slot_of(k)], load_sem.at[k])

    def with_source(k, work):
        @pl.when(k < 3 * parts)
        def _():
            work(ffn_g.at[lax.div(k, parts), lax.rem(k, parts)])

        @pl.when(k >= 3 * parts)
        def _():
            work(io_g.at[k - 3 * parts])

    def lanes(half):
        return pl.ds(half * (D // 2), D // 2)

    def across(k, half, level):
        order = high_bits(bits, half)
        bit, rest = order[level], [one - 1 for one in order[level + 1 :]]
        base = h
        for one in rest:
            base = base - (1 << one) * lax.rem(lax.div(h, 1 << one), 2)
        first = half_seqs - (half_seqs >> level)
        copies, keeps = [], []
        for at in range(1 << len(rest)):
            place = base + sum((1 << one) for n, one in enumerate(rest) if at >> n & 1)
            copies.append(
                remote(
                    acc.at[slot_of(k), flip(place, bit - 1), :, lanes(half)],
                    landed[level + 1].at[k, at, :, lanes(half)],
                    b_send.at[k, half, first + at], b_recv.at[k, half, first + at],
                    seq=flip(r, bit),
                )
            )
            keeps.append(place)
        return copies, keeps

    def fetch(src, dst):
        copy = pltpu.make_async_copy(src, dst, temp_sem)
        copy.start()
        copy.wait()

    def begin(k):
        def work(source):
            core_copy(k, source).start()
            load(k, source).start()

        with_source(k, work)

    def level_start(k, level):
        for half in range(2):
            for copy in across(k, half, level)[0]:
                copy.start()

    def fetch_level(k, level):
        return pltpu.make_async_copy(landed[level].at[k], temps[level], fetch_sem.at[level])

    def core_arrive(k):
        load(k, io_g.at[0]).wait()
        core_copy(k, io_g.at[0]).wait_recv()
        if at_once:
            fetch_level(k, 0).start()

    def core_sum(k):
        if at_once:
            fetch_level(k, 0).wait()
        for start in range(0, half_seqs, group):
            if not at_once:
                fetch(landed[0].at[k, pl.ds(start, group)], temps[0])

            @pl.loop(0, group)
            def _(b):
                acc[slot_of(k), start + b] = add_rows(acc[slot_of(k), start + b], temps[0][b])

        level_start(k, 0)

    def level_arrive(k, level):
        for half in range(2):
            for copy in across(k, half, level)[0]:
                copy.wait_recv()
        if at_once:
            fetch_level(k, level + 1).start()

    def level_sum(k, level):
        both = [across(k, half, level) for half in range(2)]
        if at_once:
            fetch_level(k, level + 1).wait()
        temp = temps[level + 1 if at_once else 0]
        count = half_seqs >> (level + 1)
        for start in range(0, count, group):
            here = min(group, count - start)
            if not at_once:
                fetch(landed[level + 1].at[k, pl.ds(start, here)], temp.at[pl.ds(0, here)])
            for half in range(2):
                for at in range(here):
                    place = both[half][1][start + at]
                    acc[slot_of(k), place, :, lanes(half)] = add_rows(
                        acc[slot_of(k), place, :, lanes(half)], temp[at, :, lanes(half)]
                    )
        if level + 1 < levels:
            level_start(k, level + 1)

    def line(k, side):
        return remote(
            acc.at[slot_of(k), h], line_land.at[side, k], z_send.at[k], z_recv.at[side, k],
            chan=c + 1 - 2 * side,
        )

    def hop(k, step):
        keeper = lax.div(k, parts)
        for side, sends in ((0, (c < keeper) & (c == step)), (1, (c > keeper) & (chans - 1 - c == step))):

            @pl.when(sends)
            def _():
                if step > 0:
                    line(k, side).wait_recv()
                    fetch(line_land.at[side, k], line_temp.at[0])
                    acc[slot_of(k), h] = add_rows(acc[slot_of(k), h], line_temp[0])
                line(k, side).start()

    def finish(k):
        keeper = lax.div(k, parts)

        @pl.when(c == keeper)
        def _():
            for side, there in ((0, c > 0), (1, c < chans - 1)):

                @pl.when(there)
                def _():
                    line(k, side).wait_recv()
                    fetch(line_land.at[side, k], line_temp.at[side])

                @pl.when(jnp.logical_not(there))
                def _():
                    line_temp[side] = jnp.zeros(line_temp.shape[1:], BF16)

            result[lax.rem(k, parts)] = (
                acc[slot_of(k), h].astype(F32) + line_temp[0].astype(F32) + line_temp[1].astype(F32)
            ).astype(BF16)

        @pl.when(c < keeper)
        def _():
            line(k, 0).wait_send()

        @pl.when(c > keeper)
        def _():
            line(k, 1).wait_send()

        core_copy(k, io_g.at[0]).wait_send()
        for level in range(levels):
            for half in range(2):
                for copy in across(k, half, level)[0]:
                    copy.wait_send()

    def small_copy(level):
        return remote(
            sent.at[level], got.at[level], n_send.at[level], n_recv.at[level], **partners[level]
        )

    def small_step(level):
        if level == 0:
            sent[0] = sums[...]
        else:
            small_copy(level - 1).wait()
            new = sent[level - 1] + got[level - 1]
            if level == len(partners):
                total[...] = new
            else:
                sent[level] = new
        if level < len(partners):
            small_copy(level).start()

    rows, full = tokens.shape
    width = out_v.shape[-1]
    length = rows // held
    size = length - HEAD
    tile, per_tile = rows // 3, held // 3
    tiles = [pl.ds(at * tile, tile) for at in range(3)]
    own_tiles = [pl.ds(at * per_tile * size, per_tile * size) for at in range(3)]

    def mix_loads(j):
        return [
            pltpu.make_async_copy(
                io_full.at[j, :, :, :, pl.ds(0, 3 * width)], in_v, mix_sem.at[0]
            ),
            pltpu.make_async_copy(
                io_full.at[j, :, :, :, pl.ds(3 * width, width)], out_v, mix_sem.at[1]
            ),
            pltpu.make_async_copy(streams.at[j], stream, mix_sem.at[2]),
        ]

    def io_out(j):
        at, first = lax.div(4 * j, half_seqs), lax.rem(4 * j, half_seqs)
        return pltpu.make_async_copy(staging, io_g.at[at, pl.ds(first, 4)], io_sem)

    def mix_prepare():
        gain_sum = jnp.zeros((1, full), F32)
        for at, here in enumerate(tiles):
            values = residual[here]
            scale = row_scale(values)
            unit = values * scale
            grad = second_grad[here]
            scaled = grad * gains[1:2]
            new = cotangent[here] + scale * (
                scaled - unit * jnp.mean(scaled * unit, axis=1, keepdims=True)
            )
            residual_low[here] = new.astype(BF16)
            for s, (one, two) in enumerate(
                zip(own_rows(new, per_tile), own_rows(grad * unit, per_tile))
            ):
                where = pl.ds((at * per_tile + s) * size, size)
                residual_grad[where] = one
                low_own[where] = one.astype(BF16)
                gain_sum += jnp.sum(two, axis=0, keepdims=True)
            first = tokens[here]
            first = first * row_scale(first) * gains[0:1]
            for s, one in enumerate(own_rows(first, per_tile)):
                first_own[pl.ds((at * per_tile + s) * size, size)] = one.astype(BF16)
        sums[...] = jnp.zeros_like(sums)
        sums[1:2] = gain_sum
        first_grad[...] = jnp.zeros_like(first_grad)
        staging[...] = jnp.zeros_like(staging)

    def mix_step(j):
        for copy in mix_loads(j):
            copy.wait()
        in_w, out_w = in_v[...].reshape(full, 3 * width), out_v[...].reshape(full, width)
        filters = taps[j]
        for here in tiles:
            mixer_grad[here] = dot(residual_low[here], out_w)
        input_gate, output_gate, value = (
            stream[:, k * width : (k + 1) * width] for k in range(3)
        )
        keep_one, keep_two = keeps[:, 0:1], keeps[:, 1:2]
        gated = input_gate * value
        back_one, back_two = pltpu.roll(gated, 1, 0), pltpu.roll(gated, 2, 0)
        filtered = (
            filters[2:3] * gated
            + filters[1:2] * keep_one * back_one
            + filters[0:1] * keep_two * back_two
        )
        grad = mixer_grad[...]
        inner = grad * output_gate
        one, two = keep_one * inner, keep_two * inner
        gated_grad = (
            filters[2:3] * inner
            + filters[1:2] * pltpu.roll(one, rows - 1, 0)
            + filters[0:1] * pltpu.roll(two, rows - 2, 0)
        )

        def own_sum(values):
            return sum(jnp.sum(part, axis=0, keepdims=True) for part in own_rows(values, held))

        where = pl.ds(pl.multiple_of(j * width, width), width)
        sums[4:5, where] = own_sum(inner * gated)
        sums[3:4, where] = own_sum(one * back_one)
        sums[2:3, where] = own_sum(two * back_two)
        for k, values in enumerate((gated_grad * value, grad * filtered, gated_grad * input_gate)):
            for s, part in enumerate(own_rows(values, held)):
                stream_own[pl.ds(s * size, size), k * width : (k + 1) * width] = part.astype(BF16)
        for s, part in enumerate(own_rows(output_gate * filtered, held)):
            mixed_own[pl.ds(s * size, size)] = part.astype(BF16)
        for here in own_tiles:
            first_grad[here] += contract_last(stream_own[here], in_w)

        @pl.when(j > 0)
        def _():
            io_out(j - 1).wait()

        for k in range(4):
            if k < 3:
                new = contract_first(stream_own[:, k * width : (k + 1) * width], first_own[...])
            else:
                new = contract_first(mixed_own[...], low_own[...])
            staging[k, :, pl.ds(0, SMALL_PIECE)] = new.astype(BF16).reshape(2, SMALL_PIECE, full)
        io_out(j).start()

        @pl.when(j + 1 < chans)
        def _():
            for copy in mix_loads(j + 1):
                copy.start()

    def mix_end():
        gain_sum = jnp.zeros((1, full), F32)
        for s in range(held):
            here = pl.ds(s * size, size)
            values = tokens[pl.ds(s * length + HEAD, size)]
            scale = row_scale(values)
            unit = values * scale
            grad = first_grad[here]
            scaled = grad * gains[0:1]
            gain_sum += jnp.sum(grad * unit, axis=0, keepdims=True)
            input_grad[here] = (
                residual_grad[here]
                + scale * (scaled - unit * jnp.mean(scaled * unit, axis=1, keepdims=True))
            ).astype(BF16)
        sums[0:1] = gain_sum
        io_out(chans - 1).wait()

    spread_out = parts == 4
    mix_first, mix_last = (1, 3 * parts - 2) if spread_out else (-1, -1)
    relay = Relay(chans, block_own, blocks, relay_sems[:3])
    input_relay = Relay(chans, input_grad, input_blocks, relay_sems[3:])
    for copy in mix_loads(0):
        copy.start()
    begin(0)
    relay.step(0)
    mix_prepare()
    if not spread_out:

        @pl.loop(0, chans)
        def _(j):
            mix_step(j)

        mix_end()

    summed = LAG * (1 + levels)

    @pl.loop(1, chunks + summed + LAG * (chans - 1))
    def _(tick):
        def stage(k, work):
            @pl.when((k >= 0) & (k < chunks))
            def _():
                work(k)

        stage(tick - summed - LAG * (chans - 1), finish)
        stage(tick, begin)
        for step in range(chans - 2, 0, -1):
            stage(tick - summed - LAG * step, lambda k: hop(k, step))
        for level in range(levels - 1, -1, -1):
            stage(tick - LAG * (2 + level), lambda k: level_arrive(k, level))
        stage(tick - LAG, core_arrive)
        for level in range(levels - 1, -1, -1):

            def work(k):
                level_sum(k, level)
                if level == levels - 1:
                    hop(k, 0)

            stage(tick - LAG * (2 + level), work)
        stage(tick - LAG, core_sum)
        if spread_out:

            @pl.when((tick >= mix_first) & (tick < mix_first + 2 * chans) & (lax.rem(tick - mix_first, 2) == 0))
            def _():
                mix_step(lax.div(tick - mix_first, 2))

            @pl.when(tick == mix_last)
            def _():
                mix_end()

        for level in range(len(partners) + 1):

            @pl.when(tick == mix_last + 2 + level)
            def _():
                small_step(level)

        for step in (1, 2):

            @pl.when(tick == 7 * step)
            def _():
                relay.step(step)

        @pl.when(tick == mix_last + 6)
        def _():
            input_relay.step(0)

    relay.finish(range(chans - 1))
    input_relay.finish([0])


def backward_pass(
    seqs, chans, held, ffn_g, io_full, streams, block_own, tokens, residual, second_grad,
    cotangent, keeps, gains, taps,
):
    dma, vmem, shape = pltpu.SemaphoreType.DMA, pltpu.VMEM, jax.ShapeDtypeStruct
    parts, half_seqs = PIECES // seqs, seqs // 2
    levels = seqs.bit_length() - 2
    chunks = chans * parts
    slots = min(chunks, LAG * (levels + chans) + 1)
    group = min(4, half_seqs)
    sizes = [group] + [half_seqs >> level if group == half_seqs else 1 for level in range(1, levels + 1)]
    partners = (seqs * chans).bit_length() - 1
    rows, width = tokens.shape
    own_count = rows - held * HEAD
    part = io_full.shape[-1] // 4
    outs = [
        shape((parts, PIECE, D), BF16),
        shape((8, width), F32),
        shape((own_count, width), BF16),
        shape((parts, half_seqs, 2, PIECE, D), BF16),
        shape((chans,) + block_own.shape, BF16),
        shape((chans,) + block_own.shape, BF16),
        shape((chunks, half_seqs, PIECE, D), BF16),
    ]
    outs += [
        shape((chunks, half_seqs >> (level + 1), PIECE, D), BF16) for level in range(levels)
    ]
    outs.append(shape((2, chunks, PIECE, D), BF16))
    return call(
        functools.partial(backward_kernel, seqs, chans, held),
        outs,
        [pl.ANY] * 4 + [vmem] * 7,
        [vmem] * 3 + [pl.ANY] * (len(outs) - 3),
        [
            *[vmem((size, PIECE, D), BF16) for size in sizes],
            vmem((slots, half_seqs, PIECE, D), BF16),
            vmem((2, PIECE, D), BF16),
            vmem((partners, 8, width), F32),
            vmem((partners, 8, width), F32),
            vmem((8, width), F32),
            vmem((rows, width), BF16),
            vmem((own_count, width), BF16),
            vmem((own_count, width), BF16),
            vmem((own_count, width), F32),
            vmem((own_count, 3 * part), BF16),
            vmem((own_count, part), BF16),
            vmem((rows, part), F32),
            vmem((own_count, width), F32),
            vmem((rows, 3 * part), F32),
            vmem(io_full.shape[1:4] + (3 * part,), BF16),
            vmem(io_full.shape[1:4] + (part,), BF16),
            vmem((4, 2, PIECE, D), BF16),
            dma((chunks,)),
            dma(()),
            dma((levels + 1,)),
            dma((chunks,)),
            dma((chunks,)),
            dma((chunks, 2, half_seqs)),
            dma((chunks, 2, half_seqs)),
            dma((chunks,)),
            dma((2, chunks)),
            dma((partners,)),
            dma((partners,)),
            dma((3,)),
            dma(()),
            *Relay.semaphores(chans),
            *Relay.semaphores(chans),
        ],
        1,
        ffn_g.reshape(3, parts, half_seqs, 2, PIECE, D),
        io_full, streams, block_own, tokens, residual, second_grad, cotangent, keeps, gains,
        taps,
        vmem=62,
    )[:6]


def shifted(value, axes, by):
    length = lax.axis_size(axes)
    pairs = [(i, i + by) for i in range(length) if 0 <= i + by < length]
    return lax.ppermute(value, axes, pairs)


def adam_update(param, gradient, first, second):
    first_new = FIRST_DECAY * first + (1.0 - FIRST_DECAY) * gradient
    second_new = SECOND_DECAY * second + (1.0 - SECOND_DECAY) * gradient * gradient
    first_fix = 1.0 - FIRST_DECAY**STEP
    second_fix = 1.0 - SECOND_DECAY**STEP
    param_new = param - ADAM_RATE * (first_new / first_fix) / (
        jnp.sqrt(second_new / second_fix) + ADAM_EPS
    )
    return (param_new, first_new, second_new)


COLUMNS = [3 * D, D, FF, FF, FF]
RATES = [1.0, 1.0, 1.0, 1.0, 0.5]


def last_kernel(block_low, input_low, grad_home, ortho_home, *refs):
    weights, moments, (block_out, input_grad) = refs[:5], refs[5:10], refs[10:12]
    moments_new, weights_new = refs[12:22:2], refs[13:22:2]
    step = pl.program_id(0)
    for low, whole in ((block_low, block_out), (input_low, input_grad)):
        rows = low.shape[2]
        for at in range(low.shape[0]):
            whole[0, at * rows : (at + 1) * rows] = low[at, 0].astype(F32)

    def update(index, at, lanes, grad, ortho):
        rate = RATES[index]
        here = at + (slice(None), lanes)
        moments_new[index][here] = MOMENTUM_DECAY * moments[index][here] + grad.astype(F32).T
        weights_new[index][here] = (
            weights[index][here] * (1.0 - WEIGHT_DECAY * rate)
            - rate * math.sqrt(COLUMNS[index] / D) * ortho.astype(F32).T
        )

    for m in range(3):

        @pl.when(step == m)
        def _():
            for t in range(TILES):
                rows = slice(t * UNIT, (t + 1) * UNIT)
                update(
                    m + 2, (), slice(t * LANES, (t + 1) * LANES),
                    *(home[m, :, rows].reshape(LANES, -1) for home in (grad_home, ortho_home)),
                )

    @pl.when(step == 3)
    def _():
        for q in range(PER_CHAN):
            lanes = slice(q % 2 * SMALL_PIECE, (q % 2 + 1) * SMALL_PIECE)
            blocks = [home[3, q, 0:SMALL_PIECE] for home in (grad_home, ortho_home)]
            update(*((0, (q // 2,)) if q < IN_PIECES else (1, ())), lanes, *blocks)


def last_pass(block_low, input_low, homes, weights, moments):
    chans, held, sub, width = block_low.shape
    low = pl.BlockSpec((chans, 1, sub, width), lambda s: (0, s, 0, 0))
    whole = pl.BlockSpec((1, chans * sub, width), lambda s: (s, 0, 0))

    def all_of(array):
        return pl.BlockSpec(array.shape, lambda s: (0,) * array.ndim)

    shape = jax.ShapeDtypeStruct
    outs = [shape((held, chans * sub, width), F32)] * 2
    out_specs = [whole] * 2
    for weight in weights:
        outs += [shape(weight.shape, F32)] * 2
        out_specs += [all_of(weight)] * 2
    return pl.pallas_call(
        last_kernel,
        grid=(held,),
        out_shape=outs,
        in_specs=[low] * 2 + [all_of(one) for one in (*homes, *weights, *moments)],
        out_specs=out_specs,
        compiler_params=pltpu.CompilerParams(vmem_limit_bytes=60 * 1024 * 1024),
    )(block_low, input_low, *homes, *weights, *moments)


def on_device(
    tokens,
    segment_ids,
    cotangent,
    norm_gains,
    filter_weight,
    in_weight,
    out_weight,
    gate_weight,
    up_weight,
    down_weight,
    norm_gains_mean,
    norm_gains_square,
    filter_mean,
    filter_square,
    in_momentum,
    out_momentum,
    gate_momentum,
    up_momentum,
    down_momentum,
):
    seqs, chans = lax.axis_size("seq"), lax.axis_size("chan")
    r, c = lax.axis_index("seq"), lax.axis_index("chan")
    seq_total, local_rows, width = tokens.shape
    sub = local_rows // chans
    chan_width = filter_weight.shape[1]

    weights = [in_weight.transpose(1, 0, 2), out_weight, gate_weight, up_weight, down_weight]
    moments = [
        in_momentum.transpose(1, 0, 2), out_momentum, gate_momentum, up_momentum, down_momentum
    ]

    def share(array, start, length):
        return lax.dynamic_slice_in_dim(array, start, length, axis=1)

    positions = r * local_rows + jnp.arange(local_rows, dtype=jnp.int32)
    local_keeps = jnp.stack(
        [(segment_ids <= positions[None, :] - offset).astype(F32) for offset in (1, 2)], axis=-1
    )
    following = jnp.where(
        c == chans - 1,
        shifted(local_keeps[:, :2], "seq", -1),
        share(local_keeps, lax.rem(c + 1, chans) * sub, 2),
    )
    following = jnp.concatenate([following[-1:], following[:-1]])
    gap = jnp.zeros((seq_total, HEAD - 2, 2), F32)
    keeps = jnp.concatenate([following, gap, share(local_keeps, c * sub, sub)], axis=1).reshape(-1, 2)

    (
        io_full, _, taps, moments_held, _, streams, ffn_grads,
        token_rows, upstream_rows, residual, second_grad, block_out,
    ) = forward_pass(
        seqs, chans, weights, moments, filter_weight, tokens, cotangent, keeps, norm_gains
    )
    moments_held = moments_held.transpose(0, 2, 1, 3).reshape(-1, D)
    grads_held, small, _, _, block_out, input_grad = backward_pass(
        seqs, chans, seq_total, ffn_grads, io_full, streams, block_out, token_rows, residual,
        second_grad, upstream_rows, keeps, norm_gains, taps,
    )

    gains_new, gains_mean_new, gains_square_new = adam_update(
        norm_gains, small[:2], norm_gains_mean, norm_gains_square
    )
    filter_new, filter_mean_new, filter_square_new = adam_update(
        filter_weight, share(small[2:5], c * chan_width, chan_width), filter_mean, filter_square
    )

    *homes, input_grad = orthogonalize(
        seqs, chans, grads_held.reshape(-1, D), moments_held, input_grad
    )
    block_out, input_grad = (
        one.reshape(chans, seq_total, sub, width) for one in (block_out, input_grad)
    )
    block_out, input_grad, *results = last_pass(block_out, input_grad, homes, weights, moments)
    results[:2] = [one.transpose(1, 0, 2) for one in results[:2]]
    return (
        block_out,
        input_grad,
        gains_new,
        gains_mean_new,
        gains_square_new,
        filter_new,
        filter_mean_new,
        filter_square_new,
        *results,
    )


def solution(mesh):
    return jax.shard_map(
        on_device,
        mesh=mesh,
        in_specs=(
            P(None, "seq", None),
            P(None, "seq"),
            P(None, "seq", None),
            P(),
            P(None, "chan"),
            P("seq", None, "chan"),
            P("seq", "chan"),
            P("seq", "chan"),
            P("seq", "chan"),
            P("seq", "chan"),
            P(),
            P(),
            P(None, "chan"),
            P(None, "chan"),
            P("seq", None, "chan"),
            P("seq", "chan"),
            P("seq", "chan"),
            P("seq", "chan"),
            P("seq", "chan"),
        ),
        out_specs=(
            P(None, "seq", None),
            P(None, "seq", None),
            P(),
            P(),
            P(),
            P(None, "chan"),
            P(None, "chan"),
            P(None, "chan"),
            P("seq", None, "chan"),
            P("seq", None, "chan"),
            P("seq", "chan"),
            P("seq", "chan"),
            P("seq", "chan"),
            P("seq", "chan"),
            P("seq", "chan"),
            P("seq", "chan"),
            P("seq", "chan"),
            P("seq", "chan"),
        ),
        check_vma=False,
    )
```

```python
import functools
import math

import jax
import jax.numpy as jnp
from jax import lax
from jax.experimental import pallas as pl
from jax.experimental.pallas import tpu as pltpu
from jax.sharding import PartitionSpec as P

D = 1024
FF = 4608
NS_ITERS = 4
STEP = 10


NORM_EPS = 1e-05
QUINTIC_FIRST = 3.4445
QUINTIC_SECOND = -4.775
QUINTIC_THIRD = 2.0315
MOMENTUM_DECAY = 0.95
FIRST_DECAY = 0.9
SECOND_DECAY = 0.999
ADAM_EPS = 1e-08
ADAM_RATE = 0.4
WEIGHT_DECAY = 0.01
ORTHO_EPS = 1e-07

MESH = pl.DeviceIdType.MESH
BF16 = jnp.bfloat16
F32 = jnp.float32

PIECES = 32
PER_CHAN = 8
PIECE = FF // PIECES
LANES = 128
TILES = FF // 4 // LANES
UNIT = LANES // PER_CHAN
SMALL_PIECE = 4 * D // PIECES
IN_PIECES = 6


def remote(src, dst, send, recv, **place):
    return pltpu.make_async_remote_copy(
        src_ref=src, dst_ref=dst, send_sem=send, recv_sem=recv, device_id=place, device_id_type=MESH
    )


def flip(index, bit):
    step = 1 << bit
    return index + step * (1 - 2 * lax.rem(lax.div(index, step), 2))


def flips(index, bits):
    found = [index]
    for bit in bits:
        found = found + [flip(one, bit) for one in found]
    return found


def greet(places):
    barrier = pltpu.get_barrier_semaphore()
    for place in places:
        pl.semaphore_signal(barrier, inc=1, device_id=place, device_id_type=MESH)
    pl.semaphore_wait(barrier, len(places))


def high_bits(bits, half):
    order = list(range(1, bits))
    return order if half == 0 else order[::-1]


def call(kernel, outs, in_spaces, out_spaces, scratch, ident, *args, vmem=48, aliases=None):
    return pl.pallas_call(
        kernel,
        out_shape=outs,
        in_specs=[pl.BlockSpec(memory_space=space) for space in in_spaces],
        out_specs=jax.tree.map(lambda space: pl.BlockSpec(memory_space=space), out_spaces),
        scratch_shapes=scratch,
        input_output_aliases=aliases or {},
        compiler_params=pltpu.CompilerParams(
            collective_id=ident, has_side_effects=True, vmem_limit_bytes=vmem * 1024 * 1024
        ),
    )(*args)


def holder(r, c, seqs):
    at = lax.rem(r + PIECES * seqs - PER_CHAN * c, seqs)
    return at, at < PER_CHAN, lax.div(PER_CHAN * c + at, seqs)


class Homeward:
    def __init__(self, seqs, chans, held, out, between, sems):
        self.seqs, self.chans, self.held, self.out, self.between = seqs, chans, held, out, between
        self.own_sem, self.stay_sem, self.a_send, self.a_recv, self.b_send, self.b_recv = sems
        self.r, self.c = lax.axis_index("seq"), lax.axis_index("chan")
        self.at_out, self.has, self.place = holder(self.r, self.c, seqs)

    def target(self, at):
        return lax.div(self.r + self.seqs * at, PER_CHAN)

    def dropping(self, at):
        return remote(
            self.held.at[at], self.between.at[self.c], self.a_send.at[at], self.a_recv.at[self.c],
            chan=self.target(at),
        )

    def keeping(self, at):
        return pltpu.make_async_copy(self.held.at[at], self.between.at[self.c], self.own_sem.at[0])

    def spreading(self, m, r_to):
        return remote(
            self.between.at[m, r_to], self.out.at[m, self.at_out],
            self.b_send.at[m, r_to], self.b_recv.at[m, self.at_out], seq=r_to,
        )

    def staying(self, m):
        return pltpu.make_async_copy(
            self.between.at[m, self.r], self.out.at[m, self.at_out], self.stay_sem.at[m]
        )

    def drop(self, at):
        @pl.when(self.target(at) != self.c)
        def _():
            self.dropping(at).start()

        @pl.when(self.target(at) == self.c)
        def _():
            self.keeping(at).start()

    def spread(self):
        @pl.when(self.has)
        def _():
            for off in (0, 1, 3, 2):
                m = lax.rem(self.c + off, self.chans)
                if off == 0:
                    self.keeping(0).wait()
                else:
                    remote(
                        self.held.at[0], self.between.at[m], self.a_send.at[0], self.a_recv.at[m], chan=m
                    ).wait_recv()
                for step in range(1, self.seqs):
                    self.spreading(m, lax.rem(self.r + step, self.seqs)).start()
                self.staying(m).start()

    def finish(self):
        @pl.when(self.has)
        def _():
            for m in range(self.chans):
                self.staying(m).wait()

        for piece in range(PER_CHAN):
            r_from = lax.rem(PER_CHAN * self.c + piece, self.seqs)

            @pl.when(r_from != self.r)
            def _():
                for m in range(self.chans):
                    remote(
                        self.between.at[m, self.r], self.out.at[m, piece],
                        self.b_send.at[m, self.r], self.b_recv.at[m, piece], seq=r_from,
                    ).wait_recv()

        for at in range(PIECES // self.seqs):

            @pl.when(self.target(at) != self.c)
            def _():
                self.dropping(at).wait_send()

        @pl.when(self.has)
        def _():
            for m in range(self.chans):
                for step in range(1, self.seqs):
                    self.spreading(m, lax.rem(self.r + step, self.seqs)).wait_send()

    @staticmethod
    def semaphores(seqs, chans):
        dma = pltpu.SemaphoreType.DMA
        return [
            dma((1,)), dma((chans,)), dma((PIECES // seqs,)), dma((chans,)),
            dma((chans, seqs)), dma((chans, PER_CHAN)),
        ]


class Relay:
    def __init__(self, chans, own, blocks, sems):
        self.chans, self.own, self.blocks = chans, own, blocks
        self.own_sem, self.send, self.recv = sems
        self.c = lax.axis_index("chan")

    def keeping(self):
        return pltpu.make_async_copy(self.own, self.blocks.at[self.c], self.own_sem.at[0])

    def copies(self, hop):
        c = self.c
        for side, block, sends in (
            (0, c - hop, (c < self.chans - 1) & (c >= hop)),
            (1, c + hop, (c > 0) & (c + hop < self.chans)),
        ):
            source = self.own if hop == 0 else self.blocks.at[block]
            yield sends, remote(
                source, self.blocks.at[block], self.send.at[side, hop], self.recv.at[side, hop],
                chan=c + 1 - 2 * side,
            )

    def await_hop(self, hop):
        c = self.c
        for side, block, comes in ((0, c - 1 - hop, c > hop), (1, c + 1 + hop, c + 1 + hop < self.chans)):

            @pl.when(comes)
            def _():
                remote(
                    self.blocks.at[block], self.blocks.at[block],
                    self.send.at[side, hop], self.recv.at[side, hop], chan=c - 1 + 2 * side,
                ).wait_recv()

    def step(self, hop, first=False):
        if hop == 0:
            self.keeping().start()
        elif not first:
            self.await_hop(hop - 1)
        for sends, copy in self.copies(hop):

            @pl.when(sends)
            def _():
                copy.start()

    def finish(self, hops):
        self.await_hop(hops[-1])
        if 0 in hops:
            self.keeping().wait()
        for hop in hops:
            for sends, copy in self.copies(hop):

                @pl.when(sends)
                def _():
                    copy.wait_send()

    @staticmethod
    def semaphores(chans):
        dma = pltpu.SemaphoreType.DMA
        return [dma((1,)), dma((2, chans - 1)), dma((2, chans - 1))]


def dot(left, right):
    return jnp.dot(left, right, preferred_element_type=F32)


def contract_last(left, right):
    return lax.dot_general(left, right, (((1,), (1,)), ((), ())), preferred_element_type=F32)


def contract_first(left, right):
    return lax.dot_general(left, right, (((0,), (0,)), ((), ())), preferred_element_type=F32)


def ortho_kernel(
    seqs, chans, grad, moment, _, grad_home, ortho_home, input_blocks,
    out, cut_grad, cut_ortho, between_grad, between_ortho,
    part, own, swapped, paired, parts, sums, gram, poly, half_way,
    x_send, x_recv, s_send, s_recv, g_send, g_recv, f_send, f_recv, *home_sems
):
    r, c = lax.axis_index("seq"), lax.axis_index("chan")
    core, h = lax.rem(r, 2), lax.div(r, 2)
    other = flip(r, 0)
    count, half, block = seqs // 2, D // 2, D // seqs
    tile = min(256, half)
    peers = [lax.rem(h + off, count) for off in range(1, count)]
    greet(
        [{"seq": lax.rem(r + off, seqs)} for off in range(1, seqs)]
        + [{"chan": lax.rem(c + off, chans)} for off in range(1, chans)]
    )
    home_grad = Homeward(seqs, chans, cut_grad, grad_home, between_grad, home_sems[:6])
    home_ortho = Homeward(seqs, chans, cut_ortho, ortho_home, between_ortho, home_sems[6:12])
    relay = Relay(chans, None, input_blocks, home_sems[12:])
    columns = out.shape[0]
    slab = PIECE

    @pl.loop(0, columns // slab)
    def _(at):
        here = pl.ds(pl.multiple_of(at * slab, slab), slab)
        out[here] = (MOMENTUM_DECAY * moment[here].astype(F32) + grad[here].astype(F32)).astype(BF16)
        for to in range(seqs):
            cut_grad[at, to] = grad[here, to * block : (to + 1) * block]

    for at in range(columns // slab):
        home_grad.drop(at)
    relay.step(1, first=True)

    apart = c == chans - 1

    def kind(pair):
        return jnp.where(lax.rem(pair, 4) == 3, 1, 0)

    mine = kind(h)
    own_first = pl.multiple_of(core * half, half)
    other_first = pl.multiple_of((1 - core) * half, half)

    def block_at(pair, which):
        return pl.ds(pl.multiple_of(which * half + pair * block, block), block)

    def exchange():
        return remote(part, swapped, x_send, x_recv, seq=other)

    def scatter(peer):
        return remote(
            paired.at[peer], parts.at[h], s_send.at[peer], s_recv.at[h], seq=2 * peer + core
        )

    def scatter_in(peer):
        return remote(
            paired.at[peer], parts.at[peer], s_send.at[peer], s_recv.at[peer], seq=2 * peer + core
        )

    def share(peer):
        return remote(
            sums.at[kind(peer)], gram.at[block_at(h, core)], g_send.at[peer], g_recv.at[h],
            seq=2 * peer + core,
        )

    def share_in(peer):
        return remote(
            sums.at[0], gram.at[block_at(peer, core)], g_send.at[peer], g_recv.at[peer],
            seq=2 * peer + core,
        )

    def forward(pair):
        return remote(
            gram.at[block_at(pair, core)], gram.at[block_at(pair, core)],
            f_send.at[pair], f_recv.at[pair], seq=other,
        )

    def forward_in(pair):
        return remote(
            gram.at[block_at(pair, 1 - core)], gram.at[block_at(pair, 1 - core)],
            f_send.at[pair], f_recv.at[pair], seq=other,
        )

    for turn in range(NS_ITERS // 2):

        @pl.loop(0, half // tile)
        def _(at):
            here = pl.ds(pl.multiple_of(at * tile, tile), tile)
            there = pl.ds(pl.multiple_of(other_first + at * tile, tile), tile)
            part[here] = contract_first(out[:, there], out[...]).astype(BF16)

        exchange().start()

        @pl.loop(0, half // tile)
        def _(at):
            here = pl.ds(pl.multiple_of(at * tile, tile), tile)
            there = pl.ds(pl.multiple_of(own_first + at * tile, tile), tile)
            own[here] = contract_first(out[:, there], out[...])

        exchange().wait()

        @pl.loop(0, count)
        def _(at):
            here = pl.ds(pl.multiple_of(at * block, block), block)
            paired[at] = (own[here] + swapped[here].astype(F32)).astype(BF16)

        for peer in peers:
            scatter(peer).start()
        parts[h] = paired[h]
        for peer in peers:
            scatter_in(peer).wait_recv()
        groups = [jnp.zeros((block, D), F32), jnp.zeros((block, D), F32)]
        for pair in range(count):
            groups[int(pair % 4 == 3)] += parts[pair].astype(F32)
        both = groups[0] + groups[1]
        sums[0] = jnp.where(apart, groups[0], both).astype(BF16)
        sums[1] = jnp.where(apart, groups[1], both).astype(BF16)
        for peer in peers:
            share(peer).start()
        gram[block_at(h, core)] = sums[mine]
        forward(h).start()
        for peer in peers:
            share_in(peer).wait_recv()
            forward(peer).start()
        for pair in [h] + peers:
            forward_in(pair).wait_recv()
        for peer in peers:
            scatter(peer).wait_send()
            share(peer).wait_send()
        for pair in [h] + peers:
            forward(pair).wait_send()

        scale = jnp.ones((1, 1), F32)
        if turn == 0:
            trace = jnp.zeros((1, 1), F32)
            for at in range(D // 128):
                square = gram[at * 128 : (at + 1) * 128, at * 128 : (at + 1) * 128].astype(F32)
                row = lax.broadcasted_iota(jnp.int32, square.shape, 0)
                column = lax.broadcasted_iota(jnp.int32, square.shape, 1)
                trace += jnp.sum(jnp.where(row == column, square, 0.0), keepdims=True)
            scale = 1.0 / (jnp.sqrt(trace) + ORTHO_EPS)

            @pl.loop(0, D // tile)
            def _(at):
                here = pl.ds(pl.multiple_of(at * tile, tile), tile)
                gram[here] = (gram[here].astype(F32) * scale * scale).astype(BF16)

        def each_tile(work):
            @pl.loop(0, D // tile)
            def _(at):
                work(pl.ds(pl.multiple_of(at * tile, tile), tile))

        def polynomial(values, whole):
            return (
                QUINTIC_SECOND * values.astype(F32) + QUINTIC_THIRD * dot(values, whole[...])
            ).astype(BF16)

        def first_poly(here):
            poly[here] = polynomial(gram[here], gram)

        def halfway(here):
            half_way[here] = (
                QUINTIC_FIRST * gram[here].astype(F32) + dot(poly[here], gram[...])
            ).astype(BF16)

        def next_gram(here):
            gram[here] = (
                QUINTIC_FIRST * half_way[here].astype(F32) + dot(half_way[here], poly[...])
            ).astype(BF16)

        def second_poly(here):
            half_way[here] = polynomial(gram[here], gram)

        for work in (first_poly, halfway, next_gram, second_poly):
            each_tile(work)

        @pl.loop(0, columns // slab)
        def _(at):
            here = pl.ds(pl.multiple_of(at * slab, slab), slab)
            new = QUINTIC_FIRST * out[here].astype(F32) + dot(out[here], poly[...])
            if turn == 0:
                new = new * scale
            new = QUINTIC_FIRST * new + dot(new.astype(BF16), half_way[...])
            if turn < NS_ITERS // 2 - 1:
                out[here] = new.astype(BF16)
            else:
                for to in range(seqs):
                    cut_ortho[at, to] = new[:, to * block : (to + 1) * block].astype(BF16)
                home_ortho.drop(at)

        if turn == 0:
            home_grad.spread()
            relay.step(2)

    home_ortho.spread()
    home_grad.finish()
    relay.finish(range(1, chans - 1))
    home_ortho.finish()


def orthogonalize(seqs, chans, grad, moment, input_blocks):
    dma = pltpu.SemaphoreType.DMA
    count, block, held = seqs // 2, D // seqs, PIECES // seqs
    return call(
        functools.partial(ortho_kernel, seqs, chans),
        [jax.ShapeDtypeStruct((chans, PER_CHAN, PIECE, block), BF16)] * 2
        + [jax.ShapeDtypeStruct(input_blocks.shape, BF16)],
        [pltpu.VMEM] * 2 + [pl.ANY],
        [pl.ANY] * 3,
        [
            pltpu.VMEM(grad.shape, BF16),
            pltpu.VMEM((held, seqs, PIECE, block), BF16),
            pltpu.VMEM((held, seqs, PIECE, block), BF16),
            pltpu.VMEM((chans, seqs, PIECE, block), BF16),
            pltpu.VMEM((chans, seqs, PIECE, block), BF16),
            pltpu.VMEM((D // 2, D), BF16),
            pltpu.VMEM((D // 2, D), F32),
            pltpu.VMEM((D // 2, D), BF16),
            pltpu.VMEM((count, block, D), BF16),
            pltpu.VMEM((count, block, D), BF16),
            pltpu.VMEM((2, block, D), BF16),
            pltpu.VMEM((D, D), BF16),
            pltpu.VMEM((D, D), BF16),
            pltpu.VMEM((D, D), BF16),
            dma(()),
            dma(()),
        ]
        + [dma((count,))] * 6
        + Homeward.semaphores(seqs, chans) * 2
        + Relay.semaphores(chans),
        2,
        grad,
        moment,
        input_blocks,
        aliases={2: 2},
    )


HEAD = 8


def own_rows(values, seqs_held):
    length = values.shape[0] // seqs_held
    return [values[s * length + HEAD : (s + 1) * length] for s in range(seqs_held)]


def row_scale(values):
    return lax.rsqrt(jnp.mean(values * values, axis=1, keepdims=True) + NORM_EPS)


def filtering(gated, taps, keep_one, keep_two):
    back_one, back_two = pltpu.roll(gated, 1, 0), pltpu.roll(gated, 2, 0)
    return taps[2:3] * gated + taps[1:2] * keep_one * back_one + taps[0:1] * keep_two * back_two


def forward_kernel(seqs, chans, held, *refs):
    forward_work(seqs, chans, held, refs[:5], refs[5:10], *refs[10:])


def forward_work(
    seqs, chans, held,
    weights, moments, own_taps, token_source, cotangent_source, keeps, gains,
    in_full, out_full, ffn_full, taps_all, held_out, between, streams, ffn_g,
    tokens, cotangent, residual, second_grad, block_out,
    in_shard, out_shard, ffn_shard, taps, packed, shelf, shelf_sem,
    u, u_own, halo, row_sem, halo_sem, halo_send, halo_recv, normed, mixed, stream, x, x_own, ffn_out, act, gate_low, up_low, in_v, out_v, taps_v, w_v, grad_v,
    own_sem, z_send, z_recv, b_send, b_recv, c_send, c_recv,
    t_own, t_send, t_recv, p_own, ps_send, ps_recv, pl_send, pl_recv,
    mix_sem, taps_sem, stream_sem, load_sem, grad_sem,
):
    bits = seqs.bit_length() - 1
    r, c = lax.axis_index("seq"), lax.axis_index("chan")
    last = TILES + 1
    greet(
        [{"chan": lax.rem(c + off, chans)} for off in range(1, chans)]
        + [{"seq": lax.rem(r + off, seqs)} for off in range(1, seqs)]
    )

    def shard(k):
        if isinstance(k, int) and k < 2:
            return (in_shard, out_shard)[k]
        return ffn_shard.at[k - 2]

    def full(k, part, block):
        if isinstance(k, int) and k < 2:
            return (in_full, out_full)[k].at[part, block]
        return ffn_full.at[k - 2, part, block]

    def own(k):
        return pltpu.make_async_copy(shard(k), full(k, c, r), own_sem.at[k])

    def along_chan(k, off, incoming):
        source = lax.rem(c + chans - off, chans) if incoming else c
        return remote(
            shard(k), full(k, source, r), z_send.at[k, off - 1], z_recv.at[k, off - 1],
            chan=lax.rem(c + off, chans),
        )

    def across(k, half, step, incoming):
        order = high_bits(bits, half)
        bit, done = order[step], order[:step]
        base = flip(r, bit) if incoming else r
        part = pl.ds(half * (chans // 2), chans // 2)
        first = (1 << step) - 1
        return [
            remote(
                full(k, part, block), full(k, part, block),
                b_send.at[k, half, first + at], b_recv.at[k, half, first + at], seq=flip(r, bit),
            )
            for at, block in enumerate(flips(base, done))
        ]

    def core(k, incoming):
        base = flip(r, 0) if incoming else r
        return [
            remote(
                full(k, slice(None), block), full(k, slice(None), block),
                c_send.at[k, at], c_recv.at[k, at], seq=flip(r, 0),
            )
            for at, block in enumerate(flips(base, range(1, bits)))
        ]

    def start_chan(k):
        own(k).start()
        for off in (2, 1, 3):
            along_chan(k, off, False).start()

    def first_level(k):
        own(k).wait()
        for off in range(1, chans):
            along_chan(k, off, True).wait_recv()
        for half in range(2):
            for copy in across(k, half, 0, False):
                copy.start()

    def next_level(k, level):
        for half in range(2):
            for copy in across(k, half, level - 1, True):
                copy.wait_recv()
            for copy in across(k, half, level, False):
                copy.start()

    def to_core(k):
        for half in range(2):
            for copy in across(k, half, bits - 2, True):
                copy.wait_recv()
        for copy in core(k, False):
            copy.start()

    def arrived(k):
        for copy in core(k, True):
            copy.wait_recv()

    def sent(k):
        for off in range(1, chans):
            along_chan(k, off, False).wait_send()
        for half in range(2):
            for step in range(bits - 1):
                for copy in across(k, half, step, False):
                    copy.wait_send()
        for copy in core(k, False):
            copy.wait_send()

    def taps_copy(off, incoming):
        source = lax.rem(c + chans - off, chans) if incoming else c
        return remote(
            taps, taps_all.at[source], t_send.at[off - 1], t_recv.at[off - 1],
            chan=lax.rem(c + off, chans),
        )

    _, has, place = holder(r, c, seqs)

    def spread(piece, r_to):
        return remote(
            packed.at[:, piece], between.at[:, r], ps_send.at[piece], ps_recv.at[r], seq=r_to
        )

    def lift(m):
        return remote(between.at[m], held_out.at[place], pl_send.at[m], pl_recv.at[place], chan=m)

    def pieces_start():
        for piece in range(PER_CHAN):
            r_to = lax.rem(PER_CHAN * c + piece, seqs)

            @pl.when(r_to != r)
            def _():
                spread(piece, r_to).start()

            @pl.when(r_to == r)
            def _():
                pltpu.make_async_copy(packed.at[:, piece], between.at[:, r], p_own.at[0]).start()

    def pieces_lift():
        @pl.when(has)
        def _():
            pltpu.make_async_copy(packed.at[:, 0], between.at[:, r], p_own.at[0]).wait()
            for off in range(1, seqs):
                r_from = lax.rem(r + off, seqs)
                remote(
                    packed.at[:, 0], between.at[:, r_from], ps_send.at[0], ps_recv.at[r_from], seq=r_from
                ).wait_recv()
            for m in range(chans):

                @pl.when(m != c)
                def _():
                    lift(m).start()

                @pl.when(m == c)
                def _():
                    copy = pltpu.make_async_copy(between.at[m], held_out.at[place], p_own.at[1])
                    copy.start()
                    copy.wait()

    def pieces_finish():
        for at in range(PIECES // seqs):
            c_from = lax.div(r + seqs * at, PER_CHAN)

            @pl.when(c_from != c)
            def _():
                remote(
                    between.at[0], held_out.at[at], pl_send.at[0], pl_recv.at[at], chan=c_from
                ).wait_recv()

        for piece in range(PER_CHAN):
            r_to = lax.rem(PER_CHAN * c + piece, seqs)

            @pl.when(r_to != r)
            def _():
                spread(piece, r_to).wait_send()

        @pl.when(has)
        def _():
            for m in range(chans):

                @pl.when(m != c)
                def _():
                    lift(m).wait_send()

    rows, width = tokens.shape
    part = out_full.shape[-1]
    tile = rows // 3
    per_tile = held // 3
    size = rows // held - HEAD
    tiles = [pl.ds(at * tile, tile) for at in range(3)]

    def mix_loads(j):
        slot = lax.rem(j, 2)
        return [
            pltpu.make_async_copy(in_full.at[j], in_v.at[slot], mix_sem.at[slot, 0]),
            pltpu.make_async_copy(out_full.at[j], out_v.at[slot], mix_sem.at[slot, 1]),
        ]

    def stream_out(j):
        return pltpu.make_async_copy(stream, streams.at[j], stream_sem)

    local_rows = token_source.shape[1]
    before_at = pl.multiple_of(lax.rem(c + chans - 1, chans) * size + size - HEAD, HEAD)
    after_at = pl.multiple_of(lax.rem(c + 1, chans) * size, HEAD)
    halos = [
        (token_source, before_at, c == 0, r > 0, r < seqs - 1, 1),
        (token_source, after_at, c == chans - 1, r < seqs - 1, r > 0, -1),
        (cotangent_source, after_at, c == chans - 1, r < seqs - 1, r > 0, -1),
    ]

    def row_copies():
        return [
            pltpu.make_async_copy(
                source.at[s, pl.ds(pl.multiple_of(c * size, size), size)],
                rows_to.at[pl.ds(s * (size + HEAD) + HEAD, size)],
                row_sem.at[n, s],
            )
            for n, (source, rows_to) in enumerate(
                ((token_source, tokens), (cotangent_source, cotangent))
            )
            for s in range(held)
        ]

    def halo_local(n):
        source, at, _, _, _, _ = halos[n]
        return pltpu.make_async_copy(source.at[:, pl.ds(at, HEAD)], halo.at[n], halo_sem.at[n])

    def halo_remote(n):
        source, at, _, _, _, step = halos[n]
        return remote(
            source.at[:, pl.ds(at, HEAD)], halo.at[n], halo_send.at[n], halo_recv.at[n], seq=r + step
        )

    def rows_start():
        for copy in row_copies():
            copy.start()
        for n, (_, _, edge, takes, gives, _) in enumerate(halos):

            @pl.when(jnp.logical_not(edge))
            def _():
                halo_local(n).start()

            @pl.when(edge & gives)
            def _():
                halo_remote(n).start()

            @pl.when(edge & jnp.logical_not(takes))
            def _():
                halo[n] = jnp.zeros(halo.shape[1:], F32)

    def rows_finish():
        for copy in row_copies():
            copy.wait()
        for n, (_, _, edge, takes, gives, _) in enumerate(halos):

            @pl.when(jnp.logical_not(edge))
            def _():
                halo_local(n).wait()

            @pl.when(edge & takes)
            def _():
                halo_remote(n).wait_recv()

            @pl.when(edge & gives)
            def _():
                halo_remote(n).wait_send()

        row = lax.broadcasted_iota(jnp.int32, (HEAD, width), 0)
        for s in range(held):
            head = pl.ds(s * (size + HEAD), HEAD)
            earlier = (s - 1) % held
            tokens[head] = jnp.where(row < 2, halo[1, earlier], halo[0, s])
            cotangent[head] = jnp.where(row < 2, halo[2, earlier], 0.0)
        for at, here in enumerate(tiles):
            values = cotangent[here]
            u[here] = values.astype(BF16)
            for s, one in enumerate(own_rows(values, per_tile)):
                u_own[pl.ds((at * per_tile + s) * size, size)] = one.astype(BF16)

    def mix_prepare():
        rows_finish()
        for here in tiles:
            values = tokens[here]
            normed[here] = (values * row_scale(values) * gains[0:1]).astype(BF16)
            residual[here] = values

    def transfers(tick):
        @pl.when(tick + 2 <= last)
        def _():
            start_chan(tick + 2)

        @pl.when(tick <= last)
        def _():
            first_level(tick)

        for level in range(1, bits - 1):

            @pl.when(tick - level <= last)
            def _():
                next_level(tick - level, level)

        @pl.when(tick - bits + 1 <= last)
        def _():
            to_core(tick - bits + 1)

        @pl.when(tick - bits <= last)
        def _():
            arrived(tick - bits)
            for copy in loads(tick - bits - 2):
                copy.start()

    def mix():
        for copy in mix_loads(0):
            copy.start()
        copy = pltpu.make_async_copy(taps_all, taps_v, taps_sem)
        copy.start()
        copy.wait()

        @pl.loop(0, chans)
        def _(j):
            slot = lax.rem(j, 2)
            for copy in mix_loads(j):
                copy.wait()

            @pl.when(j + 1 < chans)
            def _():
                for copy in mix_loads(j + 1):
                    copy.start()

            @pl.when(j > 0)
            def _():
                stream_out(j - 1).wait()

            in_w = in_v[slot].reshape(width, 3 * part)
            out_w = out_v[slot].reshape(width, part)
            for here in tiles:
                stream[here] = dot(normed[here], in_w)
            filters = taps_v[j]
            gated = stream[:, 0:part] * stream[:, 2 * part :]
            filtered = filtering(gated, filters, keeps[:, 0:1], keeps[:, 1:2])
            mixed[...] = (stream[:, part : 2 * part] * filtered).astype(BF16)
            stream_out(j).start()
            for here in tiles:
                residual[here] += contract_last(mixed[here], out_w)

            @pl.when(j == 1)
            def _():
                transfers(bits + 2)

        for at, here in enumerate(tiles):
            values = residual[here]
            new = values * row_scale(values) * gains[1:2]
            x[here] = new.astype(BF16)
            for s, one in enumerate(own_rows(new, per_tile)):
                x_own[pl.ds((at * per_tile + s) * size, size)] = one.astype(BF16)
            ffn_out[here] = jnp.zeros((tile, width), F32)
            second_grad[here] = jnp.zeros((tile, width), F32)
        stream_out(chans - 1).wait()

    def loads(t):
        slot = lax.rem(t, 2)
        return [
            pltpu.make_async_copy(
                ffn_full.at[t, j, :, m],
                w_v.at[slot, m, :, :, pl.ds(j * LANES, LANES)],
                load_sem.at[slot, m, j],
            )
            for m in range(3)
            for j in range(chans)
        ]

    def grads_out(t):
        slot = lax.rem(t, 2)
        return [
            pltpu.make_async_copy(grad_v.at[slot, m], ffn_g.at[m, :, t], grad_sem.at[slot, m])
            for m in range(3)
        ]

    def feed_forward(t):
        slot = lax.rem(t, 2)
        for copy in loads(t):
            copy.wait()

        @pl.when(t >= 2)
        def _():
            for copy in grads_out(t - 2):
                copy.wait()

        wg, wu, wd = (w_v[slot, m].reshape(width, chans * LANES) for m in range(3))
        for at, here in enumerate(tiles):
            gate = dot(x[here], wg)
            up = dot(x[here], wu)
            grad = dot(u[here], wd)
            sigmoid = jax.nn.sigmoid(gate)
            silu = gate * sigmoid
            new_act = silu * up
            new_gate = grad * up * sigmoid * (1.0 + gate * (1.0 - sigmoid))
            new_up = grad * silu
            for ref, values in ((act, new_act), (gate_low, new_gate), (up_low, new_up)):
                for s, one in enumerate(own_rows(values, per_tile)):
                    ref[pl.ds((at * per_tile + s) * size, size)] = one.astype(BF16)
            ffn_out[here] += contract_last(new_act.astype(BF16), wd)
            second_grad[here] += contract_last(new_gate.astype(BF16), wg) + contract_last(
                new_up.astype(BF16), wu
            )
        for m, (low, right) in enumerate(((gate_low, x_own), (up_low, x_own), (act, u_own))):
            grad_v[slot, m] = (
                contract_first(low[...], right[...]).astype(BF16).reshape(PIECES, UNIT, width)
            )
        for copy in grads_out(t):
            copy.start()

    def shelf_copies(group, n):
        slot = n % 2
        if n % 4 == 0:
            part_of = [(group[0].at[k], k) for k in range(3)] + [(group[1], 3)]
            return [
                pltpu.make_async_copy(
                    source, shelf.at[slot, :, pl.ds(k * part, part)], shelf_sem.at[slot, k]
                )
                for source, k in part_of
            ]
        return [pltpu.make_async_copy(group[n % 4 + 1], shelf.at[slot], shelf_sem.at[slot, 0])]

    def shelves(n):
        return shelf_copies(weights if n < 4 else moments, n)

    for copy in shelves(0):
        copy.start()
    taps[...] = jnp.zeros_like(taps)
    taps[0:3] = own_taps[...]
    rows_start()
    for n in range(8):
        if n < 7:
            for copy in shelves(n + 1):
                copy.start()
        for copy in shelves(n):
            copy.wait()
        slot, m = n % 2, n % 4 - 1
        if n == 0:
            in_shard[...] = shelf[slot, :, : 3 * part].astype(BF16)
            out_shard[...] = shelf[slot, :, 3 * part : 4 * part].astype(BF16)
            start_chan(0)
            start_chan(1)
        elif n < 4:
            for t in range(TILES):
                ffn_shard[t, m] = shelf[slot, :, t * LANES : (t + 1) * LANES].astype(BF16)
        elif n == 4:
            packed[3] = jnp.zeros(packed.shape[1:], BF16)
            for q in range(PER_CHAN):
                block = shelf[slot, :, q * SMALL_PIECE : (q + 1) * SMALL_PIECE]
                packed[3, q, 0:SMALL_PIECE] = block.T.astype(BF16)
        else:
            for t in range(TILES):
                block = shelf[slot, :, t * LANES : (t + 1) * LANES].T.astype(BF16)
                packed[m, :, t * UNIT : (t + 1) * UNIT] = block.reshape(PER_CHAN, UNIT, -1)
    taps_own = pltpu.make_async_copy(taps, taps_all.at[c], t_own)
    taps_own.start()
    for off in range(1, chans):
        taps_copy(off, False).start()
    mix_prepare()

    for tick in range(bits + 2):
        start_chan(tick + 2)
        first_level(tick)
        for level in range(1, bits - 1):
            if tick >= level:
                next_level(tick - level, level)
        if tick >= bits - 1:
            to_core(tick - bits + 1)
        if tick >= bits:
            arrived(tick - bits)
    taps_own.wait()
    for off in range(1, chans):
        taps_copy(off, True).wait_recv()
    mix()

    @pl.loop(bits + 3, last + bits + 2)
    def _(tick):
        transfers(tick)

        @pl.when(tick == last)
        def _():
            pieces_start()

        @pl.when(tick == last + 2)
        def _():
            pieces_lift()

        feed_forward(tick - bits - 3)

    for s in range(held):
        here = pl.ds(s * (size + HEAD) + HEAD, size)
        block_out[pl.ds(s * size, size)] = (residual[here] + ffn_out[here]).astype(BF16)
    for t in (TILES - 2, TILES - 1):
        for copy in grads_out(t):
            copy.wait()
    pieces_finish()
    for off in range(1, chans):
        taps_copy(off, False).wait_send()
    sent(0)
    sent(1)

    @pl.loop(2, last + 1)
    def _(k):
        sent(k)


def forward_pass(seqs, chans, weights, moments, taps, tokens, cotangent, keeps, gains):
    held, local_rows, width = tokens.shape
    block, part = weights[1].shape
    own_count, hidden = held * local_rows // chans, chans * LANES
    rows = own_count + held * HEAD
    tail = (PIECE, block)
    shape = jax.ShapeDtypeStruct
    outs = [
        shape((chans, seqs, block, 3 * part), BF16),
        shape((chans, seqs, block, part), BF16),
        shape((TILES, chans, seqs, 3, block, LANES), BF16),
        shape((chans, 8, part), F32),
        shape((PIECES // seqs, seqs) + tail, BF16),
        shape((chans, seqs) + tail, BF16),
        shape((chans, rows, 3 * part), F32),
    ]
    outs.append(shape((3, PIECES, TILES, UNIT, width), BF16))
    outs += [shape((rows, width), F32)] * 4 + [shape((own_count, width), BF16)]
    dma = pltpu.SemaphoreType.DMA
    count = TILES + 2
    vmem = pltpu.VMEM
    found = call(
        functools.partial(forward_kernel, seqs, chans, held),
        outs,
        [pl.ANY] * 10 + [vmem] + [pl.ANY] * 2 + [vmem] * 2,
        [pl.ANY] * 8 + [vmem] * 5,
        [
            vmem((block, 3 * part), BF16),
            vmem((block, part), BF16),
            vmem((TILES, 3, block, LANES), BF16),
            vmem((8, part), F32),
            vmem((chans, PER_CHAN) + tail, BF16),
            vmem((2, block, TILES * LANES), F32),
            dma((2, 4)),
            vmem((rows, width), BF16),
            vmem((own_count, width), BF16),
            vmem((3, held, HEAD, width), F32),
            dma((2, held)),
            dma((3,)),
            dma((3,)),
            dma((3,)),
            vmem((rows, width), BF16),
            vmem((rows, part), BF16),
            vmem((rows, 3 * part), F32),
            vmem((rows, width), BF16),
            vmem((own_count, width), BF16),
            vmem((rows, width), F32),
            vmem((own_count, hidden), BF16),
            vmem((own_count, hidden), BF16),
            vmem((own_count, hidden), BF16),
            vmem((2, seqs, block, 3 * part), BF16),
            vmem((2, seqs, block, part), BF16),
            vmem((chans, 8, part), F32),
            vmem((2, 3, seqs, block, hidden), BF16),
            vmem((2, 3, PIECES, UNIT, width), BF16),
            dma((count,)),
            dma((count, chans - 1)),
            dma((count, chans - 1)),
            dma((count, 2, seqs // 2 - 1)),
            dma((count, 2, seqs // 2 - 1)),
            dma((count, seqs // 2)),
            dma((count, seqs // 2)),
            dma(()),
            dma((chans - 1,)),
            dma((chans - 1,)),
            dma((2,)),
            dma((PER_CHAN,)),
            dma((seqs,)),
            dma((chans,)),
            dma((PIECES // seqs,)),
            dma((2, 2)),
            dma(()),
            dma(()),
            dma((2, 3, chans)),
            dma((2, 3)),
        ],
        0,
        *weights, *moments, taps, tokens, cotangent, keeps, gains,
        vmem=62,
    )
    return found


LAG = 2


def add_rows(acc, other):
    return (acc.astype(F32) + other.astype(F32)).astype(BF16)


def backward_kernel(
    seqs, chans, held,
    ffn_g, in_full, out_full, streams, block_own,
    tokens, residual, second_grad, cotangent, keeps, gains, taps,
    result, total, input_grad, io_g, blocks, input_blocks, *refs
):
    bits = seqs.bit_length() - 1
    levels = bits - 1
    landed, line_land = refs[: levels + 1], refs[levels + 1]
    temps, refs = refs[levels + 2 : 2 * levels + 3], refs[2 * levels + 3 :]
    (
        acc, line_temp, sent, got, sums,
        residual_low, low_own, first_own, residual_grad, stream_own, mixed_own, mixer_grad, first_grad,
        stream, in_v, out_v, staging,
        load_sem, temp_sem, fetch_sem, c_send, c_recv, b_send, b_recv, z_send, z_recv, n_send, n_recv,
        mix_sem, io_sem, *relay_sems
    ) = refs
    parts, half_seqs = PIECES // seqs, seqs // 2
    chunks = chans * parts
    slots, group = acc.shape[0], temps[0].shape[0]
    at_once = group == half_seqs
    r, c = lax.axis_index("seq"), lax.axis_index("chan")
    core, h = lax.rem(r, 2), lax.div(r, 2)
    partners = [{"seq": flip(r, bit)} for bit in range(bits)]
    greet(partners + [{"chan": lax.rem(c + off, chans)} for off in range(1, chans)])
    partners += [{"chan": flip(c, bit)} for bit in range(chans.bit_length() - 1)]

    def slot_of(k):
        return lax.rem(k, slots)

    def core_copy(k, source):
        return remote(source.at[:, 1 - core], landed[0].at[k], c_send.at[k], c_recv.at[k], seq=flip(r, 0))

    def load(k, source):
        return pltpu.make_async_copy(source.at[:, core], acc.at[slot_of(k)], load_sem.at[k])

    def with_source(k, work):
        @pl.when(k < 3 * parts)
        def _():
            work(ffn_g.at[lax.div(k, parts), lax.rem(k, parts)])

        @pl.when(k >= 3 * parts)
        def _():
            work(io_g.at[k - 3 * parts])

    def lanes(half):
        return pl.ds(half * (D // 2), D // 2)

    def across(k, half, level):
        order = high_bits(bits, half)
        bit, rest = order[level], [one - 1 for one in order[level + 1 :]]
        base = h
        for one in rest:
            base = base - (1 << one) * lax.rem(lax.div(h, 1 << one), 2)
        first = half_seqs - (half_seqs >> level)
        copies, keeps = [], []
        for at in range(1 << len(rest)):
            place = base + sum((1 << one) for n, one in enumerate(rest) if at >> n & 1)
            copies.append(
                remote(
                    acc.at[slot_of(k), flip(place, bit - 1), :, lanes(half)],
                    landed[level + 1].at[k, at, :, lanes(half)],
                    b_send.at[k, half, first + at], b_recv.at[k, half, first + at],
                    seq=flip(r, bit),
                )
            )
            keeps.append(place)
        return copies, keeps

    def fetch(src, dst):
        copy = pltpu.make_async_copy(src, dst, temp_sem)
        copy.start()
        copy.wait()

    def begin(k):
        def work(source):
            core_copy(k, source).start()
            load(k, source).start()

        with_source(k, work)

    def level_start(k, level):
        for half in range(2):
            for copy in across(k, half, level)[0]:
                copy.start()

    def fetch_level(k, level):
        return pltpu.make_async_copy(landed[level].at[k], temps[level], fetch_sem.at[level])

    def core_arrive(k):
        load(k, io_g.at[0]).wait()
        core_copy(k, io_g.at[0]).wait_recv()
        if at_once:
            fetch_level(k, 0).start()

    def core_sum(k):
        if at_once:
            fetch_level(k, 0).wait()
        for start in range(0, half_seqs, group):
            if not at_once:
                fetch(landed[0].at[k, pl.ds(start, group)], temps[0])

            @pl.loop(0, group)
            def _(b):
                acc[slot_of(k), start + b] = add_rows(acc[slot_of(k), start + b], temps[0][b])

        level_start(k, 0)

    def level_arrive(k, level):
        for half in range(2):
            for copy in across(k, half, level)[0]:
                copy.wait_recv()
        if at_once:
            fetch_level(k, level + 1).start()

    def level_sum(k, level):
        both = [across(k, half, level) for half in range(2)]
        if at_once:
            fetch_level(k, level + 1).wait()
        temp = temps[level + 1 if at_once else 0]
        count = half_seqs >> (level + 1)
        for start in range(0, count, group):
            here = min(group, count - start)
            if not at_once:
                fetch(landed[level + 1].at[k, pl.ds(start, here)], temp.at[pl.ds(0, here)])
            for half in range(2):
                for at in range(here):
                    place = both[half][1][start + at]
                    acc[slot_of(k), place, :, lanes(half)] = add_rows(
                        acc[slot_of(k), place, :, lanes(half)], temp[at, :, lanes(half)]
                    )
        if level + 1 < levels:
            level_start(k, level + 1)

    def line(k, side):
        return remote(
            acc.at[slot_of(k), h], line_land.at[side, k], z_send.at[k], z_recv.at[side, k],
            chan=c + 1 - 2 * side,
        )

    def hop(k, step):
        keeper = lax.div(k, parts)
        for side, sends in ((0, (c < keeper) & (c == step)), (1, (c > keeper) & (chans - 1 - c == step))):

            @pl.when(sends)
            def _():
                if step > 0:
                    line(k, side).wait_recv()
                    fetch(line_land.at[side, k], line_temp.at[0])
                    acc[slot_of(k), h] = add_rows(acc[slot_of(k), h], line_temp[0])
                line(k, side).start()

    def finish(k):
        keeper = lax.div(k, parts)

        @pl.when(c == keeper)
        def _():
            for side, there in ((0, c > 0), (1, c < chans - 1)):

                @pl.when(there)
                def _():
                    line(k, side).wait_recv()
                    fetch(line_land.at[side, k], line_temp.at[side])

                @pl.when(jnp.logical_not(there))
                def _():
                    line_temp[side] = jnp.zeros(line_temp.shape[1:], BF16)

            result[lax.rem(k, parts)] = (
                acc[slot_of(k), h].astype(F32) + line_temp[0].astype(F32) + line_temp[1].astype(F32)
            ).astype(BF16)

        @pl.when(c < keeper)
        def _():
            line(k, 0).wait_send()

        @pl.when(c > keeper)
        def _():
            line(k, 1).wait_send()

        core_copy(k, io_g.at[0]).wait_send()
        for level in range(levels):
            for half in range(2):
                for copy in across(k, half, level)[0]:
                    copy.wait_send()

    def small_copy(level):
        return remote(
            sent.at[level], got.at[level], n_send.at[level], n_recv.at[level], **partners[level]
        )

    def small_step(level):
        if level == 0:
            sent[0] = sums[...]
        else:
            small_copy(level - 1).wait()
            new = sent[level - 1] + got[level - 1]
            if level == len(partners):
                total[...] = new
            else:
                sent[level] = new
        if level < len(partners):
            small_copy(level).start()

    rows, full = tokens.shape
    width = out_v.shape[-1]
    length = rows // held
    size = length - HEAD
    tile, per_tile = rows // 3, held // 3
    tiles = [pl.ds(at * tile, tile) for at in range(3)]
    own_tiles = [pl.ds(at * per_tile * size, per_tile * size) for at in range(3)]

    def mix_loads(j):
        return [
            pltpu.make_async_copy(in_full.at[j], in_v, mix_sem.at[0]),
            pltpu.make_async_copy(out_full.at[j], out_v, mix_sem.at[1]),
            pltpu.make_async_copy(streams.at[j], stream, mix_sem.at[2]),
        ]

    def io_out(j):
        at, first = lax.div(4 * j, half_seqs), lax.rem(4 * j, half_seqs)
        return pltpu.make_async_copy(staging, io_g.at[at, pl.ds(first, 4)], io_sem)

    def mix_prepare():
        gain_sum = jnp.zeros((1, full), F32)
        for at, here in enumerate(tiles):
            values = residual[here]
            scale = row_scale(values)
            unit = values * scale
            grad = second_grad[here]
            scaled = grad * gains[1:2]
            new = cotangent[here] + scale * (
                scaled - unit * jnp.mean(scaled * unit, axis=1, keepdims=True)
            )
            residual_low[here] = new.astype(BF16)
            for s, (one, two) in enumerate(
                zip(own_rows(new, per_tile), own_rows(grad * unit, per_tile))
            ):
                where = pl.ds((at * per_tile + s) * size, size)
                residual_grad[where] = one
                low_own[where] = one.astype(BF16)
                gain_sum += jnp.sum(two, axis=0, keepdims=True)
            first = tokens[here]
            first = first * row_scale(first) * gains[0:1]
            for s, one in enumerate(own_rows(first, per_tile)):
                first_own[pl.ds((at * per_tile + s) * size, size)] = one.astype(BF16)
        sums[...] = jnp.zeros_like(sums)
        sums[1:2] = gain_sum
        first_grad[...] = jnp.zeros_like(first_grad)
        staging[...] = jnp.zeros_like(staging)

    def mix_step(j):
        for copy in mix_loads(j):
            copy.wait()
        in_w, out_w = in_v[...].reshape(full, 3 * width), out_v[...].reshape(full, width)
        filters = taps[j]
        for here in tiles:
            mixer_grad[here] = dot(residual_low[here], out_w)
        input_gate, output_gate, value = (
            stream[:, k * width : (k + 1) * width] for k in range(3)
        )
        keep_one, keep_two = keeps[:, 0:1], keeps[:, 1:2]
        gated = input_gate * value
        back_one, back_two = pltpu.roll(gated, 1, 0), pltpu.roll(gated, 2, 0)
        filtered = (
            filters[2:3] * gated
            + filters[1:2] * keep_one * back_one
            + filters[0:1] * keep_two * back_two
        )
        grad = mixer_grad[...]
        inner = grad * output_gate
        one, two = keep_one * inner, keep_two * inner
        gated_grad = (
            filters[2:3] * inner
            + filters[1:2] * pltpu.roll(one, rows - 1, 0)
            + filters[0:1] * pltpu.roll(two, rows - 2, 0)
        )

        def own_sum(values):
            return sum(jnp.sum(part, axis=0, keepdims=True) for part in own_rows(values, held))

        where = pl.ds(pl.multiple_of(j * width, width), width)
        sums[4:5, where] = own_sum(inner * gated)
        sums[3:4, where] = own_sum(one * back_one)
        sums[2:3, where] = own_sum(two * back_two)
        for k, values in enumerate((gated_grad * value, grad * filtered, gated_grad * input_gate)):
            for s, part in enumerate(own_rows(values, held)):
                stream_own[pl.ds(s * size, size), k * width : (k + 1) * width] = part.astype(BF16)
        for s, part in enumerate(own_rows(output_gate * filtered, held)):
            mixed_own[pl.ds(s * size, size)] = part.astype(BF16)
        for here in own_tiles:
            first_grad[here] += contract_last(stream_own[here], in_w)

        @pl.when(j > 0)
        def _():
            io_out(j - 1).wait()

        for k in range(4):
            if k < 3:
                new = contract_first(stream_own[:, k * width : (k + 1) * width], first_own[...])
            else:
                new = contract_first(mixed_own[...], low_own[...])
            staging[k, :, pl.ds(0, SMALL_PIECE)] = new.astype(BF16).reshape(2, SMALL_PIECE, full)
        io_out(j).start()

        @pl.when(j + 1 < chans)
        def _():
            for copy in mix_loads(j + 1):
                copy.start()

    def mix_end():
        gain_sum = jnp.zeros((1, full), F32)
        for s in range(held):
            here = pl.ds(s * size, size)
            values = tokens[pl.ds(s * length + HEAD, size)]
            scale = row_scale(values)
            unit = values * scale
            grad = first_grad[here]
            scaled = grad * gains[0:1]
            gain_sum += jnp.sum(grad * unit, axis=0, keepdims=True)
            input_grad[here] = (
                residual_grad[here]
                + scale * (scaled - unit * jnp.mean(scaled * unit, axis=1, keepdims=True))
            ).astype(BF16)
        sums[0:1] = gain_sum
        io_out(chans - 1).wait()

    spread_out = parts == 4
    mix_first, mix_last = (1, 3 * parts - 2) if spread_out else (-1, -1)
    relay = Relay(chans, block_own, blocks, relay_sems[:3])
    input_relay = Relay(chans, input_grad, input_blocks, relay_sems[3:])
    for copy in mix_loads(0):
        copy.start()
    begin(0)
    relay.step(0)
    mix_prepare()
    if not spread_out:

        @pl.loop(0, chans)
        def _(j):
            mix_step(j)

        mix_end()

    summed = LAG * (1 + levels)

    @pl.loop(1, chunks + summed + LAG * (chans - 1))
    def _(tick):
        def stage(k, work):
            @pl.when((k >= 0) & (k < chunks))
            def _():
                work(k)

        stage(tick - summed - LAG * (chans - 1), finish)
        stage(tick, begin)
        for step in range(chans - 2, 0, -1):
            stage(tick - summed - LAG * step, lambda k: hop(k, step))
        for level in range(levels - 1, -1, -1):
            stage(tick - LAG * (2 + level), lambda k: level_arrive(k, level))
        stage(tick - LAG, core_arrive)
        for level in range(levels - 1, -1, -1):

            def work(k):
                level_sum(k, level)
                if level == levels - 1:
                    hop(k, 0)

            stage(tick - LAG * (2 + level), work)
        stage(tick - LAG, core_sum)
        if spread_out:

            @pl.when((tick >= mix_first) & (tick < mix_first + 2 * chans) & (lax.rem(tick - mix_first, 2) == 0))
            def _():
                mix_step(lax.div(tick - mix_first, 2))

            @pl.when(tick == mix_last)
            def _():
                mix_end()

        for level in range(len(partners) + 1):

            @pl.when(tick == mix_last + 2 + level)
            def _():
                small_step(level)

        for step in (1, 2):

            @pl.when(tick == 7 * step)
            def _():
                relay.step(step)

        @pl.when(tick == mix_last + 6)
        def _():
            input_relay.step(0)

    relay.finish(range(chans - 1))
    input_relay.finish([0])


def backward_pass(
    seqs, chans, held, ffn_g, in_full, out_full, streams, block_own, tokens, residual, second_grad,
    cotangent, keeps, gains, taps,
):
    dma, vmem, shape = pltpu.SemaphoreType.DMA, pltpu.VMEM, jax.ShapeDtypeStruct
    parts, half_seqs = PIECES // seqs, seqs // 2
    levels = seqs.bit_length() - 2
    chunks = chans * parts
    slots = min(chunks, LAG * (levels + chans) + 1)
    group = min(4, half_seqs)
    sizes = [group] + [half_seqs >> level if group == half_seqs else 1 for level in range(1, levels + 1)]
    partners = (seqs * chans).bit_length() - 1
    rows, width = tokens.shape
    own_count = rows - held * HEAD
    part = out_full.shape[-1]
    outs = [
        shape((parts, PIECE, D), BF16),
        shape((8, width), F32),
        shape((own_count, width), BF16),
        shape((parts, half_seqs, 2, PIECE, D), BF16),
        shape((chans,) + block_own.shape, BF16),
        shape((chans,) + block_own.shape, BF16),
        shape((chunks, half_seqs, PIECE, D), BF16),
    ]
    outs += [
        shape((chunks, half_seqs >> (level + 1), PIECE, D), BF16) for level in range(levels)
    ]
    outs.append(shape((2, chunks, PIECE, D), BF16))
    return call(
        functools.partial(backward_kernel, seqs, chans, held),
        outs,
        [pl.ANY] * 5 + [vmem] * 7,
        [vmem] * 3 + [pl.ANY] * (len(outs) - 3),
        [
            *[vmem((size, PIECE, D), BF16) for size in sizes],
            vmem((slots, half_seqs, PIECE, D), BF16),
            vmem((2, PIECE, D), BF16),
            vmem((partners, 8, width), F32),
            vmem((partners, 8, width), F32),
            vmem((8, width), F32),
            vmem((rows, width), BF16),
            vmem((own_count, width), BF16),
            vmem((own_count, width), BF16),
            vmem((own_count, width), F32),
            vmem((own_count, 3 * part), BF16),
            vmem((own_count, part), BF16),
            vmem((rows, part), F32),
            vmem((own_count, width), F32),
            vmem((rows, 3 * part), F32),
            vmem(in_full.shape[1:], BF16),
            vmem(out_full.shape[1:], BF16),
            vmem((4, 2, PIECE, D), BF16),
            dma((chunks,)),
            dma(()),
            dma((levels + 1,)),
            dma((chunks,)),
            dma((chunks,)),
            dma((chunks, 2, half_seqs)),
            dma((chunks, 2, half_seqs)),
            dma((chunks,)),
            dma((2, chunks)),
            dma((partners,)),
            dma((partners,)),
            dma((3,)),
            dma(()),
            *Relay.semaphores(chans),
            *Relay.semaphores(chans),
        ],
        1,
        ffn_g.reshape(3, parts, half_seqs, 2, PIECE, D),
        in_full, out_full, streams, block_own, tokens, residual, second_grad, cotangent, keeps, gains,
        taps,
        vmem=62,
    )[:6]


def shifted(value, axes, by):
    length = lax.axis_size(axes)
    pairs = [(i, i + by) for i in range(length) if 0 <= i + by < length]
    return lax.ppermute(value, axes, pairs)


def adam_update(param, gradient, first, second):
    first_new = FIRST_DECAY * first + (1.0 - FIRST_DECAY) * gradient
    second_new = SECOND_DECAY * second + (1.0 - SECOND_DECAY) * gradient * gradient
    first_fix = 1.0 - FIRST_DECAY**STEP
    second_fix = 1.0 - SECOND_DECAY**STEP
    param_new = param - ADAM_RATE * (first_new / first_fix) / (
        jnp.sqrt(second_new / second_fix) + ADAM_EPS
    )
    return (param_new, first_new, second_new)


COLUMNS = [3 * D, D, FF, FF, FF]
RATES = [1.0, 1.0, 1.0, 1.0, 0.5]


def last_kernel(block_low, input_low, grad_home, ortho_home, *refs):
    weights, moments, (block_out, input_grad) = refs[:5], refs[5:10], refs[10:12]
    moments_new, weights_new = refs[12:22:2], refs[13:22:2]
    step = pl.program_id(0)
    for low, whole in ((block_low, block_out), (input_low, input_grad)):
        rows = low.shape[2]
        for at in range(low.shape[0]):
            whole[0, at * rows : (at + 1) * rows] = low[at, 0].astype(F32)

    def update(index, at, lanes, grad, ortho):
        rate = RATES[index]
        here = at + (slice(None), lanes)
        moments_new[index][here] = MOMENTUM_DECAY * moments[index][here] + grad.astype(F32).T
        weights_new[index][here] = (
            weights[index][here] * (1.0 - WEIGHT_DECAY * rate)
            - rate * math.sqrt(COLUMNS[index] / D) * ortho.astype(F32).T
        )

    for m in range(3):

        @pl.when(step == m)
        def _():
            for t in range(TILES):
                rows = slice(t * UNIT, (t + 1) * UNIT)
                update(
                    m + 2, (), slice(t * LANES, (t + 1) * LANES),
                    *(home[m, :, rows].reshape(LANES, -1) for home in (grad_home, ortho_home)),
                )

    @pl.when(step == 3)
    def _():
        for q in range(PER_CHAN):
            lanes = slice(q % 2 * SMALL_PIECE, (q % 2 + 1) * SMALL_PIECE)
            blocks = [home[3, q, 0:SMALL_PIECE] for home in (grad_home, ortho_home)]
            update(*((0, (q // 2,)) if q < IN_PIECES else (1, ())), lanes, *blocks)


def last_pass(block_low, input_low, homes, weights, moments):
    chans, held, sub, width = block_low.shape
    low = pl.BlockSpec((chans, 1, sub, width), lambda s: (0, s, 0, 0))
    whole = pl.BlockSpec((1, chans * sub, width), lambda s: (s, 0, 0))

    def all_of(array):
        return pl.BlockSpec(array.shape, lambda s: (0,) * array.ndim)

    shape = jax.ShapeDtypeStruct
    outs = [shape((held, chans * sub, width), F32)] * 2
    out_specs = [whole] * 2
    for weight in weights:
        outs += [shape(weight.shape, F32)] * 2
        out_specs += [all_of(weight)] * 2
    return pl.pallas_call(
        last_kernel,
        grid=(held,),
        out_shape=outs,
        in_specs=[low] * 2 + [all_of(one) for one in (*homes, *weights, *moments)],
        out_specs=out_specs,
        compiler_params=pltpu.CompilerParams(vmem_limit_bytes=60 * 1024 * 1024),
    )(block_low, input_low, *homes, *weights, *moments)


def on_device(
    tokens,
    segment_ids,
    cotangent,
    norm_gains,
    filter_weight,
    in_weight,
    out_weight,
    gate_weight,
    up_weight,
    down_weight,
    norm_gains_mean,
    norm_gains_square,
    filter_mean,
    filter_square,
    in_momentum,
    out_momentum,
    gate_momentum,
    up_momentum,
    down_momentum,
):
    seqs, chans = lax.axis_size("seq"), lax.axis_size("chan")
    r, c = lax.axis_index("seq"), lax.axis_index("chan")
    seq_total, local_rows, width = tokens.shape
    sub = local_rows // chans
    chan_width = filter_weight.shape[1]

    weights = [in_weight.transpose(1, 0, 2), out_weight, gate_weight, up_weight, down_weight]
    moments = [
        in_momentum.transpose(1, 0, 2), out_momentum, gate_momentum, up_momentum, down_momentum
    ]

    def share(array, start, length):
        return lax.dynamic_slice_in_dim(array, start, length, axis=1)

    positions = r * local_rows + jnp.arange(local_rows, dtype=jnp.int32)
    local_keeps = jnp.stack(
        [(segment_ids <= positions[None, :] - offset).astype(F32) for offset in (1, 2)], axis=-1
    )
    following = jnp.where(
        c == chans - 1,
        shifted(local_keeps[:, :2], "seq", -1),
        share(local_keeps, lax.rem(c + 1, chans) * sub, 2),
    )
    following = jnp.concatenate([following[-1:], following[:-1]])
    gap = jnp.zeros((seq_total, HEAD - 2, 2), F32)
    keeps = jnp.concatenate([following, gap, share(local_keeps, c * sub, sub)], axis=1).reshape(-1, 2)

    (
        in_full, out_full, _, taps, moments_held, _, streams, ffn_grads,
        token_rows, upstream_rows, residual, second_grad, block_out,
    ) = forward_pass(
        seqs, chans, weights, moments, filter_weight, tokens, cotangent, keeps, norm_gains
    )
    moments_held = moments_held.transpose(0, 2, 1, 3).reshape(-1, D)
    grads_held, small, _, _, block_out, input_grad = backward_pass(
        seqs, chans, seq_total, ffn_grads, in_full, out_full, streams, block_out, token_rows, residual,
        second_grad, upstream_rows, keeps, norm_gains, taps,
    )

    gains_new, gains_mean_new, gains_square_new = adam_update(
        norm_gains, small[:2], norm_gains_mean, norm_gains_square
    )
    filter_new, filter_mean_new, filter_square_new = adam_update(
        filter_weight, share(small[2:5], c * chan_width, chan_width), filter_mean, filter_square
    )

    *homes, input_grad = orthogonalize(
        seqs, chans, grads_held.reshape(-1, D), moments_held, input_grad
    )
    block_out, input_grad = (
        one.reshape(chans, seq_total, sub, width) for one in (block_out, input_grad)
    )
    block_out, input_grad, *results = last_pass(block_out, input_grad, homes, weights, moments)
    results[:2] = [one.transpose(1, 0, 2) for one in results[:2]]
    return (
        block_out,
        input_grad,
        gains_new,
        gains_mean_new,
        gains_square_new,
        filter_new,
        filter_mean_new,
        filter_square_new,
        *results,
    )


def solution(mesh):
    return jax.shard_map(
        on_device,
        mesh=mesh,
        in_specs=(
            P(None, "seq", None),
            P(None, "seq"),
            P(None, "seq", None),
            P(),
            P(None, "chan"),
            P("seq", None, "chan"),
            P("seq", "chan"),
            P("seq", "chan"),
            P("seq", "chan"),
            P("seq", "chan"),
            P(),
            P(),
            P(None, "chan"),
            P(None, "chan"),
            P("seq", None, "chan"),
            P("seq", "chan"),
            P("seq", "chan"),
            P("seq", "chan"),
            P("seq", "chan"),
        ),
        out_specs=(
            P(None, "seq", None),
            P(None, "seq", None),
            P(),
            P(),
            P(),
            P(None, "chan"),
            P(None, "chan"),
            P(None, "chan"),
            P("seq", None, "chan"),
            P("seq", None, "chan"),
            P("seq", "chan"),
            P("seq", "chan"),
            P("seq", "chan"),
            P("seq", "chan"),
            P("seq", "chan"),
            P("seq", "chan"),
            P("seq", "chan"),
            P("seq", "chan"),
        ),
        check_vma=False,
    )
```

```python
import functools
import math

import jax
import jax.numpy as jnp
from jax import lax
from jax.experimental import pallas as pl
from jax.experimental.pallas import tpu as pltpu
from jax.sharding import PartitionSpec as P

D = 1024
FF = 4608
NS_ITERS = 4
STEP = 10


NORM_EPS = 1e-05
QUINTIC_FIRST = 3.4445
QUINTIC_SECOND = -4.775
QUINTIC_THIRD = 2.0315
MOMENTUM_DECAY = 0.95
FIRST_DECAY = 0.9
SECOND_DECAY = 0.999
ADAM_EPS = 1e-08
ADAM_RATE = 0.4
WEIGHT_DECAY = 0.01
ORTHO_EPS = 1e-07

MESH = pl.DeviceIdType.MESH
BF16 = jnp.bfloat16
F32 = jnp.float32

PIECES = 32
PER_CHAN = 8
PIECE = FF // PIECES
LANES = 128
TILES = FF // 4 // LANES
UNIT = LANES // PER_CHAN
SMALL_PIECE = 4 * D // PIECES
IN_PIECES = 6


def remote(src, dst, send, recv, **place):
    return pltpu.make_async_remote_copy(
        src_ref=src, dst_ref=dst, send_sem=send, recv_sem=recv, device_id=place, device_id_type=MESH
    )


def flip(index, bit):
    step = 1 << bit
    return index + step * (1 - 2 * lax.rem(lax.div(index, step), 2))


def flips(index, bits):
    found = [index]
    for bit in bits:
        found = found + [flip(one, bit) for one in found]
    return found


def greet(places):
    barrier = pltpu.get_barrier_semaphore()
    for place in places:
        pl.semaphore_signal(barrier, inc=1, device_id=place, device_id_type=MESH)
    pl.semaphore_wait(barrier, len(places))


def high_bits(bits, half):
    order = list(range(1, bits))
    return order if half == 0 else order[::-1]


def call(kernel, outs, in_spaces, out_spaces, scratch, ident, *args, vmem=48):
    return pl.pallas_call(
        kernel,
        out_shape=outs,
        in_specs=[pl.BlockSpec(memory_space=space) for space in in_spaces],
        out_specs=jax.tree.map(lambda space: pl.BlockSpec(memory_space=space), out_spaces),
        scratch_shapes=scratch,
        compiler_params=pltpu.CompilerParams(
            collective_id=ident, has_side_effects=True, vmem_limit_bytes=vmem * 1024 * 1024
        ),
    )(*args)


def holder(r, c, seqs):
    at = lax.rem(r + PIECES * seqs - PER_CHAN * c, seqs)
    return at, at < PER_CHAN, lax.div(PER_CHAN * c + at, seqs)


class Homeward:
    def __init__(self, seqs, chans, held, out, between, sems):
        self.seqs, self.chans, self.held, self.out, self.between = seqs, chans, held, out, between
        self.own_sem, self.stay_sem, self.a_send, self.a_recv, self.b_send, self.b_recv = sems
        self.r, self.c = lax.axis_index("seq"), lax.axis_index("chan")
        self.at_out, self.has, self.place = holder(self.r, self.c, seqs)

    def target(self, at):
        return lax.div(self.r + self.seqs * at, PER_CHAN)

    def dropping(self, at):
        return remote(
            self.held.at[at], self.between.at[self.c], self.a_send.at[at], self.a_recv.at[self.c],
            chan=self.target(at),
        )

    def keeping(self, at):
        return pltpu.make_async_copy(self.held.at[at], self.between.at[self.c], self.own_sem.at[0])

    def spreading(self, m, r_to):
        return remote(
            self.between.at[m, r_to], self.out.at[m, self.at_out],
            self.b_send.at[m, r_to], self.b_recv.at[m, self.at_out], seq=r_to,
        )

    def staying(self, m):
        return pltpu.make_async_copy(
            self.between.at[m, self.r], self.out.at[m, self.at_out], self.stay_sem.at[m]
        )

    def drop(self, at):
        @pl.when(self.target(at) != self.c)
        def _():
            self.dropping(at).start()

        @pl.when(self.target(at) == self.c)
        def _():
            self.keeping(at).start()

    def spread(self):
        @pl.when(self.has)
        def _():
            for off in (0, 1, 3, 2):
                m = lax.rem(self.c + off, self.chans)
                if off == 0:
                    self.keeping(0).wait()
                else:
                    remote(
                        self.held.at[0], self.between.at[m], self.a_send.at[0], self.a_recv.at[m], chan=m
                    ).wait_recv()
                for step in range(1, self.seqs):
                    self.spreading(m, lax.rem(self.r + step, self.seqs)).start()
                self.staying(m).start()

    def finish(self):
        @pl.when(self.has)
        def _():
            for m in range(self.chans):
                self.staying(m).wait()

        for piece in range(PER_CHAN):
            r_from = lax.rem(PER_CHAN * self.c + piece, self.seqs)

            @pl.when(r_from != self.r)
            def _():
                for m in range(self.chans):
                    remote(
                        self.between.at[m, self.r], self.out.at[m, piece],
                        self.b_send.at[m, self.r], self.b_recv.at[m, piece], seq=r_from,
                    ).wait_recv()

        for at in range(PIECES // self.seqs):

            @pl.when(self.target(at) != self.c)
            def _():
                self.dropping(at).wait_send()

        @pl.when(self.has)
        def _():
            for m in range(self.chans):
                for step in range(1, self.seqs):
                    self.spreading(m, lax.rem(self.r + step, self.seqs)).wait_send()

    @staticmethod
    def semaphores(seqs, chans):
        dma = pltpu.SemaphoreType.DMA
        return [
            dma((1,)), dma((chans,)), dma((PIECES // seqs,)), dma((chans,)),
            dma((chans, seqs)), dma((chans, PER_CHAN)),
        ]


class Relay:
    def __init__(self, chans, own, blocks, sems):
        self.chans, self.own, self.blocks = chans, own, blocks
        self.own_sem, self.send, self.recv = sems
        self.c = lax.axis_index("chan")

    def keeping(self):
        return pltpu.make_async_copy(self.own, self.blocks.at[self.c], self.own_sem.at[0])

    def copies(self, hop):
        c = self.c
        for side, block, sends in (
            (0, c - hop, (c < self.chans - 1) & (c >= hop)),
            (1, c + hop, (c > 0) & (c + hop < self.chans)),
        ):
            source = self.own if hop == 0 else self.blocks.at[block]
            yield sends, remote(
                source, self.blocks.at[block], self.send.at[side, hop], self.recv.at[side, hop],
                chan=c + 1 - 2 * side,
            )

    def await_hop(self, hop):
        c = self.c
        for side, block, comes in ((0, c - 1 - hop, c > hop), (1, c + 1 + hop, c + 1 + hop < self.chans)):

            @pl.when(comes)
            def _():
                remote(
                    self.own, self.blocks.at[block], self.send.at[side, hop], self.recv.at[side, hop],
                    chan=c - 1 + 2 * side,
                ).wait_recv()

    def step(self, hop):
        if hop == 0:
            self.keeping().start()
        else:
            self.await_hop(hop - 1)
        for sends, copy in self.copies(hop):

            @pl.when(sends)
            def _():
                copy.start()

    def finish(self):
        self.await_hop(self.chans - 2)
        self.keeping().wait()
        for hop in range(self.chans - 1):
            for sends, copy in self.copies(hop):

                @pl.when(sends)
                def _():
                    copy.wait_send()

    @staticmethod
    def semaphores(chans):
        dma = pltpu.SemaphoreType.DMA
        return [dma((1,)), dma((2, chans - 1)), dma((2, chans - 1))]


def dot(left, right):
    return jnp.dot(left, right, preferred_element_type=F32)


def contract_last(left, right):
    return lax.dot_general(left, right, (((1,), (1,)), ((), ())), preferred_element_type=F32)


def contract_first(left, right):
    return lax.dot_general(left, right, (((0,), (0,)), ((), ())), preferred_element_type=F32)


def ortho_kernel(
    seqs, chans, grad, moment, input_grad, grad_home, ortho_home, input_blocks,
    out, cut_grad, cut_ortho, between_grad, between_ortho,
    part, own, swapped, paired, parts, sums, gram, poly, half_way,
    x_send, x_recv, s_send, s_recv, g_send, g_recv, f_send, f_recv, *home_sems
):
    r, c = lax.axis_index("seq"), lax.axis_index("chan")
    core, h = lax.rem(r, 2), lax.div(r, 2)
    other = flip(r, 0)
    count, half, block = seqs // 2, D // 2, D // seqs
    tile = min(256, half)
    peers = [lax.rem(h + off, count) for off in range(1, count)]
    greet(
        [{"seq": lax.rem(r + off, seqs)} for off in range(1, seqs)]
        + [{"chan": lax.rem(c + off, chans)} for off in range(1, chans)]
    )
    home_grad = Homeward(seqs, chans, cut_grad, grad_home, between_grad, home_sems[:6])
    home_ortho = Homeward(seqs, chans, cut_ortho, ortho_home, between_ortho, home_sems[6:12])
    relay = Relay(chans, input_grad, input_blocks, home_sems[12:])
    columns = out.shape[0]
    slab = PIECE

    @pl.loop(0, columns // slab)
    def _(at):
        here = pl.ds(pl.multiple_of(at * slab, slab), slab)
        out[here] = (MOMENTUM_DECAY * moment[here].astype(F32) + grad[here].astype(F32)).astype(BF16)
        for to in range(seqs):
            cut_grad[at, to] = grad[here, to * block : (to + 1) * block]

    for at in range(columns // slab):
        home_grad.drop(at)
    relay.step(0)

    apart = c == chans - 1

    def kind(pair):
        return jnp.where(lax.rem(pair, 4) == 3, 1, 0)

    mine = kind(h)
    own_first = pl.multiple_of(core * half, half)
    other_first = pl.multiple_of((1 - core) * half, half)

    def block_at(pair, which):
        return pl.ds(pl.multiple_of(which * half + pair * block, block), block)

    def exchange():
        return remote(part, swapped, x_send, x_recv, seq=other)

    def scatter(peer):
        return remote(
            paired.at[peer], parts.at[h], s_send.at[peer], s_recv.at[h], seq=2 * peer + core
        )

    def scatter_in(peer):
        return remote(
            paired.at[peer], parts.at[peer], s_send.at[peer], s_recv.at[peer], seq=2 * peer + core
        )

    def share(peer):
        return remote(
            sums.at[kind(peer)], gram.at[block_at(h, core)], g_send.at[peer], g_recv.at[h],
            seq=2 * peer + core,
        )

    def share_in(peer):
        return remote(
            sums.at[0], gram.at[block_at(peer, core)], g_send.at[peer], g_recv.at[peer],
            seq=2 * peer + core,
        )

    def forward(pair):
        return remote(
            gram.at[block_at(pair, core)], gram.at[block_at(pair, core)],
            f_send.at[pair], f_recv.at[pair], seq=other,
        )

    def forward_in(pair):
        return remote(
            gram.at[block_at(pair, 1 - core)], gram.at[block_at(pair, 1 - core)],
            f_send.at[pair], f_recv.at[pair], seq=other,
        )

    for turn in range(NS_ITERS // 2):

        @pl.loop(0, half // tile)
        def _(at):
            here = pl.ds(pl.multiple_of(at * tile, tile), tile)
            there = pl.ds(pl.multiple_of(other_first + at * tile, tile), tile)
            part[here] = contract_first(out[:, there], out[...]).astype(BF16)

        exchange().start()

        @pl.loop(0, half // tile)
        def _(at):
            here = pl.ds(pl.multiple_of(at * tile, tile), tile)
            there = pl.ds(pl.multiple_of(own_first + at * tile, tile), tile)
            own[here] = contract_first(out[:, there], out[...])

        exchange().wait()

        @pl.loop(0, count)
        def _(at):
            here = pl.ds(pl.multiple_of(at * block, block), block)
            paired[at] = (own[here] + swapped[here].astype(F32)).astype(BF16)

        for peer in peers:
            scatter(peer).start()
        parts[h] = paired[h]
        for peer in peers:
            scatter_in(peer).wait_recv()
        groups = [jnp.zeros((block, D), F32), jnp.zeros((block, D), F32)]
        for pair in range(count):
            groups[int(pair % 4 == 3)] += parts[pair].astype(F32)
        both = groups[0] + groups[1]
        sums[0] = jnp.where(apart, groups[0], both).astype(BF16)
        sums[1] = jnp.where(apart, groups[1], both).astype(BF16)
        for peer in peers:
            share(peer).start()
        if turn == 1:
            relay.step(2)
        gram[block_at(h, core)] = sums[mine]
        forward(h).start()
        for peer in peers:
            share_in(peer).wait_recv()
            forward(peer).start()
        for pair in [h] + peers:
            forward_in(pair).wait_recv()
        for peer in peers:
            scatter(peer).wait_send()
            share(peer).wait_send()
        for pair in [h] + peers:
            forward(pair).wait_send()
        if turn == 0:
            relay.step(1)

        scale = jnp.ones((1, 1), F32)
        if turn == 0:
            trace = jnp.zeros((1, 1), F32)
            for at in range(D // 128):
                square = gram[at * 128 : (at + 1) * 128, at * 128 : (at + 1) * 128].astype(F32)
                row = lax.broadcasted_iota(jnp.int32, square.shape, 0)
                column = lax.broadcasted_iota(jnp.int32, square.shape, 1)
                trace += jnp.sum(jnp.where(row == column, square, 0.0), keepdims=True)
            scale = 1.0 / (jnp.sqrt(trace) + ORTHO_EPS)

            @pl.loop(0, D // tile)
            def _(at):
                here = pl.ds(pl.multiple_of(at * tile, tile), tile)
                gram[here] = (gram[here].astype(F32) * scale * scale).astype(BF16)

        def each_tile(work):
            @pl.loop(0, D // tile)
            def _(at):
                work(pl.ds(pl.multiple_of(at * tile, tile), tile))

        def polynomial(values, whole):
            return (
                QUINTIC_SECOND * values.astype(F32) + QUINTIC_THIRD * dot(values, whole[...])
            ).astype(BF16)

        def first_poly(here):
            poly[here] = polynomial(gram[here], gram)

        def halfway(here):
            half_way[here] = (
                QUINTIC_FIRST * gram[here].astype(F32) + dot(poly[here], gram[...])
            ).astype(BF16)

        def next_gram(here):
            gram[here] = (
                QUINTIC_FIRST * half_way[here].astype(F32) + dot(half_way[here], poly[...])
            ).astype(BF16)

        def second_poly(here):
            half_way[here] = polynomial(gram[here], gram)

        for work in (first_poly, halfway, next_gram, second_poly):
            each_tile(work)

        @pl.loop(0, columns // slab)
        def _(at):
            here = pl.ds(pl.multiple_of(at * slab, slab), slab)
            new = QUINTIC_FIRST * out[here].astype(F32) + dot(out[here], poly[...])
            if turn == 0:
                new = new * scale
            new = QUINTIC_FIRST * new + dot(new.astype(BF16), half_way[...])
            if turn < NS_ITERS // 2 - 1:
                out[here] = new.astype(BF16)
            else:
                for to in range(seqs):
                    cut_ortho[at, to] = new[:, to * block : (to + 1) * block].astype(BF16)
                home_ortho.drop(at)

        if turn == 0:
            home_grad.spread()

    home_ortho.spread()
    home_grad.finish()
    relay.finish()
    home_ortho.finish()


def orthogonalize(seqs, chans, grad, moment, input_grad):
    dma = pltpu.SemaphoreType.DMA
    count, block, held = seqs // 2, D // seqs, PIECES // seqs
    return call(
        functools.partial(ortho_kernel, seqs, chans),
        [jax.ShapeDtypeStruct((chans, PER_CHAN, PIECE, block), BF16)] * 2
        + [jax.ShapeDtypeStruct((chans,) + input_grad.shape, BF16)],
        [pltpu.VMEM] * 2 + [pl.ANY],
        [pl.ANY] * 3,
        [
            pltpu.VMEM(grad.shape, BF16),
            pltpu.VMEM((held, seqs, PIECE, block), BF16),
            pltpu.VMEM((held, seqs, PIECE, block), BF16),
            pltpu.VMEM((chans, seqs, PIECE, block), BF16),
            pltpu.VMEM((chans, seqs, PIECE, block), BF16),
            pltpu.VMEM((D // 2, D), BF16),
            pltpu.VMEM((D // 2, D), F32),
            pltpu.VMEM((D // 2, D), BF16),
            pltpu.VMEM((count, block, D), BF16),
            pltpu.VMEM((count, block, D), BF16),
            pltpu.VMEM((2, block, D), BF16),
            pltpu.VMEM((D, D), BF16),
            pltpu.VMEM((D, D), BF16),
            pltpu.VMEM((D, D), BF16),
            dma(()),
            dma(()),
        ]
        + [dma((count,))] * 6
        + Homeward.semaphores(seqs, chans) * 2
        + Relay.semaphores(chans),
        2,
        grad,
        moment,
        input_grad,
    )


HEAD = 8


def own_rows(values, seqs_held):
    length = values.shape[0] // seqs_held
    return [values[s * length + HEAD : (s + 1) * length] for s in range(seqs_held)]


def row_scale(values):
    return lax.rsqrt(jnp.mean(values * values, axis=1, keepdims=True) + NORM_EPS)


def filtering(gated, taps, keep_one, keep_two):
    back_one, back_two = pltpu.roll(gated, 1, 0), pltpu.roll(gated, 2, 0)
    return taps[2:3] * gated + taps[1:2] * keep_one * back_one + taps[0:1] * keep_two * back_two


def forward_kernel(seqs, chans, held, *refs):
    forward_work(seqs, chans, held, refs[:5], refs[5:10], *refs[10:])


def forward_work(
    seqs, chans, held,
    weights, moments, own_taps, token_source, cotangent_source, keeps, gains,
    in_full, out_full, ffn_full, taps_all, held_out, between, streams, ffn_g,
    tokens, cotangent, residual, second_grad, block_out,
    in_shard, out_shard, ffn_shard, taps, packed, shelf, shelf_sem,
    u, u_own, halo, row_sem, halo_sem, halo_send, halo_recv, normed, mixed, stream, x, x_own, ffn_out, act, gate_low, up_low, in_v, out_v, taps_v, w_v, grad_v,
    own_sem, z_send, z_recv, b_send, b_recv, c_send, c_recv,
    t_own, t_send, t_recv, p_own, ps_send, ps_recv, pl_send, pl_recv,
    mix_sem, taps_sem, stream_sem, load_sem, grad_sem,
):
    bits = seqs.bit_length() - 1
    r, c = lax.axis_index("seq"), lax.axis_index("chan")
    last = TILES + 1
    greet(
        [{"chan": lax.rem(c + off, chans)} for off in range(1, chans)]
        + [{"seq": lax.rem(r + off, seqs)} for off in range(1, seqs)]
    )

    def shard(k):
        if isinstance(k, int) and k < 2:
            return (in_shard, out_shard)[k]
        return ffn_shard.at[k - 2]

    def full(k, part, block):
        if isinstance(k, int) and k < 2:
            return (in_full, out_full)[k].at[part, block]
        return ffn_full.at[k - 2, part, block]

    def own(k):
        return pltpu.make_async_copy(shard(k), full(k, c, r), own_sem.at[k])

    def along_chan(k, off, incoming):
        source = lax.rem(c + chans - off, chans) if incoming else c
        return remote(
            shard(k), full(k, source, r), z_send.at[k, off - 1], z_recv.at[k, off - 1],
            chan=lax.rem(c + off, chans),
        )

    def across(k, half, step, incoming):
        order = high_bits(bits, half)
        bit, done = order[step], order[:step]
        base = flip(r, bit) if incoming else r
        part = pl.ds(half * (chans // 2), chans // 2)
        first = (1 << step) - 1
        return [
            remote(
                full(k, part, block), full(k, part, block),
                b_send.at[k, half, first + at], b_recv.at[k, half, first + at], seq=flip(r, bit),
            )
            for at, block in enumerate(flips(base, done))
        ]

    def core(k, incoming):
        base = flip(r, 0) if incoming else r
        return [
            remote(
                full(k, slice(None), block), full(k, slice(None), block),
                c_send.at[k, at], c_recv.at[k, at], seq=flip(r, 0),
            )
            for at, block in enumerate(flips(base, range(1, bits)))
        ]

    def start_chan(k):
        own(k).start()
        for off in (2, 1, 3):
            along_chan(k, off, False).start()

    def first_level(k):
        own(k).wait()
        for off in range(1, chans):
            along_chan(k, off, True).wait_recv()
        for half in range(2):
            for copy in across(k, half, 0, False):
                copy.start()

    def next_level(k, level):
        for half in range(2):
            for copy in across(k, half, level - 1, True):
                copy.wait_recv()
            for copy in across(k, half, level, False):
                copy.start()

    def to_core(k):
        for half in range(2):
            for copy in across(k, half, bits - 2, True):
                copy.wait_recv()
        for copy in core(k, False):
            copy.start()

    def arrived(k):
        for copy in core(k, True):
            copy.wait_recv()

    def sent(k):
        for off in range(1, chans):
            along_chan(k, off, False).wait_send()
        for half in range(2):
            for step in range(bits - 1):
                for copy in across(k, half, step, False):
                    copy.wait_send()
        for copy in core(k, False):
            copy.wait_send()

    def taps_copy(off, incoming):
        source = lax.rem(c + chans - off, chans) if incoming else c
        return remote(
            taps, taps_all.at[source], t_send.at[off - 1], t_recv.at[off - 1],
            chan=lax.rem(c + off, chans),
        )

    _, has, place = holder(r, c, seqs)

    def spread(piece, r_to):
        return remote(
            packed.at[:, piece], between.at[:, r], ps_send.at[piece], ps_recv.at[r], seq=r_to
        )

    def lift(m):
        return remote(between.at[m], held_out.at[place], pl_send.at[m], pl_recv.at[place], chan=m)

    def pieces_start():
        for piece in range(PER_CHAN):
            r_to = lax.rem(PER_CHAN * c + piece, seqs)

            @pl.when(r_to != r)
            def _():
                spread(piece, r_to).start()

            @pl.when(r_to == r)
            def _():
                pltpu.make_async_copy(packed.at[:, piece], between.at[:, r], p_own.at[0]).start()

    def pieces_lift():
        @pl.when(has)
        def _():
            pltpu.make_async_copy(packed.at[:, 0], between.at[:, r], p_own.at[0]).wait()
            for off in range(1, seqs):
                r_from = lax.rem(r + off, seqs)
                remote(
                    packed.at[:, 0], between.at[:, r_from], ps_send.at[0], ps_recv.at[r_from], seq=r_from
                ).wait_recv()
            for m in range(chans):

                @pl.when(m != c)
                def _():
                    lift(m).start()

                @pl.when(m == c)
                def _():
                    copy = pltpu.make_async_copy(between.at[m], held_out.at[place], p_own.at[1])
                    copy.start()
                    copy.wait()

    def pieces_finish():
        for at in range(PIECES // seqs):
            c_from = lax.div(r + seqs * at, PER_CHAN)

            @pl.when(c_from != c)
            def _():
                remote(
                    between.at[0], held_out.at[at], pl_send.at[0], pl_recv.at[at], chan=c_from
                ).wait_recv()

        for piece in range(PER_CHAN):
            r_to = lax.rem(PER_CHAN * c + piece, seqs)

            @pl.when(r_to != r)
            def _():
                spread(piece, r_to).wait_send()

        @pl.when(has)
        def _():
            for m in range(chans):

                @pl.when(m != c)
                def _():
                    lift(m).wait_send()

    rows, width = tokens.shape
    part = out_full.shape[-1]
    tile = rows // 3
    per_tile = held // 3
    size = rows // held - HEAD
    tiles = [pl.ds(at * tile, tile) for at in range(3)]

    def mix_loads(j):
        slot = lax.rem(j, 2)
        return [
            pltpu.make_async_copy(in_full.at[j], in_v.at[slot], mix_sem.at[slot, 0]),
            pltpu.make_async_copy(out_full.at[j], out_v.at[slot], mix_sem.at[slot, 1]),
        ]

    def stream_out(j):
        return pltpu.make_async_copy(stream, streams.at[j], stream_sem)

    local_rows = token_source.shape[1]
    before_at = pl.multiple_of(lax.rem(c + chans - 1, chans) * size + size - HEAD, HEAD)
    after_at = pl.multiple_of(lax.rem(c + 1, chans) * size, HEAD)
    halos = [
        (token_source, before_at, c == 0, r > 0, r < seqs - 1, 1),
        (token_source, after_at, c == chans - 1, r < seqs - 1, r > 0, -1),
        (cotangent_source, after_at, c == chans - 1, r < seqs - 1, r > 0, -1),
    ]

    def row_copies():
        return [
            pltpu.make_async_copy(
                source.at[s, pl.ds(pl.multiple_of(c * size, size), size)],
                rows_to.at[pl.ds(s * (size + HEAD) + HEAD, size)],
                row_sem.at[n, s],
            )
            for n, (source, rows_to) in enumerate(
                ((token_source, tokens), (cotangent_source, cotangent))
            )
            for s in range(held)
        ]

    def halo_local(n):
        source, at, _, _, _, _ = halos[n]
        return pltpu.make_async_copy(source.at[:, pl.ds(at, HEAD)], halo.at[n], halo_sem.at[n])

    def halo_remote(n):
        source, at, _, _, _, step = halos[n]
        return remote(
            source.at[:, pl.ds(at, HEAD)], halo.at[n], halo_send.at[n], halo_recv.at[n], seq=r + step
        )

    def rows_start():
        for copy in row_copies():
            copy.start()
        for n, (_, _, edge, takes, gives, _) in enumerate(halos):

            @pl.when(jnp.logical_not(edge))
            def _():
                halo_local(n).start()

            @pl.when(edge & gives)
            def _():
                halo_remote(n).start()

            @pl.when(edge & jnp.logical_not(takes))
            def _():
                halo[n] = jnp.zeros(halo.shape[1:], F32)

    def rows_finish():
        for copy in row_copies():
            copy.wait()
        for n, (_, _, edge, takes, gives, _) in enumerate(halos):

            @pl.when(jnp.logical_not(edge))
            def _():
                halo_local(n).wait()

            @pl.when(edge & takes)
            def _():
                halo_remote(n).wait_recv()

            @pl.when(edge & gives)
            def _():
                halo_remote(n).wait_send()

        row = lax.broadcasted_iota(jnp.int32, (HEAD, width), 0)
        for s in range(held):
            head = pl.ds(s * (size + HEAD), HEAD)
            earlier = (s - 1) % held
            tokens[head] = jnp.where(row < 2, halo[1, earlier], halo[0, s])
            cotangent[head] = jnp.where(row < 2, halo[2, earlier], 0.0)
        for at, here in enumerate(tiles):
            values = cotangent[here]
            u[here] = values.astype(BF16)
            for s, one in enumerate(own_rows(values, per_tile)):
                u_own[pl.ds((at * per_tile + s) * size, size)] = one.astype(BF16)

    def mix_prepare():
        rows_finish()
        for here in tiles:
            values = tokens[here]
            normed[here] = (values * row_scale(values) * gains[0:1]).astype(BF16)
            residual[here] = values

    def transfers(tick):
        @pl.when(tick + 2 <= last)
        def _():
            start_chan(tick + 2)

        @pl.when(tick <= last)
        def _():
            first_level(tick)

        for level in range(1, bits - 1):

            @pl.when(tick - level <= last)
            def _():
                next_level(tick - level, level)

        @pl.when(tick - bits + 1 <= last)
        def _():
            to_core(tick - bits + 1)

        @pl.when(tick - bits <= last)
        def _():
            arrived(tick - bits)
            for copy in loads(tick - bits - 2):
                copy.start()

    def mix():
        for copy in mix_loads(0):
            copy.start()
        copy = pltpu.make_async_copy(taps_all, taps_v, taps_sem)
        copy.start()
        copy.wait()

        @pl.loop(0, chans)
        def _(j):
            slot = lax.rem(j, 2)
            for copy in mix_loads(j):
                copy.wait()

            @pl.when(j + 1 < chans)
            def _():
                for copy in mix_loads(j + 1):
                    copy.start()

            @pl.when(j > 0)
            def _():
                stream_out(j - 1).wait()

            in_w = in_v[slot].reshape(width, 3 * part)
            out_w = out_v[slot].reshape(width, part)
            for here in tiles:
                stream[here] = dot(normed[here], in_w)
            filters = taps_v[j]
            gated = stream[:, 0:part] * stream[:, 2 * part :]
            filtered = filtering(gated, filters, keeps[:, 0:1], keeps[:, 1:2])
            mixed[...] = (stream[:, part : 2 * part] * filtered).astype(BF16)
            stream_out(j).start()
            for here in tiles:
                residual[here] += contract_last(mixed[here], out_w)

            @pl.when(j == 1)
            def _():
                transfers(bits + 2)

        for at, here in enumerate(tiles):
            values = residual[here]
            new = values * row_scale(values) * gains[1:2]
            x[here] = new.astype(BF16)
            for s, one in enumerate(own_rows(new, per_tile)):
                x_own[pl.ds((at * per_tile + s) * size, size)] = one.astype(BF16)
            ffn_out[here] = jnp.zeros((tile, width), F32)
            second_grad[here] = jnp.zeros((tile, width), F32)
        stream_out(chans - 1).wait()

    def loads(t):
        slot = lax.rem(t, 2)
        return [
            pltpu.make_async_copy(
                ffn_full.at[t, j, :, m],
                w_v.at[slot, m, :, :, pl.ds(j * LANES, LANES)],
                load_sem.at[slot, m, j],
            )
            for m in range(3)
            for j in range(chans)
        ]

    def grads_out(t):
        slot = lax.rem(t, 2)
        return [
            pltpu.make_async_copy(grad_v.at[slot, m], ffn_g.at[m, :, t], grad_sem.at[slot, m])
            for m in range(3)
        ]

    def feed_forward(t):
        slot = lax.rem(t, 2)
        for copy in loads(t):
            copy.wait()

        @pl.when(t >= 2)
        def _():
            for copy in grads_out(t - 2):
                copy.wait()

        wg, wu, wd = (w_v[slot, m].reshape(width, chans * LANES) for m in range(3))
        for at, here in enumerate(tiles):
            gate = dot(x[here], wg)
            up = dot(x[here], wu)
            grad = dot(u[here], wd)
            sigmoid = jax.nn.sigmoid(gate)
            silu = gate * sigmoid
            new_act = silu * up
            new_gate = grad * up * sigmoid * (1.0 + gate * (1.0 - sigmoid))
            new_up = grad * silu
            for ref, values in ((act, new_act), (gate_low, new_gate), (up_low, new_up)):
                for s, one in enumerate(own_rows(values, per_tile)):
                    ref[pl.ds((at * per_tile + s) * size, size)] = one.astype(BF16)
            ffn_out[here] += contract_last(new_act.astype(BF16), wd)
            second_grad[here] += contract_last(new_gate.astype(BF16), wg) + contract_last(
                new_up.astype(BF16), wu
            )
        for m, (low, right) in enumerate(((gate_low, x_own), (up_low, x_own), (act, u_own))):
            grad_v[slot, m] = (
                contract_first(low[...], right[...]).astype(BF16).reshape(PIECES, UNIT, width)
            )
        for copy in grads_out(t):
            copy.start()

    def shelf_copies(group, n):
        slot = n % 2
        if n % 4 == 0:
            part_of = [(group[0].at[k], k) for k in range(3)] + [(group[1], 3)]
            return [
                pltpu.make_async_copy(
                    source, shelf.at[slot, :, pl.ds(k * part, part)], shelf_sem.at[slot, k]
                )
                for source, k in part_of
            ]
        return [pltpu.make_async_copy(group[n % 4 + 1], shelf.at[slot], shelf_sem.at[slot, 0])]

    def shelves(n):
        return shelf_copies(weights if n < 4 else moments, n)

    for copy in shelves(0):
        copy.start()
    taps[...] = jnp.zeros_like(taps)
    taps[0:3] = own_taps[...]
    rows_start()
    for n in range(8):
        if n < 7:
            for copy in shelves(n + 1):
                copy.start()
        for copy in shelves(n):
            copy.wait()
        slot, m = n % 2, n % 4 - 1
        if n == 0:
            in_shard[...] = shelf[slot, :, : 3 * part].astype(BF16)
            out_shard[...] = shelf[slot, :, 3 * part : 4 * part].astype(BF16)
            start_chan(0)
            start_chan(1)
        elif n < 4:
            for t in range(TILES):
                ffn_shard[t, m] = shelf[slot, :, t * LANES : (t + 1) * LANES].astype(BF16)
        elif n == 4:
            packed[3] = jnp.zeros(packed.shape[1:], BF16)
            for q in range(PER_CHAN):
                block = shelf[slot, :, q * SMALL_PIECE : (q + 1) * SMALL_PIECE]
                packed[3, q, 0:SMALL_PIECE] = block.T.astype(BF16)
        else:
            for t in range(TILES):
                block = shelf[slot, :, t * LANES : (t + 1) * LANES].T.astype(BF16)
                packed[m, :, t * UNIT : (t + 1) * UNIT] = block.reshape(PER_CHAN, UNIT, -1)
    pieces_start()
    taps_own = pltpu.make_async_copy(taps, taps_all.at[c], t_own)
    taps_own.start()
    for off in range(1, chans):
        taps_copy(off, False).start()
    mix_prepare()

    for tick in range(bits + 2):
        start_chan(tick + 2)
        first_level(tick)
        for level in range(1, bits - 1):
            if tick >= level:
                next_level(tick - level, level)
        if tick >= bits - 1:
            to_core(tick - bits + 1)
        if tick >= bits:
            arrived(tick - bits)
        if tick == 1:
            pieces_lift()
    taps_own.wait()
    for off in range(1, chans):
        taps_copy(off, True).wait_recv()
    mix()

    @pl.loop(bits + 3, last + bits + 2)
    def _(tick):
        transfers(tick)
        feed_forward(tick - bits - 3)

    for s in range(held):
        here = pl.ds(s * (size + HEAD) + HEAD, size)
        block_out[pl.ds(s * size, size)] = (residual[here] + ffn_out[here]).astype(BF16)
    for t in (TILES - 2, TILES - 1):
        for copy in grads_out(t):
            copy.wait()
    pieces_finish()
    for off in range(1, chans):
        taps_copy(off, False).wait_send()
    sent(0)
    sent(1)

    @pl.loop(2, last + 1)
    def _(k):
        sent(k)


def forward_pass(seqs, chans, weights, moments, taps, tokens, cotangent, keeps, gains):
    held, local_rows, width = tokens.shape
    block, part = weights[1].shape
    own_count, hidden = held * local_rows // chans, chans * LANES
    rows = own_count + held * HEAD
    tail = (PIECE, block)
    shape = jax.ShapeDtypeStruct
    outs = [
        shape((chans, seqs, block, 3 * part), BF16),
        shape((chans, seqs, block, part), BF16),
        shape((TILES, chans, seqs, 3, block, LANES), BF16),
        shape((chans, 8, part), F32),
        shape((PIECES // seqs, seqs) + tail, BF16),
        shape((chans, seqs) + tail, BF16),
        shape((chans, rows, 3 * part), F32),
    ]
    outs.append(shape((3, PIECES, TILES, UNIT, width), BF16))
    outs += [shape((rows, width), F32)] * 4 + [shape((own_count, width), BF16)]
    dma = pltpu.SemaphoreType.DMA
    count = TILES + 2
    vmem = pltpu.VMEM
    found = call(
        functools.partial(forward_kernel, seqs, chans, held),
        outs,
        [pl.ANY] * 10 + [vmem] + [pl.ANY] * 2 + [vmem] * 2,
        [pl.ANY] * 8 + [vmem] * 5,
        [
            vmem((block, 3 * part), BF16),
            vmem((block, part), BF16),
            vmem((TILES, 3, block, LANES), BF16),
            vmem((8, part), F32),
            vmem((chans, PER_CHAN) + tail, BF16),
            vmem((2, block, TILES * LANES), F32),
            dma((2, 4)),
            vmem((rows, width), BF16),
            vmem((own_count, width), BF16),
            vmem((3, held, HEAD, width), F32),
            dma((2, held)),
            dma((3,)),
            dma((3,)),
            dma((3,)),
            vmem((rows, width), BF16),
            vmem((rows, part), BF16),
            vmem((rows, 3 * part), F32),
            vmem((rows, width), BF16),
            vmem((own_count, width), BF16),
            vmem((rows, width), F32),
            vmem((own_count, hidden), BF16),
            vmem((own_count, hidden), BF16),
            vmem((own_count, hidden), BF16),
            vmem((2, seqs, block, 3 * part), BF16),
            vmem((2, seqs, block, part), BF16),
            vmem((chans, 8, part), F32),
            vmem((2, 3, seqs, block, hidden), BF16),
            vmem((2, 3, PIECES, UNIT, width), BF16),
            dma((count,)),
            dma((count, chans - 1)),
            dma((count, chans - 1)),
            dma((count, 2, seqs // 2 - 1)),
            dma((count, 2, seqs // 2 - 1)),
            dma((count, seqs // 2)),
            dma((count, seqs // 2)),
            dma(()),
            dma((chans - 1,)),
            dma((chans - 1,)),
            dma((2,)),
            dma((PER_CHAN,)),
            dma((seqs,)),
            dma((chans,)),
            dma((PIECES // seqs,)),
            dma((2, 2)),
            dma(()),
            dma(()),
            dma((2, 3, chans)),
            dma((2, 3)),
        ],
        0,
        *weights, *moments, taps, tokens, cotangent, keeps, gains,
        vmem=62,
    )
    return found


LAG = 2


def add_rows(acc, other):
    return (acc.astype(F32) + other.astype(F32)).astype(BF16)


def backward_kernel(
    seqs, chans, held,
    ffn_g, in_full, out_full, streams, block_own,
    tokens, residual, second_grad, cotangent, keeps, gains, taps,
    result, total, input_grad, io_g, blocks, *refs
):
    bits = seqs.bit_length() - 1
    levels = bits - 1
    landed, line_land = refs[: levels + 1], refs[levels + 1]
    temps, refs = refs[levels + 2 : 2 * levels + 3], refs[2 * levels + 3 :]
    (
        acc, line_temp, sent, got, sums,
        residual_low, low_own, first_own, residual_grad, stream_own, mixed_own, mixer_grad, first_grad,
        stream, in_v, out_v, staging,
        load_sem, temp_sem, fetch_sem, c_send, c_recv, b_send, b_recv, z_send, z_recv, n_send, n_recv,
        mix_sem, io_sem, *relay_sems
    ) = refs
    parts, half_seqs = PIECES // seqs, seqs // 2
    chunks = chans * parts
    slots, group = acc.shape[0], temps[0].shape[0]
    at_once = group == half_seqs
    r, c = lax.axis_index("seq"), lax.axis_index("chan")
    core, h = lax.rem(r, 2), lax.div(r, 2)
    partners = [{"seq": flip(r, bit)} for bit in range(bits)]
    greet(partners + [{"chan": lax.rem(c + off, chans)} for off in range(1, chans)])
    partners += [{"chan": flip(c, bit)} for bit in range(chans.bit_length() - 1)]

    def slot_of(k):
        return lax.rem(k, slots)

    def core_copy(k, source):
        return remote(source.at[:, 1 - core], landed[0].at[k], c_send.at[k], c_recv.at[k], seq=flip(r, 0))

    def load(k, source):
        return pltpu.make_async_copy(source.at[:, core], acc.at[slot_of(k)], load_sem.at[k])

    def with_source(k, work):
        @pl.when(k < 3 * parts)
        def _():
            work(ffn_g.at[lax.div(k, parts), lax.rem(k, parts)])

        @pl.when(k >= 3 * parts)
        def _():
            work(io_g.at[k - 3 * parts])

    def lanes(half):
        return pl.ds(half * (D // 2), D // 2)

    def across(k, half, level):
        order = high_bits(bits, half)
        bit, rest = order[level], [one - 1 for one in order[level + 1 :]]
        base = h
        for one in rest:
            base = base - (1 << one) * lax.rem(lax.div(h, 1 << one), 2)
        first = half_seqs - (half_seqs >> level)
        copies, keeps = [], []
        for at in range(1 << len(rest)):
            place = base + sum((1 << one) for n, one in enumerate(rest) if at >> n & 1)
            copies.append(
                remote(
                    acc.at[slot_of(k), flip(place, bit - 1), :, lanes(half)],
                    landed[level + 1].at[k, at, :, lanes(half)],
                    b_send.at[k, half, first + at], b_recv.at[k, half, first + at],
                    seq=flip(r, bit),
                )
            )
            keeps.append(place)
        return copies, keeps

    def fetch(src, dst):
        copy = pltpu.make_async_copy(src, dst, temp_sem)
        copy.start()
        copy.wait()

    def begin(k):
        def work(source):
            core_copy(k, source).start()
            load(k, source).start()

        with_source(k, work)

    def level_start(k, level):
        for half in range(2):
            for copy in across(k, half, level)[0]:
                copy.start()

    def fetch_level(k, level):
        return pltpu.make_async_copy(landed[level].at[k], temps[level], fetch_sem.at[level])

    def core_arrive(k):
        load(k, io_g.at[0]).wait()
        core_copy(k, io_g.at[0]).wait_recv()
        if at_once:
            fetch_level(k, 0).start()

    def core_sum(k):
        if at_once:
            fetch_level(k, 0).wait()
        for start in range(0, half_seqs, group):
            if not at_once:
                fetch(landed[0].at[k, pl.ds(start, group)], temps[0])

            @pl.loop(0, group)
            def _(b):
                acc[slot_of(k), start + b] = add_rows(acc[slot_of(k), start + b], temps[0][b])

        level_start(k, 0)

    def level_arrive(k, level):
        for half in range(2):
            for copy in across(k, half, level)[0]:
                copy.wait_recv()
        if at_once:
            fetch_level(k, level + 1).start()

    def level_sum(k, level):
        both = [across(k, half, level) for half in range(2)]
        if at_once:
            fetch_level(k, level + 1).wait()
        temp = temps[level + 1 if at_once else 0]
        count = half_seqs >> (level + 1)
        for start in range(0, count, group):
            here = min(group, count - start)
            if not at_once:
                fetch(landed[level + 1].at[k, pl.ds(start, here)], temp.at[pl.ds(0, here)])
            for half in range(2):
                for at in range(here):
                    place = both[half][1][start + at]
                    acc[slot_of(k), place, :, lanes(half)] = add_rows(
                        acc[slot_of(k), place, :, lanes(half)], temp[at, :, lanes(half)]
                    )
        if level + 1 < levels:
            level_start(k, level + 1)

    def line(k, side):
        return remote(
            acc.at[slot_of(k), h], line_land.at[side, k], z_send.at[k], z_recv.at[side, k],
            chan=c + 1 - 2 * side,
        )

    def hop(k, step):
        keeper = lax.div(k, parts)
        for side, sends in ((0, (c < keeper) & (c == step)), (1, (c > keeper) & (chans - 1 - c == step))):

            @pl.when(sends)
            def _():
                if step > 0:
                    line(k, side).wait_recv()
                    fetch(line_land.at[side, k], line_temp.at[0])
                    acc[slot_of(k), h] = add_rows(acc[slot_of(k), h], line_temp[0])
                line(k, side).start()

    def finish(k):
        keeper = lax.div(k, parts)

        @pl.when(c == keeper)
        def _():
            for side, there in ((0, c > 0), (1, c < chans - 1)):

                @pl.when(there)
                def _():
                    line(k, side).wait_recv()
                    fetch(line_land.at[side, k], line_temp.at[side])

                @pl.when(jnp.logical_not(there))
                def _():
                    line_temp[side] = jnp.zeros(line_temp.shape[1:], BF16)

            result[lax.rem(k, parts)] = (
                acc[slot_of(k), h].astype(F32) + line_temp[0].astype(F32) + line_temp[1].astype(F32)
            ).astype(BF16)

        @pl.when(c < keeper)
        def _():
            line(k, 0).wait_send()

        @pl.when(c > keeper)
        def _():
            line(k, 1).wait_send()

        core_copy(k, io_g.at[0]).wait_send()
        for level in range(levels):
            for half in range(2):
                for copy in across(k, half, level)[0]:
                    copy.wait_send()

    def small_copy(level):
        return remote(
            sent.at[level], got.at[level], n_send.at[level], n_recv.at[level], **partners[level]
        )

    def small_step(level):
        if level == 0:
            sent[0] = sums[...]
        else:
            small_copy(level - 1).wait()
            new = sent[level - 1] + got[level - 1]
            if level == len(partners):
                total[...] = new
            else:
                sent[level] = new
        if level < len(partners):
            small_copy(level).start()

    rows, full = tokens.shape
    width = out_v.shape[-1]
    length = rows // held
    size = length - HEAD
    tile, per_tile = rows // 3, held // 3
    tiles = [pl.ds(at * tile, tile) for at in range(3)]
    own_tiles = [pl.ds(at * per_tile * size, per_tile * size) for at in range(3)]

    def mix_loads(j):
        return [
            pltpu.make_async_copy(in_full.at[j], in_v, mix_sem.at[0]),
            pltpu.make_async_copy(out_full.at[j], out_v, mix_sem.at[1]),
            pltpu.make_async_copy(streams.at[j], stream, mix_sem.at[2]),
        ]

    def io_out(j):
        at, first = lax.div(4 * j, half_seqs), lax.rem(4 * j, half_seqs)
        return pltpu.make_async_copy(staging, io_g.at[at, pl.ds(first, 4)], io_sem)

    def mix_prepare():
        gain_sum = jnp.zeros((1, full), F32)
        for at, here in enumerate(tiles):
            values = residual[here]
            scale = row_scale(values)
            unit = values * scale
            grad = second_grad[here]
            scaled = grad * gains[1:2]
            new = cotangent[here] + scale * (
                scaled - unit * jnp.mean(scaled * unit, axis=1, keepdims=True)
            )
            residual_low[here] = new.astype(BF16)
            for s, (one, two) in enumerate(
                zip(own_rows(new, per_tile), own_rows(grad * unit, per_tile))
            ):
                where = pl.ds((at * per_tile + s) * size, size)
                residual_grad[where] = one
                low_own[where] = one.astype(BF16)
                gain_sum += jnp.sum(two, axis=0, keepdims=True)
            first = tokens[here]
            first = first * row_scale(first) * gains[0:1]
            for s, one in enumerate(own_rows(first, per_tile)):
                first_own[pl.ds((at * per_tile + s) * size, size)] = one.astype(BF16)
        sums[...] = jnp.zeros_like(sums)
        sums[1:2] = gain_sum
        first_grad[...] = jnp.zeros_like(first_grad)
        staging[...] = jnp.zeros_like(staging)

    def mix_step(j):
        for copy in mix_loads(j):
            copy.wait()
        in_w, out_w = in_v[...].reshape(full, 3 * width), out_v[...].reshape(full, width)
        filters = taps[j]
        for here in tiles:
            mixer_grad[here] = dot(residual_low[here], out_w)
        input_gate, output_gate, value = (
            stream[:, k * width : (k + 1) * width] for k in range(3)
        )
        keep_one, keep_two = keeps[:, 0:1], keeps[:, 1:2]
        gated = input_gate * value
        back_one, back_two = pltpu.roll(gated, 1, 0), pltpu.roll(gated, 2, 0)
        filtered = (
            filters[2:3] * gated
            + filters[1:2] * keep_one * back_one
            + filters[0:1] * keep_two * back_two
        )
        grad = mixer_grad[...]
        inner = grad * output_gate
        one, two = keep_one * inner, keep_two * inner
        gated_grad = (
            filters[2:3] * inner
            + filters[1:2] * pltpu.roll(one, rows - 1, 0)
            + filters[0:1] * pltpu.roll(two, rows - 2, 0)
        )

        def own_sum(values):
            return sum(jnp.sum(part, axis=0, keepdims=True) for part in own_rows(values, held))

        where = pl.ds(pl.multiple_of(j * width, width), width)
        sums[4:5, where] = own_sum(inner * gated)
        sums[3:4, where] = own_sum(one * back_one)
        sums[2:3, where] = own_sum(two * back_two)
        for k, values in enumerate((gated_grad * value, grad * filtered, gated_grad * input_gate)):
            for s, part in enumerate(own_rows(values, held)):
                stream_own[pl.ds(s * size, size), k * width : (k + 1) * width] = part.astype(BF16)
        for s, part in enumerate(own_rows(output_gate * filtered, held)):
            mixed_own[pl.ds(s * size, size)] = part.astype(BF16)
        for here in own_tiles:
            first_grad[here] += contract_last(stream_own[here], in_w)

        @pl.when(j > 0)
        def _():
            io_out(j - 1).wait()

        for k in range(4):
            if k < 3:
                new = contract_first(stream_own[:, k * width : (k + 1) * width], first_own[...])
            else:
                new = contract_first(mixed_own[...], low_own[...])
            staging[k, :, pl.ds(0, SMALL_PIECE)] = new.astype(BF16).reshape(2, SMALL_PIECE, full)
        io_out(j).start()

        @pl.when(j + 1 < chans)
        def _():
            for copy in mix_loads(j + 1):
                copy.start()

    def mix_end():
        gain_sum = jnp.zeros((1, full), F32)
        for s in range(held):
            here = pl.ds(s * size, size)
            values = tokens[pl.ds(s * length + HEAD, size)]
            scale = row_scale(values)
            unit = values * scale
            grad = first_grad[here]
            scaled = grad * gains[0:1]
            gain_sum += jnp.sum(grad * unit, axis=0, keepdims=True)
            input_grad[here] = (
                residual_grad[here]
                + scale * (scaled - unit * jnp.mean(scaled * unit, axis=1, keepdims=True))
            ).astype(BF16)
        sums[0:1] = gain_sum
        io_out(chans - 1).wait()

    spread_out = parts == 4
    mix_first, mix_last = (1, 3 * parts - 2) if spread_out else (-1, -1)
    relay = Relay(chans, block_own, blocks, relay_sems)
    for copy in mix_loads(0):
        copy.start()
    begin(0)
    relay.step(0)
    mix_prepare()
    if not spread_out:

        @pl.loop(0, chans)
        def _(j):
            mix_step(j)

        mix_end()

    summed = LAG * (1 + levels)

    @pl.loop(1, chunks + summed + LAG * (chans - 1))
    def _(tick):
        def stage(k, work):
            @pl.when((k >= 0) & (k < chunks))
            def _():
                work(k)

        stage(tick - summed - LAG * (chans - 1), finish)
        stage(tick, begin)
        for step in range(chans - 2, 0, -1):
            stage(tick - summed - LAG * step, lambda k: hop(k, step))
        for level in range(levels - 1, -1, -1):
            stage(tick - LAG * (2 + level), lambda k: level_arrive(k, level))
        stage(tick - LAG, core_arrive)
        for level in range(levels - 1, -1, -1):

            def work(k):
                level_sum(k, level)
                if level == levels - 1:
                    hop(k, 0)

            stage(tick - LAG * (2 + level), work)
        stage(tick - LAG, core_sum)
        if spread_out:

            @pl.when((tick >= mix_first) & (tick < mix_first + 2 * chans) & (lax.rem(tick - mix_first, 2) == 0))
            def _():
                mix_step(lax.div(tick - mix_first, 2))

            @pl.when(tick == mix_last)
            def _():
                mix_end()

        for level in range(len(partners) + 1):

            @pl.when(tick == mix_last + 2 + level)
            def _():
                small_step(level)

        for step in (1, 2):

            @pl.when(tick == 7 * step)
            def _():
                relay.step(step)

    relay.finish()


def backward_pass(
    seqs, chans, held, ffn_g, in_full, out_full, streams, block_own, tokens, residual, second_grad,
    cotangent, keeps, gains, taps,
):
    dma, vmem, shape = pltpu.SemaphoreType.DMA, pltpu.VMEM, jax.ShapeDtypeStruct
    parts, half_seqs = PIECES // seqs, seqs // 2
    levels = seqs.bit_length() - 2
    chunks = chans * parts
    slots = min(chunks, LAG * (levels + chans) + 1)
    group = min(4, half_seqs)
    sizes = [group] + [half_seqs >> level if group == half_seqs else 1 for level in range(1, levels + 1)]
    partners = (seqs * chans).bit_length() - 1
    rows, width = tokens.shape
    own_count = rows - held * HEAD
    part = out_full.shape[-1]
    outs = [
        shape((parts, PIECE, D), BF16),
        shape((8, width), F32),
        shape((own_count, width), BF16),
        shape((parts, half_seqs, 2, PIECE, D), BF16),
        shape((chans,) + block_own.shape, BF16),
        shape((chunks, half_seqs, PIECE, D), BF16),
    ]
    outs += [
        shape((chunks, half_seqs >> (level + 1), PIECE, D), BF16) for level in range(levels)
    ]
    outs.append(shape((2, chunks, PIECE, D), BF16))
    return call(
        functools.partial(backward_kernel, seqs, chans, held),
        outs,
        [pl.ANY] * 5 + [vmem] * 7,
        [vmem] * 3 + [pl.ANY] * (len(outs) - 3),
        [
            *[vmem((size, PIECE, D), BF16) for size in sizes],
            vmem((slots, half_seqs, PIECE, D), BF16),
            vmem((2, PIECE, D), BF16),
            vmem((partners, 8, width), F32),
            vmem((partners, 8, width), F32),
            vmem((8, width), F32),
            vmem((rows, width), BF16),
            vmem((own_count, width), BF16),
            vmem((own_count, width), BF16),
            vmem((own_count, width), F32),
            vmem((own_count, 3 * part), BF16),
            vmem((own_count, part), BF16),
            vmem((rows, part), F32),
            vmem((own_count, width), F32),
            vmem((rows, 3 * part), F32),
            vmem(in_full.shape[1:], BF16),
            vmem(out_full.shape[1:], BF16),
            vmem((4, 2, PIECE, D), BF16),
            dma((chunks,)),
            dma(()),
            dma((levels + 1,)),
            dma((chunks,)),
            dma((chunks,)),
            dma((chunks, 2, half_seqs)),
            dma((chunks, 2, half_seqs)),
            dma((chunks,)),
            dma((2, chunks)),
            dma((partners,)),
            dma((partners,)),
            dma((3,)),
            dma(()),
            *Relay.semaphores(chans),
        ],
        1,
        ffn_g.reshape(3, parts, half_seqs, 2, PIECE, D),
        in_full, out_full, streams, block_own, tokens, residual, second_grad, cotangent, keeps, gains,
        taps,
        vmem=62,
    )[:5]


def shifted(value, axes, by):
    length = lax.axis_size(axes)
    pairs = [(i, i + by) for i in range(length) if 0 <= i + by < length]
    return lax.ppermute(value, axes, pairs)


def adam_update(param, gradient, first, second):
    first_new = FIRST_DECAY * first + (1.0 - FIRST_DECAY) * gradient
    second_new = SECOND_DECAY * second + (1.0 - SECOND_DECAY) * gradient * gradient
    first_fix = 1.0 - FIRST_DECAY**STEP
    second_fix = 1.0 - SECOND_DECAY**STEP
    param_new = param - ADAM_RATE * (first_new / first_fix) / (
        jnp.sqrt(second_new / second_fix) + ADAM_EPS
    )
    return (param_new, first_new, second_new)


COLUMNS = [3 * D, D, FF, FF, FF]
RATES = [1.0, 1.0, 1.0, 1.0, 0.5]


def last_kernel(block_low, input_low, grad_home, ortho_home, *refs):
    weights, moments, (block_out, input_grad) = refs[:5], refs[5:10], refs[10:12]
    moments_new, weights_new = refs[12:22:2], refs[13:22:2]
    step = pl.program_id(0)
    for low, whole in ((block_low, block_out), (input_low, input_grad)):
        rows = low.shape[2]
        for at in range(low.shape[0]):
            whole[0, at * rows : (at + 1) * rows] = low[at, 0].astype(F32)

    def update(index, at, lanes, grad, ortho):
        rate = RATES[index]
        here = at + (slice(None), lanes)
        moments_new[index][here] = MOMENTUM_DECAY * moments[index][here] + grad.astype(F32).T
        weights_new[index][here] = (
            weights[index][here] * (1.0 - WEIGHT_DECAY * rate)
            - rate * math.sqrt(COLUMNS[index] / D) * ortho.astype(F32).T
        )

    for m in range(3):

        @pl.when(step == m)
        def _():
            for t in range(TILES):
                rows = slice(t * UNIT, (t + 1) * UNIT)
                update(
                    m + 2, (), slice(t * LANES, (t + 1) * LANES),
                    *(home[m, :, rows].reshape(LANES, -1) for home in (grad_home, ortho_home)),
                )

    @pl.when(step == 3)
    def _():
        for q in range(PER_CHAN):
            lanes = slice(q % 2 * SMALL_PIECE, (q % 2 + 1) * SMALL_PIECE)
            blocks = [home[3, q, 0:SMALL_PIECE] for home in (grad_home, ortho_home)]
            update(*((0, (q // 2,)) if q < IN_PIECES else (1, ())), lanes, *blocks)


def last_pass(block_low, input_low, homes, weights, moments):
    chans, held, sub, width = block_low.shape
    low = pl.BlockSpec((chans, 1, sub, width), lambda s: (0, s, 0, 0))
    whole = pl.BlockSpec((1, chans * sub, width), lambda s: (s, 0, 0))

    def all_of(array):
        return pl.BlockSpec(array.shape, lambda s: (0,) * array.ndim)

    shape = jax.ShapeDtypeStruct
    outs = [shape((held, chans * sub, width), F32)] * 2
    out_specs = [whole] * 2
    for weight in weights:
        outs += [shape(weight.shape, F32)] * 2
        out_specs += [all_of(weight)] * 2
    return pl.pallas_call(
        last_kernel,
        grid=(held,),
        out_shape=outs,
        in_specs=[low] * 2 + [all_of(one) for one in (*homes, *weights, *moments)],
        out_specs=out_specs,
        compiler_params=pltpu.CompilerParams(vmem_limit_bytes=60 * 1024 * 1024),
    )(block_low, input_low, *homes, *weights, *moments)


def on_device(
    tokens,
    segment_ids,
    cotangent,
    norm_gains,
    filter_weight,
    in_weight,
    out_weight,
    gate_weight,
    up_weight,
    down_weight,
    norm_gains_mean,
    norm_gains_square,
    filter_mean,
    filter_square,
    in_momentum,
    out_momentum,
    gate_momentum,
    up_momentum,
    down_momentum,
):
    seqs, chans = lax.axis_size("seq"), lax.axis_size("chan")
    r, c = lax.axis_index("seq"), lax.axis_index("chan")
    seq_total, local_rows, width = tokens.shape
    sub = local_rows // chans
    chan_width = filter_weight.shape[1]

    weights = [in_weight.transpose(1, 0, 2), out_weight, gate_weight, up_weight, down_weight]
    moments = [
        in_momentum.transpose(1, 0, 2), out_momentum, gate_momentum, up_momentum, down_momentum
    ]

    def share(array, start, length):
        return lax.dynamic_slice_in_dim(array, start, length, axis=1)

    positions = r * local_rows + jnp.arange(local_rows, dtype=jnp.int32)
    local_keeps = jnp.stack(
        [(segment_ids <= positions[None, :] - offset).astype(F32) for offset in (1, 2)], axis=-1
    )
    following = jnp.where(
        c == chans - 1,
        shifted(local_keeps[:, :2], "seq", -1),
        share(local_keeps, lax.rem(c + 1, chans) * sub, 2),
    )
    following = jnp.concatenate([following[-1:], following[:-1]])
    gap = jnp.zeros((seq_total, HEAD - 2, 2), F32)
    keeps = jnp.concatenate([following, gap, share(local_keeps, c * sub, sub)], axis=1).reshape(-1, 2)

    (
        in_full, out_full, _, taps, moments_held, _, streams, ffn_grads,
        token_rows, upstream_rows, residual, second_grad, block_out,
    ) = forward_pass(
        seqs, chans, weights, moments, filter_weight, tokens, cotangent, keeps, norm_gains
    )
    moments_held = moments_held.transpose(0, 2, 1, 3).reshape(-1, D)
    grads_held, small, input_grad, _, block_out = backward_pass(
        seqs, chans, seq_total, ffn_grads, in_full, out_full, streams, block_out, token_rows, residual,
        second_grad, upstream_rows, keeps, norm_gains, taps,
    )

    gains_new, gains_mean_new, gains_square_new = adam_update(
        norm_gains, small[:2], norm_gains_mean, norm_gains_square
    )
    filter_new, filter_mean_new, filter_square_new = adam_update(
        filter_weight, share(small[2:5], c * chan_width, chan_width), filter_mean, filter_square
    )

    *homes, input_grad = orthogonalize(
        seqs, chans, grads_held.reshape(-1, D), moments_held, input_grad
    )
    block_out, input_grad = (
        one.reshape(chans, seq_total, sub, width) for one in (block_out, input_grad)
    )
    block_out, input_grad, *results = last_pass(block_out, input_grad, homes, weights, moments)
    results[:2] = [one.transpose(1, 0, 2) for one in results[:2]]
    return (
        block_out,
        input_grad,
        gains_new,
        gains_mean_new,
        gains_square_new,
        filter_new,
        filter_mean_new,
        filter_square_new,
        *results,
    )


def solution(mesh):
    return jax.shard_map(
        on_device,
        mesh=mesh,
        in_specs=(
            P(None, "seq", None),
            P(None, "seq"),
            P(None, "seq", None),
            P(),
            P(None, "chan"),
            P("seq", None, "chan"),
            P("seq", "chan"),
            P("seq", "chan"),
            P("seq", "chan"),
            P("seq", "chan"),
            P(),
            P(),
            P(None, "chan"),
            P(None, "chan"),
            P("seq", None, "chan"),
            P("seq", "chan"),
            P("seq", "chan"),
            P("seq", "chan"),
            P("seq", "chan"),
        ),
        out_specs=(
            P(None, "seq", None),
            P(None, "seq", None),
            P(),
            P(),
            P(),
            P(None, "chan"),
            P(None, "chan"),
            P(None, "chan"),
            P("seq", None, "chan"),
            P("seq", None, "chan"),
            P("seq", "chan"),
            P("seq", "chan"),
            P("seq", "chan"),
            P("seq", "chan"),
            P("seq", "chan"),
            P("seq", "chan"),
            P("seq", "chan"),
            P("seq", "chan"),
        ),
        check_vma=False,
    )
```
